32 devices in a mesh: slab: 2 (over x), line: 8 (over z, y), band: 2 (over core).
Axes of the slice: x: 2, y: 2, z: 4, core: 2. Of those that a mesh axis runs over, the one named last changes fastest.
Arguments:
- cube: bfloat16 [230, 2048, 256], P('band', ('slab', 'line')), parts along dimension 1, may hold values from -6 to 6
- observed: bfloat16 [13, 2048, 256], P(None, ('slab', 'line')), parts along dimension 1, may hold values from -6 to 6
- along_kernels: bfloat16 [3, 128, 128], replicated, may hold values from -0.3125 to 0.3125
- along_offsets: int32 [3], replicated, may hold values from -1 to 1, as said below
- across_kernels: bfloat16 [3, 128, 128], replicated, may hold values from -0.3125 to 0.3125
- across_offsets: int32 [3], replicated, may hold values from -1 to 1, as said below
- resp_start: int32 [13], replicated, may hold values from 0 to 21
- resp_values: bfloat16 [13, 20], replicated, may hold values from 0.049804688 to 0.3984375
Outputs:
- synthetic: float32 [13, 2048, 256], P(None, ('slab', 'line')), parts along dimension 1
- angles: float32 [2048, 256], P(('slab', 'line')), parts along dimension 0
The draws below stay inside these ranges and needn't reach their ends.
There are 2 independent parts, one for each index of `slab`. The reference program is written for one: setup_inputs(seed, part) draws one part's arguments, and reference() takes and returns one part's arrays. A program takes and returns all parts, laid end to end along the dimension named above; an argument that names none is the same for every part. Nothing has to cross between parts.
Inputs may be any that keep to these rules, and one draw needn't show every extreme that they name: `along_offsets`: the three entries are -1, 0 and 1, each once. `across_offsets`: the three entries are -1, 0 and 1, each once.
All inputs are finite; a program needn't handle non-finite values.
Results may differ from the reference program's by a relative error of at most 0.0003.
Values may be sent and summed in bfloat16 or wider, within the bound.
No kernel may reach another device: no remote copies, remote signals or barrier semaphores. Data moves between devices by JAX's collectives and lax.ppermute only.
A program may use at most 192 MiB of HBM per device.

```python
import jax
import jax.numpy as jnp
from jax import lax

BANDS = 230
MS = 13
BLK = 128
SPB = 10
COLS = 256
LINES = 1024
NSB = 23


def draw_along_offsets(key, part):
    return (jax.random.permutation(jax.random.fold_in(key, 11), 3) - 1).astype(jnp.int32)


def draw_across_offsets(key, part):
    return (jax.random.permutation(jax.random.fold_in(key, 23), 3) - 1).astype(jnp.int32)


def place_ends(entries, rng, low, high):
    longest = entries.shape.index(max(entries.shape))
    spots = []
    for shift in (0, 1):
        where = [jax.random.randint(jax.random.fold_in(rng, axis), (), 0, length) for axis, length in enumerate(entries.shape)]
        where[longest] = (where[longest] + shift) % entries.shape[longest]
        spots.append(tuple(where))
    return entries.at[spots[0]].set(low).at[spots[1]].set(high)


def level_of(key, dims, shards, low, high):
    factor_of = 1.0
    for dim, shards_of in shards:
        heights = jax.random.uniform(jax.random.fold_in(jax.random.fold_in(key, 6), dim), (shards_of,), jnp.float32, low / len(shards), high / len(shards))
        factor_of = factor_of * jnp.repeat(jnp.exp(heights), dims[dim] // shards_of).reshape((-1,) + (1,) * (len(dims) - 1 - dim))
    return factor_of


def bell_draw(rng, dims, scale, reach, shards=(), held_as=jnp.bfloat16):
    entries = jax.random.normal(rng, dims, jnp.float32) * scale
    if len(shards) > 0:
        entries = level_of(rng, dims, shards, -0.22, 0.18) * entries
    return jnp.clip(entries, min=-reach, max=reach).astype(held_as)


def setup_inputs(seed: int = 0, part: int = 0) -> dict:
    key_list = jax.random.split(jax.random.key(seed), 9)
    own_keys = jax.random.split(jax.random.fold_in(key_list[8], part), 9)
    cube = bell_draw(own_keys[0], (BANDS, LINES, COLS), 1.0, 6.0, ((0, 2), (1, 8)))
    observed = bell_draw(own_keys[1], (MS, LINES, COLS), 1.0, 6.0, ((1, 8),))
    along_kernels = bell_draw(key_list[2], (3, BLK, BLK), (3 * BLK) ** -0.5, 0.3125)
    along_offsets = draw_along_offsets(jax.random.fold_in(key_list[8], 71), part)
    across_kernels = bell_draw(key_list[4], (3, BLK, BLK), (3 * BLK) ** -0.5, 0.3125)
    across_offsets = draw_across_offsets(jax.random.fold_in(key_list[8], 71), part)
    resp_start = place_ends(jax.random.randint(key_list[6], (MS,), 0, NSB - 1), jax.random.fold_in(key_list[6], 1), 0, (NSB - 1) - 1).astype(jnp.int32)
    resp_values = jnp.clip(jax.random.uniform(key_list[7], (MS, 2 * SPB), jnp.float32, 0.049804688, 0.3984375), 0.049804688, 0.3984375).astype(jnp.bfloat16)
    return {"cube": cube, "observed": observed, "along_kernels": along_kernels, "along_offsets": along_offsets, "across_kernels": across_kernels, "across_offsets": across_offsets, "resp_start": resp_start, "resp_values": resp_values}


def pick_kernels(kernels, offsets):
    shifts = jnp.arange(3, dtype=jnp.int32) - 1
    onehot = (offsets[None, :] == shifts[:, None]).astype(jnp.float32)
    return jnp.einsum('sk,kpq->spq', onehot, kernels.astype(jnp.float32), precision=lax.Precision.HIGHEST)

def dense_response(resp_start, resp_values):
    bands = jnp.arange(BANDS, dtype=jnp.int32)
    local = bands[None, :] - SPB * resp_start[:, None]
    slots = jnp.arange(2 * SPB, dtype=jnp.int32)
    hits = local[:, :, None] == slots[None, None, :]
    return lax.optimization_barrier(jnp.sum(jnp.where(hits, resp_values.astype(jnp.float32)[:, None, :], jnp.float32(0.0)), axis=-1))

def along_filter(field, chosen):
    count = field.shape[1] // BLK
    blocks = field.astype(jnp.float32).reshape(field.shape[0], count, BLK, field.shape[2])
    padded = jnp.pad(blocks, ((0, 0), (1, 1), (0, 0), (0, 0)))
    total = jnp.zeros(blocks.shape, jnp.float32)
    for index in range(3):
        total = total + jnp.einsum('pq,bnqc->bnpc', chosen[index], padded[:, index:index + count], precision=lax.Precision.HIGHEST)
    return total.reshape(field.shape)

def across_filter(field, chosen):
    count = field.shape[2] // BLK
    blocks = field.astype(jnp.float32).reshape(field.shape[0], field.shape[1], count, BLK)
    padded = jnp.pad(blocks, ((0, 0), (0, 0), (1, 1), (0, 0)))
    total = jnp.zeros(blocks.shape, jnp.float32)
    for index in range(3):
        total = total + jnp.einsum('pq,blnq->blnp', chosen[index], padded[:, :, index:index + count], precision=lax.Precision.HIGHEST)
    return total.reshape(field.shape)

def reference(cube, observed, along_kernels, along_offsets, across_kernels, across_offsets, resp_start, resp_values):
    along_pick = pick_kernels(along_kernels, along_offsets)
    across_pick = pick_kernels(across_kernels, across_offsets)
    response = dense_response(resp_start, resp_values)
    groups = cube.reshape(NSB, SPB, LINES, COLS)
    weights = response.reshape(MS, NSB, SPB).transpose(1, 0, 2)

    def accumulate(carry, item):
        group, weight = item
        along = along_filter(group, along_pick)
        across = across_filter(along, across_pick)
        return (carry + jnp.einsum('mb,blc->mlc', weight, across, precision=lax.Precision.HIGHEST), None)
    start = jnp.zeros((MS, LINES, COLS), jnp.float32)
    synthetic, unused = lax.scan(accumulate, start, (groups, weights))
    seen = observed.astype(jnp.float32)
    inner = lax.optimization_barrier(jnp.sum(synthetic * seen, axis=0))
    first = jnp.sqrt(lax.optimization_barrier(jnp.sum(synthetic * synthetic, axis=0)))
    second = jnp.sqrt(lax.optimization_barrier(jnp.sum(seen * seen, axis=0)))
    angles = jnp.arccos(jnp.clip(inner / jnp.maximum(first * second, 1.0), -1.0, 1.0))
    return (synthetic, angles)
```

```python
import functools

import jax
import jax.numpy as jnp
from jax import lax
from jax.experimental import pallas as pl
from jax.experimental.pallas import tpu as pltpu
from jax.sharding import PartitionSpec as P

BLK = 128
SPB = 10
STEPS = 16.0
PEAK = 32000.0


def which(offsets, shift):
    return sum(
        jnp.where(offsets[k] == shift, jnp.int32(k), jnp.int32(0)) for k in range(offsets.shape[0])
    )


def split(value):
    high = value.astype(jnp.bfloat16)
    low = (value - high.astype(jnp.float32)).astype(jnp.bfloat16)
    return high, low


def fold_kernel(start, offsets, values, blocks, cube, keep, send, weights, folded, across):
    bands, rows, cols = cube.shape
    count, window = values.shape
    half = cols // 2
    me = lax.axis_index("band")

    @pl.when(pl.program_id(0) == 0)
    def _():
        weights[...] = values[...].astype(jnp.float32)
        for r in range(2):
            mine = me if r == 0 else 1 - me
            for c in range(2):
                pick = which(offsets, c - mine)
                across[r * half : (r + 1) * half, c * half : (c + 1) * half] = blocks[pick]

    def one(m, carry):
        low = SPB * start[m] - bands * me
        inside = jnp.logical_and(low > -window, low < bands)

        @pl.when(inside)
        def _():
            row = weights[pl.ds(m, 1), :]
            band = low + lax.broadcasted_iota(jnp.int32, row.shape, 1)
            row = jnp.where(jnp.logical_and(band >= 0, band < bands), row, 0.0)
            total = jnp.zeros((rows, cols), jnp.float32)
            for j in range(window):
                at = jnp.clip(low + j, 0, bands - 1)
                total = total + row[:, j : j + 1] * cube[at].astype(jnp.float32)
            folded[m] = total

        @pl.when(jnp.logical_not(inside))
        def _():
            folded[m] = jnp.zeros((rows, cols), jnp.float32)

        return carry

    lax.fori_loop(0, count, one, 0)
    high, low = split(folded[...].reshape(count * rows, cols))
    dims = (((1,), (1,)), ((), ()))
    table = across[...]
    out = lax.dot_general(high, table, dims, preferred_element_type=jnp.float32)
    out = out + lax.dot_general(low, table, dims, preferred_element_type=jnp.float32)
    keep[...] = out[:, :half].reshape(count, rows, half)
    send[...] = out[:, half:].reshape(count, rows, half)


def fold(cube, start, values, blocks, offsets):
    bands, lines, cols = cube.shape
    count = values.shape[0]
    rows = 32
    half = cols // 2
    out = jax.ShapeDtypeStruct((count, lines, half), jnp.float32)
    smem = pl.BlockSpec(memory_space=pltpu.SMEM)
    vmem = pl.BlockSpec(memory_space=pltpu.VMEM)
    part = pl.BlockSpec((count, rows, half), lambda i: (0, i, 0))
    return pl.pallas_call(
        fold_kernel,
        grid=(lines // rows,),
        in_specs=[smem, smem, vmem, vmem, pl.BlockSpec((bands, rows, cols), lambda i: (0, i, 0))],
        out_specs=[part, part],
        out_shape=[out, out],
        scratch_shapes=[
            pltpu.VMEM(values.shape, jnp.float32),
            pltpu.VMEM((count, rows, cols), jnp.float32),
            pltpu.VMEM((cols, cols), jnp.bfloat16),
        ],
        compiler_params=pltpu.CompilerParams(vmem_limit_bytes=32 * 2**20),
        name="fold",
    )(start, offsets, values, blocks, cube)


def code_kernel(keep, other, total, message):
    count, lines, half = keep.shape
    value = keep[...] + other[...]
    total[...] = value
    largest = jnp.max(jnp.abs(value), axis=1)
    level = jnp.ceil(jnp.log2(jnp.maximum(largest, 1e-30)) * STEPS)
    factor = PEAK * jnp.exp2(level * (-1.0 / STEPS))
    coded = jnp.floor(value * factor[:, None, :] + 0.5).astype(jnp.int32)
    message[: count * lines, :] = coded.reshape(count * lines, half).astype(jnp.int16)
    extra = message.shape[0] - count * lines
    level = jnp.concatenate([level, jnp.zeros((extra - count, half), jnp.float32)], axis=0)
    message[count * lines :, :] = level.astype(jnp.int32).astype(jnp.int16)


def code(keep, other):
    count, lines, half = keep.shape
    extra = -(-count // 16) * 16
    return pl.pallas_call(
        code_kernel,
        out_shape=[
            jax.ShapeDtypeStruct(keep.shape, jnp.float32),
            jax.ShapeDtypeStruct((count * lines + extra, half), jnp.int16),
        ],
        compiler_params=pltpu.CompilerParams(vmem_limit_bytes=32 * 2**20),
        name="code",
    )(keep, other)


def arccos(x):
    size = jnp.abs(x)
    big = size > 0.5
    z = jnp.where(big, 0.5 * (1.0 - size), size * size)
    root = jnp.where(big, jnp.sqrt(z), size)
    poly = 4.2163199048e-2
    for term in (2.4181311049e-2, 4.5470025998e-2, 7.4953002686e-2, 1.6666752422e-1):
        poly = poly * z + term
    arcsin = poly * z * root + root
    pi = 3.14159265358979
    inner = jnp.where(x < 0, 0.5 * pi + arcsin, 0.5 * pi - arcsin)
    outer = jnp.where(x < 0, pi - 2.0 * arcsin, 2.0 * arcsin)
    return jnp.where(big, outer, inner)


def blur_kernel(offsets, blocks, total, near, far, observed, out):
    count, lines, half = total.shape
    me = lax.axis_index("band")
    even = lax.axis_index("line") % 2 == 0
    step = jnp.where(even, 1, -1)
    filters = jnp.concatenate(
        [blocks[which(offsets, s)] for s in (jnp.int32(0), step, -step)], axis=1
    )

    def levels(message):
        level = message[count * lines :, :].astype(jnp.int32).astype(jnp.float32)
        return jnp.exp2(level * (1.0 / STEPS)) * (1.0 / PEAK)

    near_scale, far_scale = levels(near), levels(far)

    def values(message, scale, m):
        coded = message[m * lines : (m + 1) * lines, :].astype(jnp.int32).astype(jnp.float32)
        return coded * scale[m : m + 1, :]

    inner = jnp.zeros((lines, half), jnp.float32)
    first = jnp.zeros((lines, half), jnp.float32)
    second = jnp.zeros((lines, half), jnp.float32)
    for m in range(count):
        parts = [total[m], values(near, near_scale, m), values(far, far_scale, m)]
        high, low = split(jnp.concatenate(parts, axis=0))
        both = jnp.dot(
            filters, jnp.concatenate([high, low], axis=1), preferred_element_type=jnp.float32
        )
        made = both[:, :half] + both[:, half:]
        out[m] = made
        seen = observed[m, :, pl.ds(pl.multiple_of(me * half, BLK), half)].astype(jnp.float32)
        inner = inner + made * seen
        first = first + made * made
        second = second + seen * seen
    bound = jnp.maximum(jnp.sqrt(first) * jnp.sqrt(second), 1.0)
    out[count] = arccos(jnp.clip(inner / bound, -1.0, 1.0))


def blur(total, near, far, observed, blocks, offsets):
    count, lines, half = total.shape
    smem = pl.BlockSpec(memory_space=pltpu.SMEM)
    vmem = pl.BlockSpec(memory_space=pltpu.VMEM)
    return pl.pallas_call(
        blur_kernel,
        in_specs=[smem] + [vmem] * 5,
        out_shape=jax.ShapeDtypeStruct((count + 1, lines, half), jnp.float32),
        compiler_params=pltpu.CompilerParams(vmem_limit_bytes=32 * 2**20),
        name="blur",
    )(offsets, blocks, total, near, far, observed)


def join_kernel(mine, other, image, angles):
    planes, _, half = mine.shape
    me = lax.axis_index("band")
    for part, where in ((mine, me), (other, 1 - me)):
        at = pl.ds(pl.multiple_of(where * half, BLK), half)
        image[:, :, at] = part[: planes - 1]
        angles[:, at] = part[planes - 1]


def join(mine, other):
    planes, lines, half = mine.shape
    return pl.pallas_call(
        join_kernel,
        out_shape=[
            jax.ShapeDtypeStruct((planes - 1, lines, 2 * half), jnp.float32),
            jax.ShapeDtypeStruct((lines, 2 * half), jnp.float32),
        ],
        compiler_params=pltpu.CompilerParams(vmem_limit_bytes=32 * 2**20),
        name="join",
    )(mine, other)


def on_device(
    cube,
    observed,
    along_kernels,
    along_offsets,
    across_kernels,
    across_offsets,
    resp_start,
    resp_values,
):
    size = lax.axis_size("line")
    swap = [(0, 1), (1, 0)]
    partner = [(i, i ^ 1) for i in range(size)]
    onward = [(i, i + 2) for i in range(0, size - 2, 2)] + [(i, i - 2) for i in range(3, size, 2)]
    keep, send = fold(cube, resp_start, resp_values, across_kernels, across_offsets)
    total, message = code(keep, lax.ppermute(send, "band", swap))
    near = lax.ppermute(message, "line", partner)
    far = lax.ppermute(near, "line", onward)
    mine = blur(total, near, far, observed, along_kernels, along_offsets)
    return tuple(join(mine, lax.ppermute(mine, "band", swap)))


def solution(mesh):
    placed = (
        P("band", ("slab", "line"), None),
        P(None, ("slab", "line"), None),
        P(),
        P(),
        P(),
        P(),
        P(),
        P(),
    )
    return jax.shard_map(
        on_device,
        mesh=mesh,
        in_specs=placed,
        out_specs=(P(None, ("slab", "line"), None), P(("slab", "line"), None)),
        check_vma=False,
    )
```

```python
import functools

import jax
import jax.numpy as jnp
from jax import lax
from jax.experimental import pallas as pl
from jax.experimental.pallas import tpu as pltpu
from jax.sharding import PartitionSpec as P

BLK = 128
SPB = 10
STEPS = 16.0
PEAK = 32000.0


def which(offsets, shift):
    return sum(
        jnp.where(offsets[k] == shift, jnp.int32(k), jnp.int32(0)) for k in range(offsets.shape[0])
    )


def split(value):
    high = value.astype(jnp.bfloat16)
    low = (value - high.astype(jnp.float32)).astype(jnp.bfloat16)
    return high, low


SMEM = pl.BlockSpec(memory_space=pltpu.SMEM)
VMEM = pl.BlockSpec(memory_space=pltpu.VMEM)
HBM = pl.BlockSpec(memory_space=pltpu.HBM)
ROWS = 32


def call(kernel, inputs, specs, outs, scratch=(), out_specs=None, aliases=None, flops=0):
    moved = sum(x.size * x.dtype.itemsize for x in (*inputs, *outs))
    return pl.pallas_call(
        kernel,
        in_specs=specs,
        out_specs=out_specs or [VMEM] * len(outs),
        out_shape=outs,
        scratch_shapes=scratch,
        input_output_aliases=aliases or {},
        compiler_params=pltpu.CompilerParams(vmem_limit_bytes=32 * 2**20),
        cost_estimate=pl.CostEstimate(flops=flops, bytes_accessed=moved, transcendentals=0),
        name=(kernel.func if isinstance(kernel, functools.partial) else kernel).__name__,
    )(*inputs)


def fold(
    start_in,
    offsets_in,
    values_in,
    blocks_in,
    cube_in,
    keep,
    send,
    start,
    offsets,
    values,
    wide,
    weights,
    blocks,
    cube,
    folded,
    table,
    active,
    small,
    large,
):
    bands, lines, cols = cube.shape
    count, window = values.shape
    half = cols // 2
    me = lax.axis_index("band")
    pairs = ((values_in, values), (start_in, start), (offsets_in, offsets), (blocks_in, blocks))
    copies = [pltpu.make_async_copy(a, b, small.at[i]) for i, (a, b) in enumerate(pairs)]

    def arrive(c):
        at = pl.ds(pl.multiple_of(c * ROWS, ROWS), ROWS)
        return pltpu.make_async_copy(cube_in.at[:, at, :], cube.at[:, at, :], large.at[c])

    for copy in copies:
        copy.start()
    for c in range(lines // ROWS):
        arrive(c).start()
    copies[0].wait()
    wide[...] = values[...].astype(jnp.float32)
    spread = pltpu.make_async_copy(wide, weights, small.at[len(pairs)])
    spread.start()
    for copy in copies[1:]:
        copy.wait()
    for r in range(2):
        mine = me if r == 0 else 1 - me
        for c in range(2):
            pick = which(offsets, c - mine)
            table[r * half : (r + 1) * half, c * half : (c + 1) * half] = blocks[pick]

    def place(m):
        return SPB * start[m] - bands * me

    def listing(m, n):
        low = place(m)
        inside = jnp.logical_and(low > -window, low < bands)

        @pl.when(inside)
        def _():
            active[n] = m

        @pl.when(jnp.logical_not(inside))
        def _():
            folded[m] = jnp.zeros((lines, cols), jnp.float32)

        return n + inside.astype(jnp.int32)

    used = lax.fori_loop(0, count, listing, jnp.int32(0))
    spread.wait()

    def chunk(c, carry):
        arrive(c).wait()
        at = pl.ds(pl.multiple_of(c * ROWS, ROWS), ROWS)

        def one(n, carry):
            m = active[n]
            low = place(m)
            whole = jnp.logical_and(low >= 0, low + window <= bands)

            @pl.when(whole)
            def _():
                total = jnp.zeros((ROWS, cols), jnp.float32)
                for j in range(window):
                    total = total + weights[m, j] * cube[low + j, at, :].astype(jnp.float32)
                folded[m, at, :] = total

            @pl.when(jnp.logical_not(whole))
            def _():
                def term(j, total):
                    return total + weights[m, j] * cube[low + j, at, :].astype(jnp.float32)

                folded[m, at, :] = lax.fori_loop(
                    jnp.maximum(0, -low),
                    jnp.minimum(window, bands - low),
                    term,
                    jnp.zeros((ROWS, cols), jnp.float32),
                )

            return carry

        return lax.fori_loop(0, used, one, carry)

    lax.fori_loop(0, lines // ROWS, chunk, 0)
    dims = (((1,), (1,)), ((), ()))
    side = table[...]
    for m in range(0, count, 4):
        n = min(4, count - m)
        high, low = split(folded[m : m + n].reshape(n * lines, cols))
        out = lax.dot_general(high, side, dims, preferred_element_type=jnp.float32)
        out = out + lax.dot_general(low, side, dims, preferred_element_type=jnp.float32)
        keep[m : m + n] = out[:, :half].reshape(n, lines, half)
        send[m : m + n] = out[:, half:].reshape(n, lines, half)


def coded_rows(count, lines):
    return count * lines + -(-count // 16) * 16


def encode(value, message):
    count, lines, half = value.shape
    largest = jnp.max(jnp.abs(value), axis=1)
    level = jnp.ceil(jnp.log2(jnp.maximum(largest, 1e-30)) * STEPS)
    factor = PEAK * jnp.exp2(level * (-1.0 / STEPS))
    coded = jnp.floor(value * factor[:, None, :] + 0.5).astype(jnp.int32)
    message[: count * lines, :] = coded.reshape(count * lines, half).astype(jnp.int16)
    spare = message.shape[0] - count * lines - count
    level = jnp.concatenate([level, jnp.zeros((spare, half), jnp.float32)], axis=0)
    message[count * lines :, :] = level.astype(jnp.int32).astype(jnp.int16)


def decode(message, count, lines):
    level = message[count * lines :, :].astype(jnp.int32).astype(jnp.float32)
    scale = jnp.exp2(level * (1.0 / STEPS)) * (1.0 / PEAK)

    def plane(m):
        coded = message[m * lines : (m + 1) * lines, :].astype(jnp.int32).astype(jnp.float32)
        return coded * scale[m : m + 1, :]

    return plane


def blurred(block, value):
    high, low = split(value)
    both = jnp.dot(
        block, jnp.concatenate([high, low], axis=1), preferred_element_type=jnp.float32
    )
    return both[:, : value.shape[1]] + both[:, value.shape[1] :]


def side_step():
    return jnp.where(lax.axis_index("line") % 2 == 0, jnp.int32(1), jnp.int32(-1))


def share(offsets, blocks, keep, other, total, whole, product):
    first = (whole.shape[0] - 1) // keep.shape[1]
    value = keep[...] + other[...]
    total[...] = value
    encode(value[:first], whole)
    block = blocks[which(offsets, side_step())]
    made = [blurred(block, value[m])[None] for m in range(first, keep.shape[0])]
    encode(jnp.concatenate(made, axis=0), product)


def centre(offsets, blocks, total, base, term):
    count, lines, _ = total.shape
    rest = term.shape[0]
    step = side_step()
    here = blocks[which(offsets, jnp.int32(0))]
    stack = jnp.concatenate([here, blocks[which(offsets, -step)]], axis=0)
    for m in range(count):
        if m < count - rest:
            base[m] = blurred(here, total[m])
        else:
            made = blurred(stack, total[m])
            base[m] = made[:lines]
            term[m - (count - rest)] = made[lines:]


def relay(term, product, message):
    count, lines, _ = term.shape
    plane = decode(product, count, lines)
    encode(jnp.concatenate([(term[m] + plane(m))[None] for m in range(count)], axis=0), message)


def beside(offsets, blocks, base, near, other_base, other_near, total, other_total):
    count, lines, _ = base.shape
    first = (near.shape[0] - 1) // lines
    block = blocks[which(offsets, side_step())]
    for source, message, out in ((base, near, total), (other_base, other_near, other_total)):
        plane = decode(message, first, lines)
        for m in range(count):
            out[m] = source[m] + blurred(block, plane(m)) if m < first else source[m]

def arccos(x):
    size = jnp.abs(x)
    big = size > 0.5
    z = jnp.where(big, 0.5 * (1.0 - size), size * size)
    root = jnp.where(big, jnp.sqrt(z), size)
    poly = 4.2163199048e-2
    for term in (2.4181311049e-2, 4.5470025998e-2, 7.4953002686e-2, 1.6666752422e-1):
        poly = poly * z + term
    arcsin = poly * z * root + root
    pi = 3.14159265358979
    inner = jnp.where(x < 0, 0.5 * pi + arcsin, 0.5 * pi - arcsin)
    outer = jnp.where(x < 0, pi - 2.0 * arcsin, 2.0 * arcsin)
    return jnp.where(big, outer, inner)


def finish(second, offsets, blocks, observed, base, far, sums, *rest):
    image, angles, made, angle, sems = rest[-5:]
    count, lines, half = base.shape
    first = (far.shape[0] - 1) // lines
    me = lax.axis_index("band")
    where = 1 - me if second else me
    at = pl.ds(pl.multiple_of(where * half, BLK), half)
    block = blocks[which(offsets, -side_step())]
    planes, others = decode(far, first, lines), decode(sums, count - first, lines)
    inner = jnp.zeros((lines, half), jnp.float32)
    left = jnp.zeros((lines, half), jnp.float32)
    right = jnp.zeros((lines, half), jnp.float32)
    copies = []
    for m in range(count):
        value = blurred(block, planes(m)) if m < first else others(m - first)
        value = base[m] + value
        made[m] = value
        copies.append(pltpu.make_async_copy(made.at[m], image.at[m, :, at], sems.at[m]))
        copies[-1].start()
        seen = observed[m, :, at].astype(jnp.float32)
        inner = inner + value * seen
        left = left + value * value
        right = right + seen * seen
    bound = jnp.maximum(jnp.sqrt(left) * jnp.sqrt(right), 1.0)
    angle[...] = arccos(jnp.clip(inner / bound, -1.0, 1.0))
    copies.append(pltpu.make_async_copy(angle, angles.at[:, at], sems.at[count]))
    copies[-1].start()
    for copy in copies:
        copy.wait()


def on_device(
    cube,
    observed,
    along_kernels,
    along_offsets,
    across_kernels,
    across_offsets,
    resp_start,
    resp_values,
):
    f32, i16 = jnp.float32, jnp.int16
    size = lax.axis_size("line")
    bands, lines, cols = cube.shape
    count = resp_values.shape[0]
    half = cols // 2
    first = (count + 1) // 2
    rest = count - first
    shape = jax.ShapeDtypeStruct
    swap = [(0, 1), (1, 0)]
    partner = [(i, i ^ 1) for i in range(size)]
    even_up = [(i, i + 2) for i in range(0, size - 2, 2)] + [(i, i - 2) for i in range(3, size, 2)]
    odd_up = [(i, i + 2) for i in range(1, size - 2, 2)] + [(i, i - 2) for i in range(2, size, 2)]
    along = (along_offsets, along_kernels)
    part = shape((count, lines, half), f32)
    whole_message = shape((coded_rows(first, lines), half), i16)
    sum_message = shape((coded_rows(rest, lines), half), i16)
    unit = 4 * lines * lines * half

    inputs = (resp_start, across_offsets, resp_values, across_kernels, cube)
    keep, send = call(
        fold,
        [pltpu.with_memory_space_constraint(x, pltpu.HBM) for x in inputs],
        [HBM] * 5,
        [part, part],
        scratch=[
            pltpu.SMEM(resp_start.shape, jnp.int32),
            pltpu.SMEM(across_offsets.shape, jnp.int32),
            pltpu.VMEM(resp_values.shape, resp_values.dtype),
            pltpu.VMEM(resp_values.shape, f32),
            pltpu.SMEM(resp_values.shape, f32),
            pltpu.VMEM(across_kernels.shape, across_kernels.dtype),
            pltpu.VMEM(cube.shape, cube.dtype),
            pltpu.VMEM((count, lines, cols), f32),
            pltpu.VMEM((cols, cols), across_kernels.dtype),
            pltpu.SMEM((count,), jnp.int32),
            pltpu.SemaphoreType.DMA((5,)),
            pltpu.SemaphoreType.DMA((lines // ROWS,)),
        ],
        flops=4 * count * lines * cols * cols,
    )
    other = lax.ppermute(send, "band", swap)
    total, message, product = call(
        share, (*along, keep, other), [SMEM] + [VMEM] * 3, [part, whole_message, sum_message]
    )
    near = lax.ppermute(message, "line", partner)
    product = lax.ppermute(product, "line", odd_up)
    base, term = call(
        centre,
        (*along, total),
        [SMEM] + [VMEM] * 2,
        [part, shape((rest, lines, half), f32)],
        flops=unit * (count + rest),
    )
    near, product, base = lax.optimization_barrier((near, product, base))
    (sums,) = call(relay, (term, product), [VMEM] * 2, [sum_message])
    sums = lax.ppermute(sums, "line", partner)
    far = lax.ppermute(near, "line", even_up)
    base, other_base = call(
        beside,
        (*along, base, near, lax.ppermute(base, "band", swap), lax.ppermute(near, "band", swap)),
        [SMEM] + [VMEM] * 5,
        [part, part],
        flops=2 * unit * first,
    )
    far, sums, base, other_base = lax.optimization_barrier((far, sums, base, other_base))
    other_sums = lax.ppermute(sums, "band", swap)
    other_far = lax.ppermute(far, "band", swap)
    outs = [shape((count, lines, cols), f32), shape((lines, cols), f32)]
    scratch = [
        pltpu.VMEM((count, lines, half), f32),
        pltpu.VMEM((lines, half), f32),
        pltpu.SemaphoreType.DMA((count + 1,)),
    ]
    specs = [SMEM] + [VMEM] * 5
    made = call(
        functools.partial(finish, False),
        (*along, observed, base, far, sums),
        specs,
        outs,
        scratch=scratch,
        out_specs=[HBM] * 2,
        flops=unit * first,
    )
    made = call(
        functools.partial(finish, True),
        (*along, observed, other_base, other_far, other_sums, *made),
        specs + [HBM] * 2,
        outs,
        scratch=scratch,
        out_specs=[HBM] * 2,
        aliases={6: 0, 7: 1},
        flops=unit * first,
    )
    return tuple(made)


def solution(mesh):
    placed = (
        P("band", ("slab", "line"), None),
        P(None, ("slab", "line"), None),
        P(),
        P(),
        P(),
        P(),
        P(),
        P(),
    )
    return jax.shard_map(
        on_device,
        mesh=mesh,
        in_specs=placed,
        out_specs=(P(None, ("slab", "line"), None), P(("slab", "line"), None)),
        check_vma=False,
    )
```

```python
import functools
import math

import jax
import jax.numpy as jnp
from jax import lax
from jax.experimental import pallas as pl
from jax.experimental.pallas import tpu as pltpu
from jax.sharding import PartitionSpec as P

BLK = 128
SPB = 10
STEPS = 16.0
PEAK = 32000.0


def which(offsets, shift):
    return sum(
        jnp.where(offsets[k] == shift, jnp.int32(k), jnp.int32(0)) for k in range(offsets.shape[0])
    )


def split(value):
    high = value.astype(jnp.bfloat16)
    low = (value - high.astype(jnp.float32)).astype(jnp.bfloat16)
    return high, low


SMEM = pl.BlockSpec(memory_space=pltpu.SMEM)
VMEM = pl.BlockSpec(memory_space=pltpu.VMEM)
HBM = pl.BlockSpec(memory_space=pltpu.HBM)
ROWS = 64


def call(kernel, inputs, specs, outs, scratch=(), out_specs=None, aliases=None, flops=0):
    moved = sum(x.size * x.dtype.itemsize for x in (*inputs, *outs))
    return pl.pallas_call(
        kernel,
        in_specs=specs,
        out_specs=out_specs or [VMEM] * len(outs),
        out_shape=outs,
        scratch_shapes=scratch,
        input_output_aliases=aliases or {},
        compiler_params=pltpu.CompilerParams(vmem_limit_bytes=32 * 2**20),
        cost_estimate=pl.CostEstimate(flops=flops, bytes_accessed=moved, transcendentals=0),
        name=(kernel.func if isinstance(kernel, functools.partial) else kernel).__name__,
    )(*inputs)


def ownership(count):
    pairs = count // 2
    return pairs, count % 2, 2 * pairs + count % 2


def units_of(core, count):
    pairs, odd, _ = ownership(count)
    first = core * (pairs + odd)
    return [(first + i, c) for i in range(pairs) for c in range(2)] + [(pairs, core)] * odd


def fold(
    start_in,
    offsets_in,
    values_in,
    blocks_in,
    cube_in,
    keep,
    send,
    start,
    offsets,
    values,
    wide,
    weights,
    blocks,
    cube,
    folded,
    table,
    order,
    small,
    large,
):
    bands, lines, cols = cube.shape
    count, window = values.shape
    half = cols // 2
    group = math.gcd(SPB, bands)
    me = lax.axis_index("band")
    pairs = ((start_in, start), (values_in, values), (offsets_in, offsets), (blocks_in, blocks))
    copies = [pltpu.make_async_copy(a, b, small.at[i]) for i, (a, b) in enumerate(pairs)]

    def arrive(q):
        at = pl.ds(q * group, group)
        return pltpu.make_async_copy(cube_in.at[at], cube.at[at], large.at[q])

    for copy in copies:
        copy.start()
    for q in range(bands // group):
        arrive(q).start()
    copies[1].wait()
    wide[...] = values[...].astype(jnp.float32)
    spread = pltpu.make_async_copy(wide, weights, small.at[len(pairs)])
    spread.start()
    copies[0].wait()

    places = [SPB * start[m] - bands * me for m in range(count)]
    ranks = [jnp.int32(0)] * count
    for m in range(count):
        for n in range(m + 1, count):
            later = (places[n] < places[m]).astype(jnp.int32)
            ranks[m] = ranks[m] + later
            ranks[n] = ranks[n] + (1 - later)
    before = jnp.int32(0)
    until = jnp.int32(0)
    for m in range(count):
        order[ranks[m]] = jnp.int32(m)
        before = before + (places[m] <= -window).astype(jnp.int32)
        until = until + (places[m] < bands).astype(jnp.int32)

    def clear(n, carry):
        folded[order[n]] = jnp.zeros((lines, cols), jnp.float32)
        return carry

    lax.fori_loop(0, before, clear, 0)
    lax.fori_loop(until, count, clear, 0)
    copies[2].wait()
    copies[3].wait()
    for r in range(2):
        for c in range(2):
            pick = which(offsets, jnp.int32(c - r))
            table[r * half : (r + 1) * half, c * half : (c + 1) * half] = blocks[pick]
    spread.wait()

    def ready(q, carry):
        arrive(q).wait()
        return carry

    def one(n, arrived):
        m = order[n]
        low = SPB * start[m] - bands * me
        stop = jnp.minimum(low + window, bands)
        needed = lax.div(stop + (group - 1), jnp.int32(group))
        lax.fori_loop(arrived, needed, ready, 0)
        whole = jnp.logical_and(low >= 0, low + window <= bands)

        def term(band, weight, r):
            return weight * cube[band, r : r + ROWS, :].astype(jnp.float32)

        @pl.when(whole)
        def _():
            for r in range(0, lines, ROWS):
                total = term(low, weights[m, 0], r)
                for j in range(1, window):
                    total = total + term(low + j, weights[m, j], r)
                folded[m, r : r + ROWS, :] = total

        @pl.when(jnp.logical_not(whole))
        def _():
            first = jnp.maximum(low, 0)
            for r in range(0, lines, ROWS):

                def some(t, total):
                    for i in range(group):
                        band = first + t * group + i
                        total = total + term(band, weights[m, band - low], r)
                    return total

                folded[m, r : r + ROWS, :] = lax.fori_loop(
                    0,
                    lax.div(stop - first, jnp.int32(group)),
                    some,
                    jnp.zeros((ROWS, cols), jnp.float32),
                )

        return jnp.maximum(arrived, needed)

    arrived = lax.fori_loop(before, until, one, jnp.int32(0))
    lax.fori_loop(arrived, bands // group, ready, 0)

    dims = (((1,), (1,)), ((), ()))
    side = table[...]
    planes, odd, units = ownership(count)

    def across(value):
        high, low = split(value)
        out = lax.dot_general(high, side, dims, preferred_element_type=jnp.float32)
        return out + lax.dot_general(low, side, dims, preferred_element_type=jnp.float32)

    for owner, out in ((me, keep), (1 - me, send)):
        base = owner * (planes + odd)
        for i in range(planes):
            made = across(folded[base + i])
            out[2 * i] = made[:, :half]
            out[2 * i + 1] = made[:, half:]
    if odd:
        made = across(folded[planes])
        left, right = made[:, :half], made[:, half:]
        keep[units - 1] = jnp.where(me == 0, left, right)
        send[units - 1] = jnp.where(me == 0, right, left)


def coded_rows(count, lines):
    return count * lines + -(-count // 16) * 16


def encode(count, plane, message):
    levels = []
    for m in range(count):
        value = plane(m)
        lines, half = value.shape
        largest = jnp.max(jnp.abs(value), axis=0, keepdims=True)
        level = jnp.ceil(jnp.log2(jnp.maximum(largest, 1e-30)) * STEPS)
        factor = PEAK * jnp.exp2(level * (-1.0 / STEPS))
        coded = jnp.floor(value * factor + 0.5).astype(jnp.int32)
        message[m * lines : (m + 1) * lines, :] = coded.astype(jnp.int16)
        levels.append(level)
    spare = message.shape[0] - count * lines - count
    levels.append(jnp.zeros((spare, half), jnp.float32))
    levels = jnp.concatenate(levels, axis=0)
    message[count * lines :, :] = levels.astype(jnp.int32).astype(jnp.int16)


def decode(message, count, lines):
    level = message[count * lines :, :].astype(jnp.int32).astype(jnp.float32)
    scale = jnp.exp2(level * (1.0 / STEPS)) * (1.0 / PEAK)

    def plane(m):
        coded = message[m * lines : (m + 1) * lines, :].astype(jnp.int32).astype(jnp.float32)
        return coded * scale[m : m + 1, :]

    return plane


def blurred(block, value):
    high, low = split(value)
    both = jnp.dot(
        block, jnp.concatenate([high, low], axis=1), preferred_element_type=jnp.float32
    )
    return both[:, : value.shape[1]] + both[:, value.shape[1] :]


def side_step():
    return jnp.where(lax.axis_index("line") % 2 == 0, jnp.int32(1), jnp.int32(-1))


def by_core(zero, one):
    me = lax.axis_index("band")
    pl.when(me == 0)(zero)
    pl.when(me != 0)(one)


def share(offsets, blocks, keep, other, total, message):
    units = keep.shape[0]
    total[...] = keep[...] + other[...]
    block = blocks[which(offsets, side_step())]
    by_core(
        lambda: encode(units, lambda m: total[m], message),
        lambda: encode(units, lambda m: blurred(block, total[m]), message),
    )


def centre(offsets, blocks, total, other_total, base, other_base, term):
    units = total.shape[0]
    here = blocks[which(offsets, jnp.int32(0))]
    block = blocks[which(offsets, -side_step())]
    for m in range(units):
        base[m] = blurred(here, total[m])
        other_base[m] = blurred(here, other_total[m])
        term[m] = blurred(block, total[m])


def relay(term, received, message):
    units, lines, _ = term.shape

    def forward():
        message[...] = received[...]

    def add():
        plane = decode(received, units, lines)
        encode(units, lambda m: term[m] + plane(m), message)

    by_core(forward, add)


def beside(offsets, blocks, base, near, other_base, other_near, total):
    units, lines, _ = base.shape
    block = blocks[which(offsets, side_step())]

    def work(source, message):
        plane = decode(message, units, lines)
        for m in range(units):
            total[m] = source[m] + blurred(block, plane(m))

    by_core(lambda: work(base, near), lambda: work(other_base, other_near))

def arccos(x):
    size = jnp.abs(x)
    big = size > 0.5
    z = jnp.where(big, 0.5 * (1.0 - size), size * size)
    root = jnp.where(big, jnp.sqrt(z), size)
    poly = 4.2163199048e-2
    for term in (2.4181311049e-2, 4.5470025998e-2, 7.4953002686e-2, 1.6666752422e-1):
        poly = poly * z + term
    arcsin = poly * z * root + root
    pi = 3.14159265358979
    inner = jnp.where(x < 0, 0.5 * pi + arcsin, 0.5 * pi - arcsin)
    outer = jnp.where(x < 0, pi - 2.0 * arcsin, 2.0 * arcsin)
    return jnp.where(big, outer, inner)


def finish(second, offsets, blocks, observed, spread, summed, message, *rest):
    if second:
        sums, image, angles, made, angle, sems = rest[0], *rest[-5:]
    else:
        image, sums, made, sems = rest
    units, lines, half = spread.shape
    count = observed.shape[0]
    plane = decode(message, units, lines)

    def work(core):
        block = blocks[which(offsets, -side_step())]
        zero = jnp.zeros((lines, half), jnp.float32)
        inner, left = [zero, zero], [zero, zero]
        for n, (m, c) in enumerate(units_of(core, count)):
            at = slice(c * half, (c + 1) * half)
            if core == 0:
                value = spread[n] + blurred(block, plane(n))
            else:
                value = summed[n] + plane(n)
            made[n] = value
            pltpu.make_async_copy(made.at[n], image.at[m, :, at], sems.at[n]).start()
            inner[c] = inner[c] + value * observed[m, :, at].astype(jnp.float32)
            left[c] = left[c] + value * value
        for c in range(2):
            at = slice(c * half, (c + 1) * half)
            if not second:
                sums[0, :, at] = inner[c]
                sums[1, :, at] = left[c]
                continue
            right = zero
            for m in range(count):
                seen = observed[m, :, at].astype(jnp.float32)
                right = right + seen * seen
            bound = jnp.sqrt(left[c] + sums[1, :, at]) * jnp.sqrt(right)
            ratio = (inner[c] + sums[0, :, at]) / jnp.maximum(bound, 1.0)
            angle[:, at] = arccos(jnp.clip(ratio, -1.0, 1.0))
        if second:
            last = pltpu.make_async_copy(angle, angles, sems.at[units])
            last.start()
        for n, (m, c) in enumerate(units_of(core, count)):
            at = slice(c * half, (c + 1) * half)
            pltpu.make_async_copy(made.at[n], image.at[m, :, at], sems.at[n]).wait()
        if second:
            last.wait()

    if second:
        by_core(lambda: work(1), lambda: work(0))
    else:
        by_core(lambda: work(0), lambda: work(1))


def on_device(
    cube,
    observed,
    along_kernels,
    along_offsets,
    across_kernels,
    across_offsets,
    resp_start,
    resp_values,
):
    f32, i16 = jnp.float32, jnp.int16
    size = lax.axis_size("line")
    bands, lines, cols = cube.shape
    count = resp_values.shape[0]
    half = cols // 2
    _, _, units = ownership(count)
    shape = jax.ShapeDtypeStruct
    swap = [(0, 1), (1, 0)]
    partner = [(i, i ^ 1) for i in range(size)]
    even_up = [(i, i + 2) for i in range(0, size - 2, 2)] + [(i, i - 2) for i in range(3, size, 2)]
    odd_up = [(i, i + 2) for i in range(1, size - 2, 2)] + [(i, i - 2) for i in range(2, size, 2)]

    def cores(zero, one):
        return [(2 * a, 2 * b) for a, b in zero] + [(2 * a + 1, 2 * b + 1) for a, b in one]

    along = (along_offsets, along_kernels)
    part = shape((units, lines, half), f32)
    coded = shape((coded_rows(units, lines), half), i16)
    unit = 4 * lines * lines * half

    inputs = (resp_start, across_offsets, resp_values, across_kernels, cube)
    keep, send = call(
        fold,
        [pltpu.with_memory_space_constraint(x, pltpu.HBM) for x in inputs],
        [HBM] * 5,
        [part, part],
        scratch=[
            pltpu.SMEM(resp_start.shape, jnp.int32),
            pltpu.SMEM(across_offsets.shape, jnp.int32),
            pltpu.VMEM(resp_values.shape, resp_values.dtype),
            pltpu.VMEM(resp_values.shape, f32),
            pltpu.SMEM(resp_values.shape, f32),
            pltpu.VMEM(across_kernels.shape, across_kernels.dtype),
            pltpu.VMEM(cube.shape, cube.dtype),
            pltpu.VMEM((count, lines, cols), f32),
            pltpu.VMEM((cols, cols), across_kernels.dtype),
            pltpu.SMEM((count,), jnp.int32),
            pltpu.SemaphoreType.DMA((5,)),
            pltpu.SemaphoreType.DMA((bands // math.gcd(SPB, bands),)),
        ],
        flops=4 * count * lines * cols * cols,
    )
    other = lax.ppermute(send, "band", swap)
    total, message = call(share, (*along, keep, other), [SMEM] + [VMEM] * 3, [part, coded])
    near = lax.ppermute(message, ("line", "band"), cores(partner, odd_up))
    other_total = lax.ppermute(total, "band", swap)
    base, other_base, term = call(
        centre, (*along, total, other_total), [SMEM] + [VMEM] * 3, [part] * 3, flops=unit * units * 3
    )
    near, term = lax.optimization_barrier((near, term))
    (message,) = call(relay, (term, near), [VMEM] * 2, [coded])
    message, near = lax.optimization_barrier((message, near))
    far = lax.ppermute(message, ("line", "band"), cores(even_up, partner))
    other_near = lax.ppermute(near, "band", swap)
    (spread,) = call(
        beside,
        (*along, base, near, other_base, other_near),
        [SMEM] + [VMEM] * 5,
        [part],
        flops=unit * units,
    )
    far, spread = lax.optimization_barrier((far, spread))
    other_far = lax.ppermute(far, "band", swap)
    image = shape((count, lines, cols), f32)
    made = [pltpu.VMEM((units, lines, half), f32)]
    image, sums = call(
        functools.partial(finish, False),
        (*along, observed, spread, base, far),
        [SMEM] + [VMEM] * 5,
        [image, shape((2, lines, cols), f32)],
        scratch=made + [pltpu.SemaphoreType.DMA((units,))],
        out_specs=[HBM, VMEM],
        flops=unit * units,
    )
    image, angles = call(
        functools.partial(finish, True),
        (*along, observed, spread, other_base, other_far, sums, image),
        [SMEM] + [VMEM] * 6 + [HBM],
        [image, shape((lines, cols), f32)],
        scratch=made + [pltpu.VMEM((lines, cols), f32), pltpu.SemaphoreType.DMA((units + 1,))],
        out_specs=[HBM] * 2,
        aliases={7: 0},
        flops=unit * units,
    )
    return image, angles


def solution(mesh):
    placed = (
        P("band", ("slab", "line"), None),
        P(None, ("slab", "line"), None),
        P(),
        P(),
        P(),
        P(),
        P(),
        P(),
    )
    return jax.shard_map(
        on_device,
        mesh=mesh,
        in_specs=placed,
        out_specs=(P(None, ("slab", "line"), None), P(("slab", "line"), None)),
        check_vma=False,
    )
```

```python
import functools
import math

import jax
import jax.numpy as jnp
from jax import lax
from jax.experimental import pallas as pl
from jax.experimental.pallas import tpu as pltpu
from jax.sharding import PartitionSpec as P

BLK = 128
SPB = 10
STEPS = 16.0
PEAK = 32000.0


def which(offsets, shift):
    return sum(
        jnp.where(offsets[k] == shift, jnp.int32(k), jnp.int32(0)) for k in range(offsets.shape[0])
    )


def split(value):
    high = value.astype(jnp.bfloat16)
    low = (value - high.astype(jnp.float32)).astype(jnp.bfloat16)
    return high, low


SMEM = pl.BlockSpec(memory_space=pltpu.SMEM)
VMEM = pl.BlockSpec(memory_space=pltpu.VMEM)
HBM = pl.BlockSpec(memory_space=pltpu.HBM)
ROWS = 64


def call(kernel, inputs, specs, outs, scratch=(), out_specs=None, aliases=None, flops=0):
    moved = sum(x.size * x.dtype.itemsize for x in (*inputs, *outs))
    return pl.pallas_call(
        kernel,
        in_specs=specs,
        out_specs=out_specs or [VMEM] * len(outs),
        out_shape=outs,
        scratch_shapes=scratch,
        input_output_aliases=aliases or {},
        compiler_params=pltpu.CompilerParams(vmem_limit_bytes=32 * 2**20),
        cost_estimate=pl.CostEstimate(flops=flops, bytes_accessed=moved, transcendentals=0),
        name=(kernel.func if isinstance(kernel, functools.partial) else kernel).__name__,
    )(*inputs)


def ownership(count):
    pairs = count // 2
    return pairs, count % 2, 2 * pairs + count % 2


def units_of(core, count):
    pairs, odd, _ = ownership(count)
    first = core * (pairs + odd)
    return [(first + i, c) for i in range(pairs) for c in range(2)] + [(pairs, core)] * odd


def fold(
    start_in,
    offsets_in,
    values_in,
    blocks_in,
    along_offsets_in,
    along_blocks_in,
    cube_in,
    keep,
    send,
    picked,
    start,
    offsets,
    values,
    wide,
    weights,
    blocks,
    along_offsets,
    along_blocks,
    cube,
    folded,
    table,
    order,
    small,
    large,
):
    bands, lines, cols = cube.shape
    count, window = values.shape
    half = cols // 2
    group = math.gcd(SPB, bands)
    me = lax.axis_index("band")
    pairs = (
        (start_in, start),
        (values_in, values),
        (offsets_in, offsets),
        (blocks_in, blocks),
        (along_offsets_in, along_offsets),
        (along_blocks_in, along_blocks),
    )
    copies = [pltpu.make_async_copy(a, b, small.at[i]) for i, (a, b) in enumerate(pairs)]

    def arrive(q):
        at = pl.ds(q * group, group)
        return pltpu.make_async_copy(cube_in.at[at], cube.at[at], large.at[q])

    for copy in copies:
        copy.start()
    for q in range(bands // group):
        arrive(q).start()
    copies[1].wait()
    wide[...] = values[...].astype(jnp.float32)
    spread = pltpu.make_async_copy(wide, weights, small.at[len(pairs)])
    spread.start()
    copies[0].wait()

    places = [SPB * start[m] - bands * me for m in range(count)]
    ranks = [jnp.int32(0)] * count
    for m in range(count):
        for n in range(m + 1, count):
            later = (places[n] < places[m]).astype(jnp.int32)
            ranks[m] = ranks[m] + later
            ranks[n] = ranks[n] + (1 - later)
    before = jnp.int32(0)
    until = jnp.int32(0)
    for m in range(count):
        order[ranks[m]] = jnp.int32(m)
        before = before + (places[m] <= -window).astype(jnp.int32)
        until = until + (places[m] < bands).astype(jnp.int32)

    def clear(n, carry):
        folded[order[n]] = jnp.zeros((lines, cols), jnp.float32)
        return carry

    lax.fori_loop(0, before, clear, 0)
    lax.fori_loop(until, count, clear, 0)
    for copy in copies[2:]:
        copy.wait()
    for r in range(2):
        for c in range(2):
            block = blocks[which(offsets, jnp.int32(r - c))].astype(jnp.float32).T
            for top in (0, cols):
                at = slice(top + r * half, top + (r + 1) * half)
                table[at, c * half : (c + 1) * half] = block.astype(jnp.bfloat16)
    step = side_step()
    for i, shift in enumerate((jnp.int32(0), step, -step)):
        picked[i] = along_blocks[which(along_offsets, shift)]
    spread.wait()

    def ready(q, carry):
        arrive(q).wait()
        return carry

    def one(n, arrived):
        m = order[n]
        low = SPB * start[m] - bands * me
        stop = jnp.minimum(low + window, bands)
        needed = lax.div(stop + (group - 1), jnp.int32(group))
        lax.fori_loop(arrived, needed, ready, 0)
        whole = jnp.logical_and(low >= 0, low + window <= bands)

        def term(band, weight, r):
            return weight * cube[band, r : r + ROWS, :].astype(jnp.float32)

        @pl.when(whole)
        def _():
            for r in range(0, lines, ROWS):
                total = term(low, weights[m, 0], r)
                for j in range(1, window):
                    total = total + term(low + j, weights[m, j], r)
                folded[m, r : r + ROWS, :] = total

        @pl.when(jnp.logical_not(whole))
        def _():
            first = jnp.maximum(low, 0)
            for r in range(0, lines, ROWS):

                def some(t, total):
                    for i in range(group):
                        band = first + t * group + i
                        total = total + term(band, weights[m, band - low], r)
                    return total

                folded[m, r : r + ROWS, :] = lax.fori_loop(
                    0,
                    lax.div(stop - first, jnp.int32(group)),
                    some,
                    jnp.zeros((ROWS, cols), jnp.float32),
                )

        return jnp.maximum(arrived, needed)

    arrived = lax.fori_loop(before, until, one, jnp.int32(0))
    lax.fori_loop(arrived, bands // group, ready, 0)

    side = table[...]
    planes, odd, units = ownership(count)

    def across(at, planes):
        value = folded[pl.ds(at, planes)].reshape(planes * lines, cols)
        both = jnp.concatenate(split(value), axis=1)
        made = jnp.dot(both, side, preferred_element_type=jnp.float32)
        return made.reshape(planes, lines, cols)

    for owner, out in ((me, keep), (1 - me, send)):
        made = across(owner * (planes + odd), planes)
        for i in range(planes):
            out[2 * i] = made[i, :, :half]
            out[2 * i + 1] = made[i, :, half:]
    if odd:
        made = across(planes, 1)[0]
        left, right = made[:, :half], made[:, half:]
        keep[units - 1] = jnp.where(me == 0, left, right)
        send[units - 1] = jnp.where(me == 0, right, left)


def coded_rows(count, lines):
    return count * lines + -(-count // 16) * 16


def encode(source, message):
    units, lines, half = source.shape
    largest = jnp.max(jnp.abs(source[...]), axis=1)
    level = jnp.ceil(jnp.log2(jnp.maximum(largest, 1e-30)) * STEPS)
    factor = PEAK * jnp.exp2(level * (-1.0 / STEPS))
    for m in range(units):
        coded = jnp.floor(source[m] * factor[m : m + 1, :] + 0.5).astype(jnp.int32)
        message[m * lines : (m + 1) * lines, :] = coded.astype(jnp.int16)
    spare = message.shape[0] - units * lines - units
    level = jnp.concatenate([level, jnp.zeros((spare, half), jnp.float32)], axis=0)
    message[units * lines :, :] = level.astype(jnp.int32).astype(jnp.int16)


def decode(message, count, lines):
    level = message[count * lines :, :].astype(jnp.int32).astype(jnp.float32)
    scale = jnp.exp2(level * (1.0 / STEPS)) * (1.0 / PEAK)

    def plane(m):
        coded = message[m * lines : (m + 1) * lines, :].astype(jnp.int32).astype(jnp.float32)
        return coded * scale[m : m + 1, :]

    return plane


def blurred(filters, count, plane, put):
    wide = jnp.concatenate([filters, filters], axis=1)
    for m in range(0, count, 2):
        parts = [split(plane(n)) for n in range(m, min(m + 2, count))]
        high = jnp.concatenate([p[0] for p in parts], axis=1)
        low = jnp.concatenate([p[1] for p in parts], axis=1)
        made = jnp.dot(
            wide, jnp.concatenate([high, low], axis=0), preferred_element_type=jnp.float32
        )
        half = made.shape[1] // len(parts)
        for i in range(len(parts)):
            put(m + i, made[:, i * half : (i + 1) * half])


def side_step():
    return jnp.where(lax.axis_index("line") % 2 == 0, jnp.int32(1), jnp.int32(-1))


def by_core(zero, one):
    me = lax.axis_index("band")
    pl.when(me == 0)(zero)
    pl.when(me != 0)(one)


def share(picked, keep, other, total, message, product):
    total[...] = keep[...] + other[...]

    def summing():
        def put(m, value):
            product[m] = value

        blurred(picked[1], total.shape[0], lambda m: total[m], put)
        encode(product, message)

    by_core(lambda: encode(total, message), summing)


def centre(picked, total, base, term):
    units, lines, _ = total.shape

    def only(m, value):
        base[m] = value

    def both(m, value):
        base[m] = value[:lines]
        term[m] = value[lines:]

    stack = jnp.concatenate([picked[0], picked[2]], axis=0)
    by_core(
        lambda: blurred(picked[0], units, lambda m: total[m], only),
        lambda: blurred(stack, units, lambda m: total[m], both),
    )


def relay(term, received, message, total):
    units, lines, _ = term.shape

    def forward():
        message[...] = received[...]

    def add():
        plane = decode(received, units, lines)
        for m in range(units):
            total[m] = term[m] + plane(m)
        encode(total, message)

    by_core(forward, add)


def beside(picked, base, near, total):
    units, lines, _ = base.shape

    def put(m, value):
        total[m] = base[m] + value

    def keep():
        total[...] = base[...]

    by_core(lambda: blurred(picked[1], units, decode(near, units, lines), put), keep)


def settle(picked, base, received, total):
    units, lines, _ = base.shape
    plane = decode(received, units, lines)

    def put(m, value):
        total[m] = base[m] + value

    def add():
        for m in range(units):
            put(m, plane(m))

    by_core(lambda: blurred(picked[2], units, plane, put), add)

def arccos(x):
    size = jnp.abs(x)
    big = size > 0.5
    z = jnp.where(big, 0.5 * (1.0 - size), size * size)
    root = jnp.where(big, jnp.sqrt(z), size)
    poly = 4.2163199048e-2
    for term in (2.4181311049e-2, 4.5470025998e-2, 7.4953002686e-2, 1.6666752422e-1):
        poly = poly * z + term
    arcsin = poly * z * root + root
    pi = 3.14159265358979
    inner = jnp.where(x < 0, 0.5 * pi + arcsin, 0.5 * pi - arcsin)
    outer = jnp.where(x < 0, pi - 2.0 * arcsin, 2.0 * arcsin)
    return jnp.where(big, outer, inner)


def finish(second, observed, value, *rest):
    if second:
        sums, _, image, angles, angle, sems = rest
    else:
        image, sums, sems = rest
    units, lines, half = value.shape
    count = observed.shape[0]

    def work(core):
        places = [(m, slice(c * half, (c + 1) * half)) for m, c in units_of(core, count)]
        copies = [
            pltpu.make_async_copy(value.at[n], image.at[m, :, at], sems.at[n])
            for n, (m, at) in enumerate(places)
        ]
        for copy in copies:
            copy.start()
        for c in range(2):
            at = slice(c * half, (c + 1) * half)
            inner = jnp.zeros((lines, half), jnp.float32)
            left = jnp.zeros((lines, half), jnp.float32)
            for n, (m, where) in enumerate(places):
                if where == at:
                    inner = inner + value[n] * observed[m, :, at].astype(jnp.float32)
                    left = left + value[n] * value[n]
            if second:
                bound = jnp.sqrt(left + sums[1, :, at]) * sums[2, :, at]
                ratio = (inner + sums[0, :, at]) / jnp.maximum(bound, 1.0)
                angle[:, at] = arccos(jnp.clip(ratio, -1.0, 1.0))
            else:
                right = jnp.zeros((lines, half), jnp.float32)
                for m in range(count):
                    seen = observed[m, :, at].astype(jnp.float32)
                    right = right + seen * seen
                sums[0, :, at] = inner
                sums[1, :, at] = left
                sums[2, :, at] = jnp.sqrt(right)
        if second:
            copies.append(pltpu.make_async_copy(angle, angles, sems.at[units]))
            copies[-1].start()
        for copy in copies:
            copy.wait()

    if second:
        by_core(lambda: work(1), lambda: work(0))
    else:
        by_core(lambda: work(0), lambda: work(1))


def on_device(
    cube,
    observed,
    along_kernels,
    along_offsets,
    across_kernels,
    across_offsets,
    resp_start,
    resp_values,
):
    f32, i16 = jnp.float32, jnp.int16
    size = lax.axis_size("line")
    bands, lines, cols = cube.shape
    count = resp_values.shape[0]
    half = cols // 2
    _, _, units = ownership(count)
    shape = jax.ShapeDtypeStruct
    swap = [(0, 1), (1, 0)]
    partner = [(i, i ^ 1) for i in range(size)]
    even_up = [(i, i + 2) for i in range(0, size - 2, 2)] + [(i, i - 2) for i in range(3, size, 2)]
    odd_up = [(i, i + 2) for i in range(1, size - 2, 2)] + [(i, i - 2) for i in range(2, size, 2)]

    def cores(zero, one):
        return [(2 * a, 2 * b) for a, b in zero] + [(2 * a + 1, 2 * b + 1) for a, b in one]

    part = shape((units, lines, half), f32)
    coded = shape((coded_rows(units, lines), half), i16)
    unit = 4 * lines * lines * half

    inputs = (
        resp_start,
        across_offsets,
        resp_values,
        across_kernels,
        along_offsets,
        along_kernels,
        cube,
    )
    keep, send, picked = call(
        fold,
        [pltpu.with_memory_space_constraint(x, pltpu.HBM) for x in inputs],
        [HBM] * len(inputs),
        [part, part, shape(along_kernels.shape, along_kernels.dtype)],
        scratch=[
            pltpu.SMEM(resp_start.shape, jnp.int32),
            pltpu.SMEM(across_offsets.shape, jnp.int32),
            pltpu.VMEM(resp_values.shape, resp_values.dtype),
            pltpu.VMEM(resp_values.shape, f32),
            pltpu.SMEM(resp_values.shape, f32),
            pltpu.VMEM(across_kernels.shape, across_kernels.dtype),
            pltpu.SMEM(along_offsets.shape, jnp.int32),
            pltpu.VMEM(along_kernels.shape, along_kernels.dtype),
            pltpu.VMEM(cube.shape, cube.dtype),
            pltpu.VMEM((count, lines, cols), f32),
            pltpu.VMEM((2 * cols, cols), across_kernels.dtype),
            pltpu.SMEM((count,), jnp.int32),
            pltpu.SemaphoreType.DMA((len(inputs),)),
            pltpu.SemaphoreType.DMA((bands // math.gcd(SPB, bands),)),
        ],
        flops=4 * count * lines * cols * cols,
    )
    work = [pltpu.VMEM(part.shape, f32)]
    other = lax.ppermute(send, "band", swap)
    total, message = call(share, (picked, keep, other), [VMEM] * 3, [part, coded], scratch=work)
    near = lax.ppermute(message, ("line", "band"), cores(partner, odd_up))
    base, term = call(centre, (picked, total), [VMEM] * 2, [part] * 2, flops=2 * unit * units)
    near, base, term = lax.optimization_barrier((near, base, term))
    (message,) = call(relay, (term, near), [VMEM] * 2, [coded], scratch=work)
    message, near, base = lax.optimization_barrier((message, near, base))
    far = lax.ppermute(message, ("line", "band"), cores(even_up, partner))
    (base,) = call(beside, (picked, base, near), [VMEM] * 3, [part], flops=unit * units)
    (mine,) = call(settle, (picked, base, far), [VMEM] * 3, [part], flops=unit * units)
    other = lax.ppermute(mine, "band", swap)
    image = shape((count, lines, cols), f32)
    image, sums = call(
        functools.partial(finish, False),
        (observed, mine),
        [VMEM] * 2,
        [image, shape((3, lines, cols), f32)],
        scratch=[pltpu.SemaphoreType.DMA((units,))],
        out_specs=[HBM, VMEM],
    )
    image, angles = call(
        functools.partial(finish, True),
        (observed, other, sums, image),
        [VMEM] * 3 + [HBM],
        [image, shape((lines, cols), f32)],
        scratch=[pltpu.VMEM((lines, cols), f32), pltpu.SemaphoreType.DMA((units + 1,))],
        out_specs=[HBM] * 2,
        aliases={3: 0},
    )
    return image, angles


def solution(mesh):
    placed = (
        P("band", ("slab", "line"), None),
        P(None, ("slab", "line"), None),
        P(),
        P(),
        P(),
        P(),
        P(),
        P(),
    )
    return jax.shard_map(
        on_device,
        mesh=mesh,
        in_specs=placed,
        out_specs=(P(None, ("slab", "line"), None), P(("slab", "line"), None)),
        check_vma=False,
    )
```

```python
import functools
import math

import jax
import jax.numpy as jnp
from jax import lax
from jax.experimental import pallas as pl
from jax.experimental.pallas import tpu as pltpu
from jax.sharding import PartitionSpec as P

BLK = 128
SPB = 10
STEPS = 16.0
PEAK = 32000.0


def which(offsets, shift):
    return sum(
        jnp.where(offsets[k] == shift, jnp.int32(k), jnp.int32(0)) for k in range(offsets.shape[0])
    )


def split(value):
    high = value.astype(jnp.bfloat16)
    low = (value - high.astype(jnp.float32)).astype(jnp.bfloat16)
    return high, low


SMEM = pl.BlockSpec(memory_space=pltpu.SMEM)
VMEM = pl.BlockSpec(memory_space=pltpu.VMEM)
HBM = pl.BlockSpec(memory_space=pltpu.HBM)
ROWS = 64


def call(kernel, inputs, specs, outs, scratch=(), out_specs=None, aliases=None, flops=0):
    moved = sum(x.size * x.dtype.itemsize for x in (*inputs, *outs))
    return pl.pallas_call(
        kernel,
        in_specs=specs,
        out_specs=out_specs or [VMEM] * len(outs),
        out_shape=outs,
        scratch_shapes=scratch,
        input_output_aliases=aliases or {},
        compiler_params=pltpu.CompilerParams(vmem_limit_bytes=32 * 2**20),
        cost_estimate=pl.CostEstimate(flops=flops, bytes_accessed=moved, transcendentals=0),
        name=(kernel.func if isinstance(kernel, functools.partial) else kernel).__name__,
    )(*inputs)


def ownership(count):
    pairs = count // 2
    return pairs, count % 2, 2 * pairs + count % 2


def units_of(core, count):
    pairs, odd, _ = ownership(count)
    first = core * (pairs + odd)
    return [(first + i, c) for i in range(pairs) for c in range(2)] + [(pairs, core)] * odd


def fold(
    start_in,
    offsets_in,
    values_in,
    blocks_in,
    along_offsets_in,
    along_blocks_in,
    cube_in,
    keep,
    send,
    picked,
    start,
    offsets,
    values,
    wide,
    weights,
    blocks,
    along_offsets,
    along_blocks,
    cube,
    folded,
    table,
    order,
    small,
    large,
):
    bands, lines, cols = cube.shape
    count, window = values.shape
    half = cols // 2
    group = math.gcd(SPB, bands)
    me = lax.axis_index("band")
    pairs = (
        (start_in, start),
        (values_in, values),
        (offsets_in, offsets),
        (blocks_in, blocks),
        (along_offsets_in, along_offsets),
        (along_blocks_in, along_blocks),
    )
    copies = [pltpu.make_async_copy(a, b, small.at[i]) for i, (a, b) in enumerate(pairs)]

    chunks = -(-bands // window)
    last = bands - (chunks - 1) * window

    def arrive(q, size):
        at = pl.ds(q * window, size)
        return pltpu.make_async_copy(cube_in.at[at], cube.at[at], large.at[q])

    for copy in copies:
        copy.start()
    for q in range(chunks):
        arrive(q, window if q < chunks - 1 else last).start()
    copies[1].wait()
    wide[...] = values[...].astype(jnp.float32)
    spread = pltpu.make_async_copy(wide, weights, small.at[len(pairs)])
    spread.start()
    copies[0].wait()

    places = [SPB * start[m] - bands * me for m in range(count)]
    ranks = [jnp.int32(0)] * count
    for m in range(count):
        for n in range(m + 1, count):
            later = (places[n] < places[m]).astype(jnp.int32)
            ranks[m] = ranks[m] + later
            ranks[n] = ranks[n] + (1 - later)
    before = jnp.int32(0)
    until = jnp.int32(0)
    for m in range(count):
        order[ranks[m]] = jnp.int32(m)
        before = before + (places[m] <= -window).astype(jnp.int32)
        until = until + (places[m] < bands).astype(jnp.int32)

    def clear(n, carry):
        folded[order[n]] = jnp.zeros((lines, cols), jnp.float32)
        return carry

    lax.fori_loop(0, before, clear, 0)
    lax.fori_loop(until, count, clear, 0)
    for copy in copies[2:]:
        copy.wait()
    for r in range(2):
        for c in range(2):
            block = blocks[which(offsets, jnp.int32(r - c))].astype(jnp.float32).T
            for top in (0, cols):
                at = slice(top + r * half, top + (r + 1) * half)
                table[at, c * half : (c + 1) * half] = block.astype(jnp.bfloat16)
    step = side_step()
    for i, shift in enumerate((jnp.int32(0), step, -step)):
        picked[i] = along_blocks[which(along_offsets, shift)]
    spread.wait()

    def ready(q, carry):
        pl.when(q < chunks - 1)(lambda: arrive(q, window).wait())
        pl.when(q == chunks - 1)(lambda: arrive(chunks - 1, last).wait())
        return carry

    def one(n, arrived):
        m = order[n]
        low = SPB * start[m] - bands * me
        stop = jnp.minimum(low + window, bands)
        needed = lax.div(stop - 1, jnp.int32(window)) + 1
        lax.fori_loop(arrived, needed, ready, 0)
        whole = jnp.logical_and(low >= 0, low + window <= bands)

        def term(band, weight, r):
            return weight * cube[band, r : r + ROWS, :].astype(jnp.float32)

        @pl.when(whole)
        def _():
            for r in range(0, lines, ROWS):
                total = term(low, weights[m, 0], r)
                for j in range(1, window):
                    total = total + term(low + j, weights[m, j], r)
                folded[m, r : r + ROWS, :] = total

        @pl.when(jnp.logical_not(whole))
        def _():
            first = jnp.maximum(low, 0)
            for r in range(0, lines, ROWS):

                def some(t, total):
                    for i in range(group):
                        band = first + t * group + i
                        total = total + term(band, weights[m, band - low], r)
                    return total

                folded[m, r : r + ROWS, :] = lax.fori_loop(
                    0,
                    lax.div(stop - first, jnp.int32(group)),
                    some,
                    jnp.zeros((ROWS, cols), jnp.float32),
                )

        return jnp.maximum(arrived, needed)

    arrived = lax.fori_loop(before, until, one, jnp.int32(0))
    lax.fori_loop(arrived, chunks, ready, 0)

    side = table[...]
    planes, odd, units = ownership(count)

    def across(at, planes):
        value = folded[pl.ds(at, planes)].reshape(planes * lines, cols)
        both = jnp.concatenate(split(value), axis=1)
        made = jnp.dot(both, side, preferred_element_type=jnp.float32)
        return made.reshape(planes, lines, cols)

    for owner, out in ((me, keep), (1 - me, send)):
        made = across(owner * (planes + odd), planes)
        for i in range(planes):
            out[2 * i] = made[i, :, :half]
            out[2 * i + 1] = made[i, :, half:]
    if odd:
        made = across(planes, 1)[0]
        left, right = made[:, :half], made[:, half:]
        keep[units - 1] = jnp.where(me == 0, left, right)
        send[units - 1] = jnp.where(me == 0, right, left)


def coded_rows(count, lines):
    return count * lines + -(-count // 16) * 16


def encode(source, message):
    units, lines, half = source.shape
    largest = jnp.max(jnp.abs(source[...]), axis=1)
    level = jnp.ceil(jnp.log2(jnp.maximum(largest, 1e-30)) * STEPS)
    factor = PEAK * jnp.exp2(level * (-1.0 / STEPS))
    for m in range(units):
        coded = jnp.floor(source[m] * factor[m : m + 1, :] + 0.5).astype(jnp.int32)
        message[m * lines : (m + 1) * lines, :] = coded.astype(jnp.int16)
    spare = message.shape[0] - units * lines - units
    level = jnp.concatenate([level, jnp.zeros((spare, half), jnp.float32)], axis=0)
    message[units * lines :, :] = level.astype(jnp.int32).astype(jnp.int16)


def decode(message, count, lines):
    level = message[count * lines :, :].astype(jnp.int32).astype(jnp.float32)
    scale = jnp.exp2(level * (1.0 / STEPS)) * (1.0 / PEAK)

    def plane(m):
        coded = message[m * lines : (m + 1) * lines, :].astype(jnp.int32).astype(jnp.float32)
        return coded * scale[m : m + 1, :]

    return plane


def blurred(filters, count, plane, put):
    wide = jnp.concatenate([filters, filters], axis=1)
    for m in range(0, count, 2):
        parts = [split(plane(n)) for n in range(m, min(m + 2, count))]
        high = jnp.concatenate([p[0] for p in parts], axis=1)
        low = jnp.concatenate([p[1] for p in parts], axis=1)
        made = jnp.dot(
            wide, jnp.concatenate([high, low], axis=0), preferred_element_type=jnp.float32
        )
        half = made.shape[1] // len(parts)
        for i in range(len(parts)):
            put(m + i, made[:, i * half : (i + 1) * half])


def side_step():
    return jnp.where(lax.axis_index("line") % 2 == 0, jnp.int32(1), jnp.int32(-1))


def by_core(zero, one):
    me = lax.axis_index("band")
    pl.when(me == 0)(zero)
    pl.when(me != 0)(one)


def share(picked, keep, other, total, message, product):
    total[...] = keep[...] + other[...]

    def summing():
        def put(m, value):
            product[m] = value

        blurred(picked[1], total.shape[0], lambda m: total[m], put)
        encode(product, message)

    by_core(lambda: encode(total, message), summing)


def centre(picked, total, other_total, base, other_base, term):
    units = total.shape[0]

    def into(out):
        def put(m, value):
            out[m] = value

        return put

    blurred(picked[0], units, lambda m: total[m], into(base))
    blurred(picked[0], units, lambda m: other_total[m], into(other_base))
    pl.when(lax.axis_index("band") != 0)(
        lambda: blurred(picked[2], units, lambda m: total[m], into(term))
    )


def relay(term, received, message, total):
    units, lines, _ = term.shape

    def forward():
        message[...] = received[...]

    def add():
        plane = decode(received, units, lines)
        for m in range(units):
            total[m] = term[m] + plane(m)
        encode(total, message)

    by_core(forward, add)


def beside(picked, near, product):
    units, lines, _ = product.shape

    def put(m, value):
        product[m] = value

    plane = decode(near, units, lines)
    pl.when(lax.axis_index("band") == 0)(lambda: blurred(picked[1], units, plane, put))


def settle(picked, product, received, message, total):
    units, lines, _ = product.shape

    def put(m, value):
        total[m] = product[m] + value

    def add():
        blurred(picked[2], units, decode(received, units, lines), put)
        encode(total, message)

    def forward():
        message[...] = received[...]

    by_core(add, forward)

def arccos(x):
    size = jnp.abs(x)
    big = size > 0.5
    z = jnp.where(big, 0.5 * (1.0 - size), size * size)
    root = jnp.where(big, jnp.sqrt(z), size)
    poly = 4.2163199048e-2
    for term in (2.4181311049e-2, 4.5470025998e-2, 7.4953002686e-2, 1.6666752422e-1):
        poly = poly * z + term
    arcsin = poly * z * root + root
    pi = 3.14159265358979
    inner = jnp.where(x < 0, 0.5 * pi + arcsin, 0.5 * pi - arcsin)
    outer = jnp.where(x < 0, pi - 2.0 * arcsin, 2.0 * arcsin)
    return jnp.where(big, outer, inner)


def finish(second, observed, base, message, *rest):
    if second:
        sums, _, image, angles, angle, value, sems = rest
    else:
        image, sums, value, sems = rest
    units, lines, half = base.shape
    count = observed.shape[0]
    plane = decode(message, units, lines)

    def work(core):
        places = [(m, slice(c * half, (c + 1) * half)) for m, c in units_of(core, count)]
        copies = [
            pltpu.make_async_copy(value.at[n], image.at[m, :, at], sems.at[n])
            for n, (m, at) in enumerate(places)
        ]
        for n in range(units):
            value[n] = base[n] + plane(n)
            copies[n].start()
        for c in range(2):
            at = slice(c * half, (c + 1) * half)
            inner = jnp.zeros((lines, half), jnp.float32)
            left = jnp.zeros((lines, half), jnp.float32)
            for n, (m, where) in enumerate(places):
                if where == at:
                    inner = inner + value[n] * observed[m, :, at].astype(jnp.float32)
                    left = left + value[n] * value[n]
            if second:
                bound = jnp.sqrt(left + sums[1, :, at]) * sums[2, :, at]
                ratio = (inner + sums[0, :, at]) / jnp.maximum(bound, 1.0)
                angle[:, at] = arccos(jnp.clip(ratio, -1.0, 1.0))
            else:
                right = jnp.zeros((lines, half), jnp.float32)
                for m in range(count):
                    seen = observed[m, :, at].astype(jnp.float32)
                    right = right + seen * seen
                sums[0, :, at] = inner
                sums[1, :, at] = left
                sums[2, :, at] = jnp.sqrt(right)
        if second:
            copies.append(pltpu.make_async_copy(angle, angles, sems.at[units]))
            copies[-1].start()
        for copy in copies:
            copy.wait()

    if second:
        by_core(lambda: work(1), lambda: work(0))
    else:
        by_core(lambda: work(0), lambda: work(1))


def on_device(
    cube,
    observed,
    along_kernels,
    along_offsets,
    across_kernels,
    across_offsets,
    resp_start,
    resp_values,
):
    f32, i16 = jnp.float32, jnp.int16
    size = lax.axis_size("line")
    bands, lines, cols = cube.shape
    count = resp_values.shape[0]
    half = cols // 2
    _, _, units = ownership(count)
    shape = jax.ShapeDtypeStruct
    swap = [(0, 1), (1, 0)]
    partner = [(i, i ^ 1) for i in range(size)]
    even_up = [(i, i + 2) for i in range(0, size - 2, 2)] + [(i, i - 2) for i in range(3, size, 2)]
    odd_up = [(i, i + 2) for i in range(1, size - 2, 2)] + [(i, i - 2) for i in range(2, size, 2)]

    def cores(zero, one):
        return [(2 * a, 2 * b) for a, b in zero] + [(2 * a + 1, 2 * b + 1) for a, b in one]

    part = shape((units, lines, half), f32)
    coded = shape((coded_rows(units, lines), half), i16)
    unit = 4 * lines * lines * half

    inputs = (
        resp_start,
        across_offsets,
        resp_values,
        across_kernels,
        along_offsets,
        along_kernels,
        cube,
    )
    keep, send, picked = call(
        fold,
        [pltpu.with_memory_space_constraint(x, pltpu.HBM) for x in inputs],
        [HBM] * len(inputs),
        [part, part, shape(along_kernels.shape, along_kernels.dtype)],
        scratch=[
            pltpu.SMEM(resp_start.shape, jnp.int32),
            pltpu.SMEM(across_offsets.shape, jnp.int32),
            pltpu.VMEM(resp_values.shape, resp_values.dtype),
            pltpu.VMEM(resp_values.shape, f32),
            pltpu.SMEM(resp_values.shape, f32),
            pltpu.VMEM(across_kernels.shape, across_kernels.dtype),
            pltpu.SMEM(along_offsets.shape, jnp.int32),
            pltpu.VMEM(along_kernels.shape, along_kernels.dtype),
            pltpu.VMEM(cube.shape, cube.dtype),
            pltpu.VMEM((count, lines, cols), f32),
            pltpu.VMEM((2 * cols, cols), across_kernels.dtype),
            pltpu.SMEM((count,), jnp.int32),
            pltpu.SemaphoreType.DMA((len(inputs),)),
            pltpu.SemaphoreType.DMA((-(-bands // resp_values.shape[1]),)),
        ],
        flops=4 * count * lines * cols * cols,
    )
    work = [pltpu.VMEM(part.shape, f32)]
    other = lax.ppermute(send, "band", swap)
    total, message = call(share, (picked, keep, other), [VMEM] * 3, [part, coded], scratch=work)
    near = lax.ppermute(message, ("line", "band"), cores(partner, odd_up))
    other_total = lax.ppermute(total, "band", swap)
    base, other_base, term = call(
        centre, (picked, total, other_total), [VMEM] * 3, [part] * 3, flops=3 * unit * units
    )
    near, base, other_base, term = lax.optimization_barrier((near, base, other_base, term))
    (message,) = call(relay, (term, near), [VMEM] * 2, [coded], scratch=work)
    message, near = lax.optimization_barrier((message, near))
    far = lax.ppermute(message, ("line", "band"), cores(even_up, partner))
    (product,) = call(beside, (picked, near), [VMEM] * 2, [part], flops=unit * units)
    (message,) = call(
        settle, (picked, product, far), [VMEM] * 3, [coded], scratch=work, flops=unit * units
    )
    other_message = lax.ppermute(message, "band", swap)
    image = shape((count, lines, cols), f32)
    image, sums = call(
        functools.partial(finish, False),
        (observed, base, message),
        [VMEM] * 3,
        [image, shape((3, lines, cols), f32)],
        scratch=work + [pltpu.SemaphoreType.DMA((units,))],
        out_specs=[HBM, VMEM],
    )
    image, angles = call(
        functools.partial(finish, True),
        (observed, other_base, other_message, sums, image),
        [VMEM] * 4 + [HBM],
        [image, shape((lines, cols), f32)],
        scratch=[pltpu.VMEM((lines, cols), f32), *work, pltpu.SemaphoreType.DMA((units + 1,))],
        out_specs=[HBM] * 2,
        aliases={4: 0},
    )
    return image, angles


def solution(mesh):
    placed = (
        P("band", ("slab", "line"), None),
        P(None, ("slab", "line"), None),
        P(),
        P(),
        P(),
        P(),
        P(),
        P(),
    )
    return jax.shard_map(
        on_device,
        mesh=mesh,
        in_specs=placed,
        out_specs=(P(None, ("slab", "line"), None), P(("slab", "line"), None)),
        check_vma=False,
    )
```

```python
import functools
import math

import jax
import jax.numpy as jnp
from jax import lax
from jax.experimental import pallas as pl
from jax.experimental.pallas import tpu as pltpu
from jax.sharding import PartitionSpec as P

BLK = 128
SPB = 10
STEPS = 16.0
PEAK = 32000.0


def which(offsets, shift):
    return sum(
        jnp.where(offsets[k] == shift, jnp.int32(k), jnp.int32(0)) for k in range(offsets.shape[0])
    )


def split(value):
    high = value.astype(jnp.bfloat16)
    low = (value - high.astype(jnp.float32)).astype(jnp.bfloat16)
    return high, low


SMEM = pl.BlockSpec(memory_space=pltpu.SMEM)
VMEM = pl.BlockSpec(memory_space=pltpu.VMEM)
HBM = pl.BlockSpec(memory_space=pltpu.HBM)
ROWS = 64


def call(kernel, inputs, specs, outs, scratch=(), out_specs=None, aliases=None, flops=0):
    moved = sum(x.size * x.dtype.itemsize for x in (*inputs, *outs))
    return pl.pallas_call(
        kernel,
        in_specs=specs,
        out_specs=out_specs or [VMEM] * len(outs),
        out_shape=outs,
        scratch_shapes=scratch,
        input_output_aliases=aliases or {},
        compiler_params=pltpu.CompilerParams(vmem_limit_bytes=32 * 2**20),
        cost_estimate=pl.CostEstimate(flops=flops, bytes_accessed=moved, transcendentals=0),
        name=(kernel.func if isinstance(kernel, functools.partial) else kernel).__name__,
    )(*inputs)


def ownership(count):
    pairs = count // 2
    return pairs, count % 2, 2 * pairs + count % 2


def units_of(core, count):
    pairs, odd, _ = ownership(count)
    first = core * (pairs + odd)
    return [(first + i, c) for i in range(pairs) for c in range(2)] + [(pairs, core)] * odd


def fold(
    start_in,
    offsets_in,
    values_in,
    blocks_in,
    along_offsets_in,
    along_blocks_in,
    cube_in,
    keep,
    send,
    picked,
    start,
    offsets,
    values,
    wide,
    weights,
    blocks,
    along_offsets,
    along_blocks,
    cube,
    folded,
    table,
    order,
    small,
    large,
):
    bands, lines, cols = cube.shape
    count, window = values.shape
    half = cols // 2
    group = math.gcd(SPB, bands)
    me = lax.axis_index("band")
    pairs = (
        (start_in, start),
        (values_in, values),
        (offsets_in, offsets),
        (blocks_in, blocks),
        (along_offsets_in, along_offsets),
        (along_blocks_in, along_blocks),
    )
    copies = [pltpu.make_async_copy(a, b, small.at[i]) for i, (a, b) in enumerate(pairs)]

    chunks = -(-bands // window)
    last = bands - (chunks - 1) * window

    def arrive(q, size):
        at = pl.ds(q * window, size)
        return pltpu.make_async_copy(cube_in.at[at], cube.at[at], large.at[q])

    for copy in copies:
        copy.start()
    for q in range(chunks):
        arrive(q, window if q < chunks - 1 else last).start()
    copies[1].wait()
    wide[...] = values[...].astype(jnp.float32)
    spread = pltpu.make_async_copy(wide, weights, small.at[len(pairs)])
    spread.start()
    copies[0].wait()

    places = [SPB * start[m] - bands * me for m in range(count)]
    ranks = [jnp.int32(0)] * count
    for m in range(count):
        for n in range(m + 1, count):
            later = (places[n] < places[m]).astype(jnp.int32)
            ranks[m] = ranks[m] + later
            ranks[n] = ranks[n] + (1 - later)
    before = jnp.int32(0)
    until = jnp.int32(0)
    for m in range(count):
        order[ranks[m]] = jnp.int32(m)
        before = before + (places[m] <= -window).astype(jnp.int32)
        until = until + (places[m] < bands).astype(jnp.int32)

    def clear(n, carry):
        folded[order[n]] = jnp.zeros((lines, cols), jnp.float32)
        return carry

    lax.fori_loop(0, before, clear, 0)
    lax.fori_loop(until, count, clear, 0)
    for copy in copies[2:]:
        copy.wait()
    for r in range(2):
        for c in range(2):
            block = blocks[which(offsets, jnp.int32(r - c))].astype(jnp.float32).T
            for top in (0, cols):
                at = slice(top + r * half, top + (r + 1) * half)
                table[at, c * half : (c + 1) * half] = block.astype(jnp.bfloat16)
    step = side_step()
    for i, shift in enumerate((jnp.int32(0), step, -step)):
        picked[i] = along_blocks[which(along_offsets, shift)]
    spread.wait()

    def ready(q, carry):
        pl.when(q < chunks - 1)(lambda: arrive(q, window).wait())
        pl.when(q == chunks - 1)(lambda: arrive(chunks - 1, last).wait())
        return carry

    def one(n, arrived):
        m = order[n]
        low = SPB * start[m] - bands * me
        stop = jnp.minimum(low + window, bands)
        needed = lax.div(stop - 1, jnp.int32(window)) + 1
        lax.fori_loop(arrived, needed, ready, 0)
        whole = jnp.logical_and(low >= 0, low + window <= bands)

        def term(band, weight, r):
            return weight * cube[band, r : r + ROWS, :].astype(jnp.float32)

        @pl.when(whole)
        def _():
            for r in range(0, lines, ROWS):
                total = term(low, weights[m, 0], r)
                for j in range(1, window):
                    total = total + term(low + j, weights[m, j], r)
                folded[m, r : r + ROWS, :] = total

        @pl.when(jnp.logical_not(whole))
        def _():
            first = jnp.maximum(low, 0)
            for r in range(0, lines, ROWS):

                def some(t, total):
                    for i in range(group):
                        band = first + t * group + i
                        total = total + term(band, weights[m, band - low], r)
                    return total

                folded[m, r : r + ROWS, :] = lax.fori_loop(
                    0,
                    lax.div(stop - first, jnp.int32(group)),
                    some,
                    jnp.zeros((ROWS, cols), jnp.float32),
                )

        return jnp.maximum(arrived, needed)

    arrived = lax.fori_loop(before, until, one, jnp.int32(0))
    lax.fori_loop(arrived, chunks, ready, 0)

    side = table[...]
    planes, odd, units = ownership(count)

    def across(at, planes):
        value = folded[pl.ds(at, planes)].reshape(planes * lines, cols)
        both = jnp.concatenate(split(value), axis=1)
        made = jnp.dot(both, side, preferred_element_type=jnp.float32)
        return made.reshape(planes, lines, cols)

    for owner, out in ((me, keep), (1 - me, send)):
        made = across(owner * (planes + odd), planes)
        for i in range(planes):
            out[2 * i] = made[i, :, :half]
            out[2 * i + 1] = made[i, :, half:]
    if odd:
        made = across(planes, 1)[0]
        left, right = made[:, :half], made[:, half:]
        keep[units - 1] = jnp.where(me == 0, left, right)
        send[units - 1] = jnp.where(me == 0, right, left)


def coded_rows(count, lines):
    return count * lines + -(-count // 16) * 16


def encode(source, span, message):
    _, lines, half = source.shape
    units = span[1] - span[0]
    largest = jnp.max(jnp.abs(source[span[0] : span[1]]), axis=1)
    level = jnp.ceil(jnp.log2(jnp.maximum(largest, 1e-30)) * STEPS)
    factor = PEAK * jnp.exp2(level * (-1.0 / STEPS))
    for m in range(units):
        coded = jnp.floor(source[span[0] + m] * factor[m : m + 1, :] + 0.5).astype(jnp.int32)
        message[m * lines : (m + 1) * lines, :] = coded.astype(jnp.int16)
    spare = message.shape[0] - units * lines - units
    level = jnp.concatenate([level, jnp.zeros((spare, half), jnp.float32)], axis=0)
    message[units * lines :, :] = level.astype(jnp.int32).astype(jnp.int16)


def decode(message, span, lines):
    units = span[1] - span[0]
    level = message[units * lines :, :].astype(jnp.int32).astype(jnp.float32)
    scale = jnp.exp2(level * (1.0 / STEPS)) * (1.0 / PEAK)

    def plane(m):
        coded = message[m * lines : (m + 1) * lines, :].astype(jnp.int32).astype(jnp.float32)
        return coded * scale[m : m + 1, :]

    return plane


def blurred(filters, count, plane, put):
    wide = jnp.concatenate([filters, filters], axis=1)
    for m in range(0, count, 2):
        parts = [split(plane(n)) for n in range(m, min(m + 2, count))]
        high = jnp.concatenate([p[0] for p in parts], axis=1)
        low = jnp.concatenate([p[1] for p in parts], axis=1)
        made = jnp.dot(
            wide, jnp.concatenate([high, low], axis=0), preferred_element_type=jnp.float32
        )
        half = made.shape[1] // len(parts)
        for i in range(len(parts)):
            put(m + i, made[:, i * half : (i + 1) * half])


def side_step():
    return jnp.where(lax.axis_index("line") % 2 == 0, jnp.int32(1), jnp.int32(-1))


def by_core(zero, one):
    me = lax.axis_index("band")
    pl.when(me == 0)(zero)
    pl.when(me != 0)(one)


def share(spans, picked, keep, other, total, *rest):
    messages, product = rest[:-1], rest[-1]
    total[...] = keep[...] + other[...]

    def coding(source):
        for span, message in zip(spans, messages):
            encode(source, span, message)

    def summing():
        def put(m, value):
            product[m] = value

        blurred(picked[1], total.shape[0], lambda m: total[m], put)
        coding(product)

    by_core(lambda: coding(total), summing)


def centre(picked, total, other_total, base, other_base, term):
    units = total.shape[0]

    def into(out):
        def put(m, value):
            out[m] = value

        return put

    blurred(picked[0], units, lambda m: total[m], into(base))
    blurred(picked[0], units, lambda m: other_total[m], into(other_base))
    pl.when(lax.axis_index("band") != 0)(
        lambda: blurred(picked[2], units, lambda m: total[m], into(term))
    )


def relay(span, term, received, message, total):
    def forward():
        message[...] = received[...]

    def add():
        plane = decode(received, span, term.shape[1])
        for m in range(*span):
            total[m] = term[m] + plane(m - span[0])
        encode(total, span, message)

    by_core(forward, add)


def beside(span, picked, near, product):
    units, lines, _ = product.shape

    def put(m, value):
        product[m] = value

    plane = decode(near, span, lines)
    pl.when(lax.axis_index("band") == 0)(lambda: blurred(picked[1], units, plane, put))


def settle(span, picked, product, received, message, total):
    units, lines, _ = product.shape

    def put(m, value):
        total[m] = product[m] + value

    def add():
        blurred(picked[2], units, decode(received, span, lines), put)
        encode(total, (0, units), message)

    def forward():
        message[...] = received[...]

    by_core(add, forward)


def arccos(x):
    size = jnp.abs(x)
    big = size > 0.5
    z = jnp.where(big, 0.5 * (1.0 - size), size * size)
    root = jnp.where(big, jnp.sqrt(z), size)
    poly = 4.2163199048e-2
    for term in (2.4181311049e-2, 4.5470025998e-2, 7.4953002686e-2, 1.6666752422e-1):
        poly = poly * z + term
    arcsin = poly * z * root + root
    pi = 3.14159265358979
    inner = jnp.where(x < 0, 0.5 * pi + arcsin, 0.5 * pi - arcsin)
    outer = jnp.where(x < 0, pi - 2.0 * arcsin, 2.0 * arcsin)
    return jnp.where(big, outer, inner)


def finish(flip, span, given, observed, base, message, *rest):
    begun, rest = rest[:given], rest[given:]
    if flip or span[0] > 0:
        rest = rest[1:]
    image, out, value, *rest, sems = rest
    units = span[1] - span[0]
    _, lines, half = base.shape
    count = observed.shape[0]
    plane = decode(message, span, lines)

    def work(core):
        places = [
            (m, slice(c * half, (c + 1) * half)) for m, c in units_of(core, count)[slice(*span)]
        ]
        copies = [
            pltpu.make_async_copy(value.at[n], image.at[m, :, at], sems.at[n])
            for n, (m, at) in enumerate(places)
        ]
        for n in range(units):
            value[n] = base[span[0] + n] + plane(n)
            copies[n].start()
        for c in range(2):
            at = slice(c * half, (c + 1) * half)
            inner = jnp.zeros((lines, half), jnp.float32)
            left = jnp.zeros((lines, half), jnp.float32)
            for n, (m, where) in enumerate(places):
                if where == at:
                    inner = inner + value[n] * observed[m, :, at].astype(jnp.float32)
                    left = left + value[n] * value[n]
            if given:
                inner = inner + begun[0][0, :, at]
                left = left + begun[0][1, :, at]
            if given == 2:
                bound = jnp.sqrt(left + begun[1][1, :, at]) * begun[1][2, :, at]
                ratio = (inner + begun[1][0, :, at]) / jnp.maximum(bound, 1.0)
                rest[0][:, at] = arccos(jnp.clip(ratio, -1.0, 1.0))
                continue
            out[0, :, at] = inner
            out[1, :, at] = left
            if given:
                out[2, :, at] = begun[0][2, :, at]
            elif not flip:
                right = jnp.zeros((lines, half), jnp.float32)
                for m in range(count):
                    seen = observed[m, :, at].astype(jnp.float32)
                    right = right + seen * seen
                out[2, :, at] = jnp.sqrt(right)
        if given == 2:
            copies.append(pltpu.make_async_copy(rest[0], out, sems.at[units]))
            copies[-1].start()
        for copy in copies:
            copy.wait()

    by_core(lambda: work(1 if flip else 0), lambda: work(0 if flip else 1))


def on_device(
    cube,
    observed,
    along_kernels,
    along_offsets,
    across_kernels,
    across_offsets,
    resp_start,
    resp_values,
):
    f32, i16 = jnp.float32, jnp.int16
    size = lax.axis_size("line")
    bands, lines, cols = cube.shape
    count = resp_values.shape[0]
    half = cols // 2
    _, _, units = ownership(count)
    shape = jax.ShapeDtypeStruct
    swap = [(0, 1), (1, 0)]
    partner = [(i, i ^ 1) for i in range(size)]
    even_up = [(i, i + 2) for i in range(0, size - 2, 2)] + [(i, i - 2) for i in range(3, size, 2)]
    odd_up = [(i, i + 2) for i in range(1, size - 2, 2)] + [(i, i - 2) for i in range(2, size, 2)]

    def cores(zero, one):
        return [(2 * a, 2 * b) for a, b in zero] + [(2 * a + 1, 2 * b + 1) for a, b in one]

    part = shape((units, lines, half), f32)
    spans = [(0, (units + 1) // 2), ((units + 1) // 2, units)]
    coded = [shape((coded_rows(b - a, lines), half), i16) for a, b in spans]
    unit = 4 * lines * lines * half

    inputs = (
        resp_start,
        across_offsets,
        resp_values,
        across_kernels,
        along_offsets,
        along_kernels,
        cube,
    )
    keep, send, picked = call(
        fold,
        [pltpu.with_memory_space_constraint(x, pltpu.HBM) for x in inputs],
        [HBM] * len(inputs),
        [part, part, shape(along_kernels.shape, along_kernels.dtype)],
        scratch=[
            pltpu.SMEM(resp_start.shape, jnp.int32),
            pltpu.SMEM(across_offsets.shape, jnp.int32),
            pltpu.VMEM(resp_values.shape, resp_values.dtype),
            pltpu.VMEM(resp_values.shape, f32),
            pltpu.SMEM(resp_values.shape, f32),
            pltpu.VMEM(across_kernels.shape, across_kernels.dtype),
            pltpu.SMEM(along_offsets.shape, jnp.int32),
            pltpu.VMEM(along_kernels.shape, along_kernels.dtype),
            pltpu.VMEM(cube.shape, cube.dtype),
            pltpu.VMEM((count, lines, cols), f32),
            pltpu.VMEM((2 * cols, cols), across_kernels.dtype),
            pltpu.SMEM((count,), jnp.int32),
            pltpu.SemaphoreType.DMA((len(inputs),)),
            pltpu.SemaphoreType.DMA((-(-bands // resp_values.shape[1]),)),
        ],
        flops=4 * count * lines * cols * cols,
    )
    work = [pltpu.VMEM(part.shape, f32)]
    other = lax.ppermute(send, "band", swap)
    total, *sent = call(
        functools.partial(share, spans),
        (picked, keep, other),
        [VMEM] * 3,
        [part, *coded],
        scratch=work,
        flops=unit * units,
    )
    near = [lax.ppermute(x, ("line", "band"), cores(partner, odd_up)) for x in sent]
    other_total = lax.ppermute(total, "band", swap)
    base, other_base, term = call(
        centre, (picked, total, other_total), [VMEM] * 3, [part] * 3, flops=3 * unit * units
    )
    far, product = [], []
    for i, span in enumerate(spans):
        (message,) = call(
            functools.partial(relay, span), (term, near[i]), [VMEM] * 2, [coded[i]], scratch=work
        )
        message, near[i] = lax.optimization_barrier((message, near[i]))
        far.append(lax.ppermute(message, ("line", "band"), cores(even_up, partner)))
        planes = shape((span[1] - span[0], lines, half), f32)
        product += call(
            functools.partial(beside, span),
            (picked, near[i]),
            [VMEM] * 2,
            [planes],
            flops=unit * planes.shape[0],
        )
    image = shape((count, lines, cols), f32)
    three = shape((3, lines, cols), f32)
    made = None
    sums = [[], []]
    for i, span in enumerate(spans):
        planes = product[i].shape
        if i:
            far[i], made, sums = lax.optimization_barrier((far[i], made, sums))
        (message,) = call(
            functools.partial(settle, span),
            (picked, product[i], far[i]),
            [VMEM] * 3,
            [coded[i]],
            scratch=[pltpu.VMEM(planes, f32)],
            flops=unit * planes[0],
        )
        other_message = lax.ppermute(message, "band", swap)
        for flip, (start, coming) in enumerate(((base, message), (other_base, other_message))):
            given = sums[flip] + (sums[0] if flip and i else [])
            last = len(given) == 2
            inputs = [observed, start, coming, *given]
            scratch = [pltpu.VMEM(planes, f32)] + [pltpu.VMEM((lines, cols), f32)] * last
            made, out = call(
                functools.partial(finish, flip, span, len(given)),
                inputs + ([] if made is None else [made]),
                [VMEM] * len(inputs) + ([] if made is None else [HBM]),
                [image, shape((lines, cols), f32) if last else three],
                scratch=scratch + [pltpu.SemaphoreType.DMA((planes[0] + 1,))],
                out_specs=[HBM, HBM if last else VMEM],
                aliases={} if made is None else {len(inputs): 0},
            )
            sums[flip] = [out]
    return made, out


def solution(mesh):
    placed = (
        P("band", ("slab", "line"), None),
        P(None, ("slab", "line"), None),
        P(),
        P(),
        P(),
        P(),
        P(),
        P(),
    )
    return jax.shard_map(
        on_device,
        mesh=mesh,
        in_specs=placed,
        out_specs=(P(None, ("slab", "line"), None), P(("slab", "line"), None)),
        check_vma=False,
    )
```

```python
import functools
import math

import jax
import jax.numpy as jnp
from jax import lax
from jax.experimental import pallas as pl
from jax.experimental.pallas import tpu as pltpu
from jax.sharding import PartitionSpec as P

BLK = 128
SPB = 10
STEPS = 16.0
PEAK = 32000.0


def which(offsets, shift):
    return sum(
        jnp.where(offsets[k] == shift, jnp.int32(k), jnp.int32(0)) for k in range(offsets.shape[0])
    )


def split(value):
    high = value.astype(jnp.bfloat16)
    low = (value - high.astype(jnp.float32)).astype(jnp.bfloat16)
    return high, low


SMEM = pl.BlockSpec(memory_space=pltpu.SMEM)
VMEM = pl.BlockSpec(memory_space=pltpu.VMEM)
HBM = pl.BlockSpec(memory_space=pltpu.HBM)
ROWS = 64


def call(kernel, inputs, specs, outs, scratch=(), out_specs=None, aliases=None, flops=0):
    moved = sum(x.size * x.dtype.itemsize for x in (*inputs, *outs))
    return pl.pallas_call(
        kernel,
        in_specs=specs,
        out_specs=out_specs or [VMEM] * len(outs),
        out_shape=outs,
        scratch_shapes=scratch,
        input_output_aliases=aliases or {},
        compiler_params=pltpu.CompilerParams(vmem_limit_bytes=32 * 2**20),
        cost_estimate=pl.CostEstimate(flops=flops, bytes_accessed=moved, transcendentals=0),
        name=(kernel.func if isinstance(kernel, functools.partial) else kernel).__name__,
    )(*inputs)


def ownership(count):
    pairs = count // 2
    return pairs, count % 2, 2 * pairs + count % 2


def units_of(core, count):
    pairs, odd, _ = ownership(count)
    first = core * (pairs + odd)
    return [(first + i, c) for i in range(pairs) for c in range(2)] + [(pairs, core)] * odd


def fold(
    start_in,
    offsets_in,
    values_in,
    blocks_in,
    along_offsets_in,
    along_blocks_in,
    cube_in,
    keep,
    send,
    picked,
    start,
    offsets,
    values,
    wide,
    weights,
    blocks,
    along_offsets,
    along_blocks,
    cube,
    folded,
    table,
    order,
    small,
    large,
):
    bands, lines, cols = cube.shape
    count, window = values.shape
    half = cols // 2
    group = math.gcd(SPB, bands)
    me = lax.axis_index("band")
    pairs = (
        (start_in, start),
        (values_in, values),
        (offsets_in, offsets),
        (blocks_in, blocks),
        (along_offsets_in, along_offsets),
        (along_blocks_in, along_blocks),
    )
    copies = [pltpu.make_async_copy(a, b, small.at[i]) for i, (a, b) in enumerate(pairs)]

    chunks = -(-bands // window)
    last = bands - (chunks - 1) * window

    def arrive(q, size):
        at = pl.ds(q * window, size)
        return pltpu.make_async_copy(cube_in.at[at], cube.at[at], large.at[q])

    for copy in copies:
        copy.start()
    for q in range(chunks):
        arrive(q, window if q < chunks - 1 else last).start()
    copies[1].wait()
    wide[...] = values[...].astype(jnp.float32)
    spread = pltpu.make_async_copy(wide, weights, small.at[len(pairs)])
    spread.start()
    copies[0].wait()

    places = [SPB * start[m] - bands * me for m in range(count)]
    ranks = [jnp.int32(0)] * count
    for m in range(count):
        for n in range(m + 1, count):
            later = (places[n] < places[m]).astype(jnp.int32)
            ranks[m] = ranks[m] + later
            ranks[n] = ranks[n] + (1 - later)
    before = jnp.int32(0)
    until = jnp.int32(0)
    for m in range(count):
        order[ranks[m]] = jnp.int32(m)
        before = before + (places[m] <= -window).astype(jnp.int32)
        until = until + (places[m] < bands).astype(jnp.int32)

    def clear(n, carry):
        folded[order[n]] = jnp.zeros((lines, cols), jnp.float32)
        return carry

    lax.fori_loop(0, before, clear, 0)
    lax.fori_loop(until, count, clear, 0)
    for copy in copies[2:]:
        copy.wait()
    for r in range(2):
        for c in range(2):
            block = blocks[which(offsets, jnp.int32(r - c))].astype(jnp.float32).T
            for top in (0, cols):
                at = slice(top + r * half, top + (r + 1) * half)
                table[at, c * half : (c + 1) * half] = block.astype(jnp.bfloat16)
    step = side_step()
    for i, shift in enumerate((jnp.int32(0), step, -step)):
        picked[i] = along_blocks[which(along_offsets, shift)]
    spread.wait()

    def ready(q, carry):
        pl.when(q < chunks - 1)(lambda: arrive(q, window).wait())
        pl.when(q == chunks - 1)(lambda: arrive(chunks - 1, last).wait())
        return carry

    def one(n, arrived):
        m = order[n]
        low = SPB * start[m] - bands * me
        stop = jnp.minimum(low + window, bands)
        needed = lax.div(stop - 1, jnp.int32(window)) + 1
        lax.fori_loop(arrived, needed, ready, 0)
        whole = jnp.logical_and(low >= 0, low + window <= bands)

        def term(band, weight, r):
            return weight * cube[band, r : r + ROWS, :].astype(jnp.float32)

        @pl.when(whole)
        def _():
            for r in range(0, lines, ROWS):
                total = term(low, weights[m, 0], r)
                for j in range(1, window):
                    total = total + term(low + j, weights[m, j], r)
                folded[m, r : r + ROWS, :] = total

        @pl.when(jnp.logical_not(whole))
        def _():
            first = jnp.maximum(low, 0)
            for r in range(0, lines, ROWS):

                def some(t, total):
                    for i in range(group):
                        band = first + t * group + i
                        total = total + term(band, weights[m, band - low], r)
                    return total

                folded[m, r : r + ROWS, :] = lax.fori_loop(
                    0,
                    lax.div(stop - first, jnp.int32(group)),
                    some,
                    jnp.zeros((ROWS, cols), jnp.float32),
                )

        return jnp.maximum(arrived, needed)

    arrived = lax.fori_loop(before, until, one, jnp.int32(0))
    lax.fori_loop(arrived, chunks, ready, 0)

    side = table[...]
    planes, odd, units = ownership(count)

    def across(at, planes):
        value = folded[pl.ds(at, planes)].reshape(planes * lines, cols)
        both = jnp.concatenate(split(value), axis=1)
        made = jnp.dot(both, side, preferred_element_type=jnp.float32)
        return made.reshape(planes, lines, cols)

    for owner, out in ((me, keep), (1 - me, send)):
        made = across(owner * (planes + odd), planes)
        for i in range(planes):
            out[2 * i] = made[i, :, :half]
            out[2 * i + 1] = made[i, :, half:]
    if odd:
        made = across(planes, 1)[0]
        left, right = made[:, :half], made[:, half:]
        keep[units - 1] = jnp.where(me == 0, left, right)
        send[units - 1] = jnp.where(me == 0, right, left)


def coded_rows(count, lines):
    return count * lines + -(-count // 16) * 16


def encode(source, message):
    units, lines, half = source.shape
    largest = jnp.max(jnp.abs(source[...]), axis=1)
    level = jnp.ceil(jnp.log2(jnp.maximum(largest, 1e-30)) * STEPS)
    factor = PEAK * jnp.exp2(level * (-1.0 / STEPS))
    for m in range(units):
        coded = jnp.floor(source[m] * factor[m : m + 1, :] + 0.5).astype(jnp.int32)
        message[m * lines : (m + 1) * lines, :] = coded.astype(jnp.int16)
    spare = message.shape[0] - units * lines - units
    level = jnp.concatenate([level, jnp.zeros((spare, half), jnp.float32)], axis=0)
    message[units * lines :, :] = level.astype(jnp.int32).astype(jnp.int16)


def decode(message, count, lines):
    level = message[count * lines :, :].astype(jnp.int32).astype(jnp.float32)
    scale = jnp.exp2(level * (1.0 / STEPS)) * (1.0 / PEAK)

    def plane(m):
        coded = message[m * lines : (m + 1) * lines, :].astype(jnp.int32).astype(jnp.float32)
        return coded * scale[m : m + 1, :]

    return plane


def blurred(filters, count, plane, put):
    wide = jnp.concatenate([filters, filters], axis=1)
    for m in range(0, count, 2):
        parts = [split(plane(n)) for n in range(m, min(m + 2, count))]
        high = jnp.concatenate([p[0] for p in parts], axis=1)
        low = jnp.concatenate([p[1] for p in parts], axis=1)
        made = jnp.dot(
            wide, jnp.concatenate([high, low], axis=0), preferred_element_type=jnp.float32
        )
        half = made.shape[1] // len(parts)
        for i in range(len(parts)):
            put(m + i, made[:, i * half : (i + 1) * half])


def side_step():
    return jnp.where(lax.axis_index("line") % 2 == 0, jnp.int32(1), jnp.int32(-1))


def by_core(zero, one):
    me = lax.axis_index("band")
    pl.when(me == 0)(zero)
    pl.when(me != 0)(one)


def share(picked, keep, other, total, message, product):
    total[...] = keep[...] + other[...]

    def summing():
        def put(m, value):
            product[m] = value

        blurred(picked[1], total.shape[0], lambda m: total[m], put)
        encode(product, message)

    by_core(lambda: encode(total, message), summing)


def centre(picked, total, other_total, base, other_base, term):
    units = total.shape[0]

    def into(out):
        def put(m, value):
            out[m] = value

        return put

    blurred(picked[0], units, lambda m: total[m], into(base))
    blurred(picked[0], units, lambda m: other_total[m], into(other_base))
    pl.when(lax.axis_index("band") != 0)(
        lambda: blurred(picked[2], units, lambda m: total[m], into(term))
    )


def relay(term, received, message, total):
    units, lines, _ = term.shape

    def add():
        plane = decode(received, units, lines)
        for m in range(units):
            total[m] = term[m] + plane(m)
        encode(total, message)

    pl.when(lax.axis_index("band") != 0)(add)


def beside(picked, near, product):
    units, lines, _ = product.shape

    def put(m, value):
        product[m] = value

    plane = decode(near, units, lines)
    pl.when(lax.axis_index("band") == 0)(lambda: blurred(picked[1], units, plane, put))


def settle(picked, product, received, summed, message, total):
    units, lines, _ = product.shape

    def put(m, value):
        total[m] = product[m] + value

    def add():
        blurred(picked[2], units, decode(received, units, lines), put)
        encode(total, message)

    def forward():
        message[...] = summed[...]

    by_core(add, forward)

def arccos(x):
    size = jnp.abs(x)
    big = size > 0.5
    z = jnp.where(big, 0.5 * (1.0 - size), size * size)
    root = jnp.where(big, jnp.sqrt(z), size)
    poly = 4.2163199048e-2
    for term in (2.4181311049e-2, 4.5470025998e-2, 7.4953002686e-2, 1.6666752422e-1):
        poly = poly * z + term
    arcsin = poly * z * root + root
    pi = 3.14159265358979
    inner = jnp.where(x < 0, 0.5 * pi + arcsin, 0.5 * pi - arcsin)
    outer = jnp.where(x < 0, pi - 2.0 * arcsin, 2.0 * arcsin)
    return jnp.where(big, outer, inner)


def finish(second, observed, base, message, *rest):
    if second:
        sums, _, image, angles, angle, value, sems = rest
    else:
        image, sums, value, sems = rest
    units, lines, half = base.shape
    count = observed.shape[0]
    plane = decode(message, units, lines)

    def work(core):
        places = [(m, slice(c * half, (c + 1) * half)) for m, c in units_of(core, count)]
        copies = [
            pltpu.make_async_copy(value.at[n], image.at[m, :, at], sems.at[n])
            for n, (m, at) in enumerate(places)
        ]
        for n in range(units):
            value[n] = base[n] + plane(n)
            copies[n].start()
        for c in range(2):
            at = slice(c * half, (c + 1) * half)
            inner = jnp.zeros((lines, half), jnp.float32)
            left = jnp.zeros((lines, half), jnp.float32)
            for n, (m, where) in enumerate(places):
                if where == at:
                    inner = inner + value[n] * observed[m, :, at].astype(jnp.float32)
                    left = left + value[n] * value[n]
            if second:
                bound = jnp.sqrt(left + sums[1, :, at]) * sums[2, :, at]
                ratio = (inner + sums[0, :, at]) / jnp.maximum(bound, 1.0)
                angle[:, at] = arccos(jnp.clip(ratio, -1.0, 1.0))
            else:
                right = jnp.zeros((lines, half), jnp.float32)
                for m in range(count):
                    seen = observed[m, :, at].astype(jnp.float32)
                    right = right + seen * seen
                sums[0, :, at] = inner
                sums[1, :, at] = left
                sums[2, :, at] = jnp.sqrt(right)
        if second:
            copies.append(pltpu.make_async_copy(angle, angles, sems.at[units]))
            copies[-1].start()
        for copy in copies:
            copy.wait()

    if second:
        by_core(lambda: work(1), lambda: work(0))
    else:
        by_core(lambda: work(0), lambda: work(1))


def on_device(
    cube,
    observed,
    along_kernels,
    along_offsets,
    across_kernels,
    across_offsets,
    resp_start,
    resp_values,
):
    f32, i16 = jnp.float32, jnp.int16
    size = lax.axis_size("line")
    bands, lines, cols = cube.shape
    count = resp_values.shape[0]
    half = cols // 2
    _, _, units = ownership(count)
    shape = jax.ShapeDtypeStruct
    swap = [(0, 1), (1, 0)]
    partner = [(i, i ^ 1) for i in range(size)]
    even_up = [(i, i + 2) for i in range(0, size - 2, 2)] + [(i, i - 2) for i in range(3, size, 2)]
    odd_up = [(i, i + 2) for i in range(1, size - 2, 2)] + [(i, i - 2) for i in range(2, size, 2)]

    def cores(zero, one):
        return [(2 * a, 2 * b) for a, b in zero] + [(2 * a + 1, 2 * b + 1) for a, b in one]

    part = shape((units, lines, half), f32)
    coded = shape((coded_rows(units, lines), half), i16)
    unit = 4 * lines * lines * half

    inputs = (
        resp_start,
        across_offsets,
        resp_values,
        across_kernels,
        along_offsets,
        along_kernels,
        cube,
    )
    keep, send, picked = call(
        fold,
        [pltpu.with_memory_space_constraint(x, pltpu.HBM) for x in inputs],
        [HBM] * len(inputs),
        [part, part, shape(along_kernels.shape, along_kernels.dtype)],
        scratch=[
            pltpu.SMEM(resp_start.shape, jnp.int32),
            pltpu.SMEM(across_offsets.shape, jnp.int32),
            pltpu.VMEM(resp_values.shape, resp_values.dtype),
            pltpu.VMEM(resp_values.shape, f32),
            pltpu.SMEM(resp_values.shape, f32),
            pltpu.VMEM(across_kernels.shape, across_kernels.dtype),
            pltpu.SMEM(along_offsets.shape, jnp.int32),
            pltpu.VMEM(along_kernels.shape, along_kernels.dtype),
            pltpu.VMEM(cube.shape, cube.dtype),
            pltpu.VMEM((count, lines, cols), f32),
            pltpu.VMEM((2 * cols, cols), across_kernels.dtype),
            pltpu.SMEM((count,), jnp.int32),
            pltpu.SemaphoreType.DMA((len(inputs),)),
            pltpu.SemaphoreType.DMA((-(-bands // resp_values.shape[1]),)),
        ],
        flops=4 * count * lines * cols * cols,
    )
    work = [pltpu.VMEM(part.shape, f32)]
    other = lax.ppermute(send, "band", swap)
    total, message = call(share, (picked, keep, other), [VMEM] * 3, [part, coded], scratch=work)
    near = lax.ppermute(message, ("line", "band"), cores(partner, []))
    received = lax.ppermute(message, ("line", "band"), cores([], odd_up))
    other_total = lax.ppermute(total, "band", swap)
    base, other_base, term = call(
        centre, (picked, total, other_total), [VMEM] * 3, [part] * 3, flops=3 * unit * units
    )
    near, received, base, other_base, term = lax.optimization_barrier(
        (near, received, base, other_base, term)
    )
    (message,) = call(relay, (term, received), [VMEM] * 2, [coded], scratch=work)
    message, near = lax.optimization_barrier((message, near))
    far = lax.ppermute(near, ("line", "band"), cores(even_up, []))
    sums = lax.ppermute(message, ("line", "band"), cores([], partner))
    (product,) = call(beside, (picked, near), [VMEM] * 2, [part], flops=unit * units)
    (message,) = call(
        settle,
        (picked, product, far, sums),
        [VMEM] * 4,
        [coded],
        scratch=work,
        flops=unit * units,
    )
    other_message = lax.ppermute(message, "band", swap)
    image = shape((count, lines, cols), f32)
    image, sums = call(
        functools.partial(finish, False),
        (observed, base, message),
        [VMEM] * 3,
        [image, shape((3, lines, cols), f32)],
        scratch=work + [pltpu.SemaphoreType.DMA((units,))],
        out_specs=[HBM, VMEM],
    )
    image, angles = call(
        functools.partial(finish, True),
        (observed, other_base, other_message, sums, image),
        [VMEM] * 4 + [HBM],
        [image, shape((lines, cols), f32)],
        scratch=[pltpu.VMEM((lines, cols), f32), *work, pltpu.SemaphoreType.DMA((units + 1,))],
        out_specs=[HBM] * 2,
        aliases={4: 0},
    )
    return image, angles


def solution(mesh):
    placed = (
        P("band", ("slab", "line"), None),
        P(None, ("slab", "line"), None),
        P(),
        P(),
        P(),
        P(),
        P(),
        P(),
    )
    return jax.shard_map(
        on_device,
        mesh=mesh,
        in_specs=placed,
        out_specs=(P(None, ("slab", "line"), None), P(("slab", "line"), None)),
        check_vma=False,
    )
```

```python
import functools
import math

import jax
import jax.numpy as jnp
from jax import lax
from jax.experimental import pallas as pl
from jax.experimental.pallas import tpu as pltpu
from jax.sharding import PartitionSpec as P

BLK = 128
SPB = 10
STEPS = 16.0
PEAK = 32000.0


def which(offsets, shift):
    return sum(
        jnp.where(offsets[k] == shift, jnp.int32(k), jnp.int32(0)) for k in range(offsets.shape[0])
    )


def split(value):
    high = value.astype(jnp.bfloat16)
    low = (value - high.astype(jnp.float32)).astype(jnp.bfloat16)
    return high, low


SMEM = pl.BlockSpec(memory_space=pltpu.SMEM)
VMEM = pl.BlockSpec(memory_space=pltpu.VMEM)
HBM = pl.BlockSpec(memory_space=pltpu.HBM)
ROWS = 64


def call(kernel, inputs, specs, outs, scratch=(), out_specs=None, aliases=None, flops=0):
    moved = sum(x.size * x.dtype.itemsize for x in (*inputs, *outs))
    return pl.pallas_call(
        kernel,
        in_specs=specs,
        out_specs=out_specs or [VMEM] * len(outs),
        out_shape=outs,
        scratch_shapes=scratch,
        input_output_aliases=aliases or {},
        compiler_params=pltpu.CompilerParams(vmem_limit_bytes=32 * 2**20),
        cost_estimate=pl.CostEstimate(flops=flops, bytes_accessed=moved, transcendentals=0),
        name=(kernel.func if isinstance(kernel, functools.partial) else kernel).__name__,
    )(*inputs)


def ownership(count):
    pairs = count // 2
    return pairs, count % 2, 2 * pairs + count % 2


def units_of(core, count):
    pairs, odd, _ = ownership(count)
    first = core * (pairs + odd)
    return [(first + i, c) for i in range(pairs) for c in range(2)] + [(pairs, core)] * odd


def fold(
    start_in,
    offsets_in,
    values_in,
    blocks_in,
    along_offsets_in,
    along_blocks_in,
    cube_in,
    keep,
    send,
    picked,
    start,
    offsets,
    values,
    wide,
    weights,
    blocks,
    along_offsets,
    along_blocks,
    cube,
    folded,
    table,
    order,
    small,
    large,
):
    bands, lines, cols = cube.shape
    count, window = values.shape
    half = cols // 2
    group = math.gcd(SPB, bands)
    me = lax.axis_index("band")
    pairs = (
        (start_in, start),
        (values_in, values),
        (offsets_in, offsets),
        (blocks_in, blocks),
        (along_offsets_in, along_offsets),
        (along_blocks_in, along_blocks),
    )
    copies = [pltpu.make_async_copy(a, b, small.at[i]) for i, (a, b) in enumerate(pairs)]

    chunks = -(-bands // window)
    last = bands - (chunks - 1) * window

    def arrive(q, size):
        at = pl.ds(q * window, size)
        return pltpu.make_async_copy(cube_in.at[at], cube.at[at], large.at[q])

    for copy in copies:
        copy.start()
    for q in range(chunks):
        arrive(q, window if q < chunks - 1 else last).start()
    copies[1].wait()
    wide[...] = values[...].astype(jnp.float32)
    spread = pltpu.make_async_copy(wide, weights, small.at[len(pairs)])
    spread.start()
    copies[0].wait()

    places = [SPB * start[m] - bands * me for m in range(count)]
    ranks = [jnp.int32(0)] * count
    for m in range(count):
        for n in range(m + 1, count):
            later = (places[n] < places[m]).astype(jnp.int32)
            ranks[m] = ranks[m] + later
            ranks[n] = ranks[n] + (1 - later)
    before = jnp.int32(0)
    until = jnp.int32(0)
    for m in range(count):
        order[ranks[m]] = jnp.int32(m)
        before = before + (places[m] <= -window).astype(jnp.int32)
        until = until + (places[m] < bands).astype(jnp.int32)

    def clear(n, carry):
        folded[order[n]] = jnp.zeros((lines, cols), jnp.float32)
        return carry

    lax.fori_loop(0, before, clear, 0)
    lax.fori_loop(until, count, clear, 0)
    for copy in copies[2:]:
        copy.wait()
    for r in range(2):
        for c in range(2):
            block = blocks[which(offsets, jnp.int32(r - c))].astype(jnp.float32).T
            for top in (0, cols):
                at = slice(top + r * half, top + (r + 1) * half)
                table[at, c * half : (c + 1) * half] = block.astype(jnp.bfloat16)
    step = side_step()
    for i, shift in enumerate((jnp.int32(0), step, -step)):
        picked[i] = along_blocks[which(along_offsets, shift)]
    spread.wait()

    def ready(q, carry):
        pl.when(q < chunks - 1)(lambda: arrive(q, window).wait())
        pl.when(q == chunks - 1)(lambda: arrive(chunks - 1, last).wait())
        return carry

    def one(n, arrived):
        m = order[n]
        low = SPB * start[m] - bands * me
        stop = jnp.minimum(low + window, bands)
        needed = lax.div(stop - 1, jnp.int32(window)) + 1
        lax.fori_loop(arrived, needed, ready, 0)
        whole = jnp.logical_and(low >= 0, low + window <= bands)

        def term(band, weight, r):
            return weight * cube[band, r : r + ROWS, :].astype(jnp.float32)

        @pl.when(whole)
        def _():
            for r in range(0, lines, ROWS):
                total = term(low, weights[m, 0], r)
                for j in range(1, window):
                    total = total + term(low + j, weights[m, j], r)
                folded[m, r : r + ROWS, :] = total

        @pl.when(jnp.logical_not(whole))
        def _():
            first = jnp.maximum(low, 0)
            for r in range(0, lines, ROWS):

                def some(t, total):
                    for i in range(group):
                        band = first + t * group + i
                        total = total + term(band, weights[m, band - low], r)
                    return total

                folded[m, r : r + ROWS, :] = lax.fori_loop(
                    0,
                    lax.div(stop - first, jnp.int32(group)),
                    some,
                    jnp.zeros((ROWS, cols), jnp.float32),
                )

        return jnp.maximum(arrived, needed)

    arrived = lax.fori_loop(before, until, one, jnp.int32(0))
    lax.fori_loop(arrived, chunks, ready, 0)

    side = table[...]
    planes, odd, units = ownership(count)

    def across(at, planes):
        value = folded[pl.ds(at, planes)].reshape(planes * lines, cols)
        both = jnp.concatenate(split(value), axis=1)
        made = jnp.dot(both, side, preferred_element_type=jnp.float32)
        return made.reshape(planes, lines, cols)

    for owner, out in ((me, keep), (1 - me, send)):
        made = across(owner * (planes + odd), planes)
        for i in range(planes):
            out[2 * i] = made[i, :, :half]
            out[2 * i + 1] = made[i, :, half:]
    if odd:
        made = across(planes, 1)[0]
        left, right = made[:, :half], made[:, half:]
        keep[units - 1] = jnp.where(me == 0, left, right)
        send[units - 1] = jnp.where(me == 0, right, left)


def coded_rows(count, lines):
    return count * lines + -(-count // 16) * 16


def encode(source, message):
    units, lines, half = source.shape
    largest = jnp.max(jnp.abs(source[...]), axis=1)
    level = jnp.ceil(jnp.log2(jnp.maximum(largest, 1e-30)) * STEPS)
    factor = PEAK * jnp.exp2(level * (-1.0 / STEPS))
    for m in range(units):
        coded = jnp.floor(source[m] * factor[m : m + 1, :] + 0.5).astype(jnp.int32)
        message[m * lines : (m + 1) * lines, :] = coded.astype(jnp.int16)
    spare = message.shape[0] - units * lines - units
    level = jnp.concatenate([level, jnp.zeros((spare, half), jnp.float32)], axis=0)
    message[units * lines :, :] = level.astype(jnp.int32).astype(jnp.int16)


def decode(message, count, lines, valid=True):
    level = message[count * lines :, :].astype(jnp.int32).astype(jnp.float32)
    scale = jnp.where(valid, jnp.exp2(level * (1.0 / STEPS)) * (1.0 / PEAK), 0.0)

    def plane(m):
        coded = message[m * lines : (m + 1) * lines, :].astype(jnp.int32).astype(jnp.float32)
        return coded * scale[m : m + 1, :]

    return plane


def blurred(filters, count, plane, put):
    wide = jnp.concatenate([filters, filters], axis=1)
    for m in range(0, count, 2):
        parts = [split(plane(n)) for n in range(m, min(m + 2, count))]
        high = jnp.concatenate([p[0] for p in parts], axis=1)
        low = jnp.concatenate([p[1] for p in parts], axis=1)
        made = jnp.dot(
            wide, jnp.concatenate([high, low], axis=0), preferred_element_type=jnp.float32
        )
        half = made.shape[1] // len(parts)
        for i in range(len(parts)):
            put(m + i, made[:, i * half : (i + 1) * half])


def side_step():
    return jnp.where(lax.axis_index("line") % 2 == 0, jnp.int32(1), jnp.int32(-1))


def outside(*lines):
    return functools.reduce(jnp.logical_or, [lax.axis_index("line") == i for i in lines])


def by_core(zero, one):
    me = lax.axis_index("band")
    pl.when(me == 0)(zero)
    pl.when(me != 0)(one)


def share(picked, keep, other, total, message, product):
    total[...] = keep[...] + other[...]

    def summing():
        def put(m, value):
            product[m] = value

        blurred(picked[1], total.shape[0], lambda m: total[m], put)
        encode(product, message)

    by_core(lambda: encode(total, message), summing)


def centre(picked, total, other_total, base, other_base, term):
    units = total.shape[0]

    def into(out):
        def put(m, value):
            out[m] = value

        return put

    blurred(picked[0], units, lambda m: total[m], into(base))
    blurred(picked[0], units, lambda m: other_total[m], into(other_base))
    pl.when(lax.axis_index("band") != 0)(
        lambda: blurred(picked[2], units, lambda m: total[m], into(term))
    )


def relay(term, received, message, total):
    units, lines, _ = term.shape

    def forward():
        message[...] = received[...]

    def add():
        missing = outside(1, lax.axis_size("line") - 2)
        plane = decode(received, units, lines, jnp.logical_not(missing))
        for m in range(units):
            total[m] = term[m] + plane(m)
        encode(total, message)

    by_core(forward, add)


def beside(picked, near, product):
    units, lines, _ = product.shape

    def put(m, value):
        product[m] = value

    plane = decode(near, units, lines)
    pl.when(lax.axis_index("band") == 0)(lambda: blurred(picked[1], units, plane, put))


def settle(picked, product, received, message, total):
    units, lines, _ = product.shape

    def put(m, value):
        total[m] = product[m] + value

    def add():
        missing = outside(0, lax.axis_size("line") - 1)
        plane = decode(received, units, lines, jnp.logical_not(missing))
        blurred(picked[2], units, plane, put)
        encode(total, message)

    def forward():
        message[...] = received[...]

    by_core(add, forward)

def arccos(x):
    size = jnp.abs(x)
    big = size > 0.5
    z = jnp.where(big, 0.5 * (1.0 - size), size * size)
    root = jnp.where(big, jnp.sqrt(z), size)
    poly = 4.2163199048e-2
    for term in (2.4181311049e-2, 4.5470025998e-2, 7.4953002686e-2, 1.6666752422e-1):
        poly = poly * z + term
    arcsin = poly * z * root + root
    pi = 3.14159265358979
    inner = jnp.where(x < 0, 0.5 * pi + arcsin, 0.5 * pi - arcsin)
    outer = jnp.where(x < 0, pi - 2.0 * arcsin, 2.0 * arcsin)
    return jnp.where(big, outer, inner)


def finish(second, observed, base, message, *rest):
    if second:
        sums, _, image, angles, angle, value, sems = rest
    else:
        image, sums, value, sems = rest
    units, lines, half = base.shape
    count = observed.shape[0]
    plane = decode(message, units, lines)

    def work(core):
        places = [(m, slice(c * half, (c + 1) * half)) for m, c in units_of(core, count)]
        copies = [
            pltpu.make_async_copy(value.at[n], image.at[m, :, at], sems.at[n])
            for n, (m, at) in enumerate(places)
        ]
        for n in range(units):
            value[n] = base[n] + plane(n)
            copies[n].start()
        for c in range(2):
            at = slice(c * half, (c + 1) * half)
            inner = jnp.zeros((lines, half), jnp.float32)
            left = jnp.zeros((lines, half), jnp.float32)
            for n, (m, where) in enumerate(places):
                if where == at:
                    inner = inner + value[n] * observed[m, :, at].astype(jnp.float32)
                    left = left + value[n] * value[n]
            if second:
                bound = jnp.sqrt(left + sums[1, :, at]) * sums[2, :, at]
                ratio = (inner + sums[0, :, at]) / jnp.maximum(bound, 1.0)
                angle[:, at] = arccos(jnp.clip(ratio, -1.0, 1.0))
            else:
                right = jnp.zeros((lines, half), jnp.float32)
                for m in range(count):
                    seen = observed[m, :, at].astype(jnp.float32)
                    right = right + seen * seen
                sums[0, :, at] = inner
                sums[1, :, at] = left
                sums[2, :, at] = jnp.sqrt(right)
        if second:
            copies.append(pltpu.make_async_copy(angle, angles, sems.at[units]))
            copies[-1].start()
        for copy in copies:
            copy.wait()

    if second:
        by_core(lambda: work(1), lambda: work(0))
    else:
        by_core(lambda: work(0), lambda: work(1))


def on_device(
    cube,
    observed,
    along_kernels,
    along_offsets,
    across_kernels,
    across_offsets,
    resp_start,
    resp_values,
):
    f32, i16 = jnp.float32, jnp.int16
    size = lax.axis_size("line")
    bands, lines, cols = cube.shape
    count = resp_values.shape[0]
    half = cols // 2
    _, _, units = ownership(count)
    shape = jax.ShapeDtypeStruct
    swap = [(0, 1), (1, 0)]
    partner = [(i, i ^ 1) for i in range(size)]
    even_up = [(i, (i + 2 - 4 * (i % 2)) % size) for i in range(size)]
    odd_up = [(j, i) for i, j in even_up]

    def cores(zero, one):
        return [(2 * a, 2 * b) for a, b in zero] + [(2 * a + 1, 2 * b + 1) for a, b in one]

    part = shape((units, lines, half), f32)
    coded = shape((coded_rows(units, lines), half), i16)
    unit = 4 * lines * lines * half

    inputs = (
        resp_start,
        across_offsets,
        resp_values,
        across_kernels,
        along_offsets,
        along_kernels,
        cube,
    )
    keep, send, picked = call(
        fold,
        [pltpu.with_memory_space_constraint(x, pltpu.HBM) for x in inputs],
        [HBM] * len(inputs),
        [part, part, shape(along_kernels.shape, along_kernels.dtype)],
        scratch=[
            pltpu.SMEM(resp_start.shape, jnp.int32),
            pltpu.SMEM(across_offsets.shape, jnp.int32),
            pltpu.VMEM(resp_values.shape, resp_values.dtype),
            pltpu.VMEM(resp_values.shape, f32),
            pltpu.SMEM(resp_values.shape, f32),
            pltpu.VMEM(across_kernels.shape, across_kernels.dtype),
            pltpu.SMEM(along_offsets.shape, jnp.int32),
            pltpu.VMEM(along_kernels.shape, along_kernels.dtype),
            pltpu.VMEM(cube.shape, cube.dtype),
            pltpu.VMEM((count, lines, cols), f32),
            pltpu.VMEM((2 * cols, cols), across_kernels.dtype),
            pltpu.SMEM((count,), jnp.int32),
            pltpu.SemaphoreType.DMA((len(inputs),)),
            pltpu.SemaphoreType.DMA((-(-bands // resp_values.shape[1]),)),
        ],
        flops=4 * count * lines * cols * cols,
    )
    work = [pltpu.VMEM(part.shape, f32)]
    other = lax.ppermute(send, "band", swap)
    total, message = call(share, (picked, keep, other), [VMEM] * 3, [part, coded], scratch=work)
    near = lax.ppermute(message, ("line", "band"), cores(partner, odd_up))
    other_total = lax.ppermute(total, "band", swap)
    base, other_base, term = call(
        centre, (picked, total, other_total), [VMEM] * 3, [part] * 3, flops=3 * unit * units
    )
    near, base, other_base, term = lax.optimization_barrier((near, base, other_base, term))
    (message,) = call(relay, (term, near), [VMEM] * 2, [coded], scratch=work)
    message, near = lax.optimization_barrier((message, near))
    far = lax.ppermute(message, ("line", "band"), cores(even_up, partner))
    (product,) = call(beside, (picked, near), [VMEM] * 2, [part], flops=unit * units)
    (message,) = call(
        settle, (picked, product, far), [VMEM] * 3, [coded], scratch=work, flops=unit * units
    )
    other_message = lax.ppermute(message, "band", swap)
    image = shape((count, lines, cols), f32)
    image, sums = call(
        functools.partial(finish, False),
        (observed, base, message),
        [VMEM] * 3,
        [image, shape((3, lines, cols), f32)],
        scratch=work + [pltpu.SemaphoreType.DMA((units,))],
        out_specs=[HBM, VMEM],
    )
    image, angles = call(
        functools.partial(finish, True),
        (observed, other_base, other_message, sums, image),
        [VMEM] * 4 + [HBM],
        [image, shape((lines, cols), f32)],
        scratch=[pltpu.VMEM((lines, cols), f32), *work, pltpu.SemaphoreType.DMA((units + 1,))],
        out_specs=[HBM] * 2,
        aliases={4: 0},
    )
    return image, angles


def solution(mesh):
    placed = (
        P("band", ("slab", "line"), None),
        P(None, ("slab", "line"), None),
        P(),
        P(),
        P(),
        P(),
        P(),
        P(),
    )
    return jax.shard_map(
        on_device,
        mesh=mesh,
        in_specs=placed,
        out_specs=(P(None, ("slab", "line"), None), P(("slab", "line"), None)),
        check_vma=False,
    )
```

```python
import functools
import math

import jax
import jax.numpy as jnp
from jax import lax
from jax.experimental import pallas as pl
from jax.experimental.pallas import tpu as pltpu
from jax.sharding import PartitionSpec as P

BLK = 128
SPB = 10
STEPS = 16.0
PEAK = 32000.0


def which(offsets, shift):
    return sum(
        jnp.where(offsets[k] == shift, jnp.int32(k), jnp.int32(0)) for k in range(offsets.shape[0])
    )


def split(value):
    high = value.astype(jnp.bfloat16)
    low = (value - high.astype(jnp.float32)).astype(jnp.bfloat16)
    return high, low


SMEM = pl.BlockSpec(memory_space=pltpu.SMEM)
VMEM = pl.BlockSpec(memory_space=pltpu.VMEM)
HBM = pl.BlockSpec(memory_space=pltpu.HBM)
ROWS = 64


def call(kernel, inputs, specs, outs, scratch=(), out_specs=None, aliases=None):
    return pl.pallas_call(
        kernel,
        in_specs=specs,
        out_specs=out_specs or [VMEM] * len(outs),
        out_shape=outs,
        scratch_shapes=scratch,
        input_output_aliases=aliases or {},
        compiler_params=pltpu.CompilerParams(vmem_limit_bytes=32 * 2**20),
        cost_estimate=pl.CostEstimate(flops=0, bytes_accessed=0, transcendentals=0),
        name=(kernel.func if isinstance(kernel, functools.partial) else kernel).__name__,
    )(*inputs)


def ownership(count):
    pairs = count // 2
    return pairs, count % 2, 2 * pairs + count % 2


def units_of(core, count):
    pairs, odd, _ = ownership(count)
    first = core * (pairs + odd)
    return [(first + i, c) for i in range(pairs) for c in range(2)] + [(pairs, core)] * odd


def fold(
    start_in,
    offsets_in,
    values_in,
    blocks_in,
    along_offsets_in,
    along_blocks_in,
    cube_in,
    keep,
    send,
    picked,
    start,
    offsets,
    values,
    wide,
    weights,
    blocks,
    along_offsets,
    along_blocks,
    cube,
    folded,
    table,
    order,
    small,
    large,
):
    bands, lines, cols = cube.shape
    count, window = values.shape
    half = cols // 2
    group = math.gcd(SPB, bands)
    me = lax.axis_index("band")
    pairs = (
        (start_in, start),
        (values_in, values),
        (offsets_in, offsets),
        (blocks_in, blocks),
        (along_offsets_in, along_offsets),
        (along_blocks_in, along_blocks),
    )
    copies = [pltpu.make_async_copy(a, b, small.at[i]) for i, (a, b) in enumerate(pairs)]

    chunks = -(-bands // window)
    last = bands - (chunks - 1) * window

    def arrive(q, size):
        at = pl.ds(q * window, size)
        return pltpu.make_async_copy(cube_in.at[at], cube.at[at], large.at[q])

    for copy in copies:
        copy.start()
    for q in range(chunks):
        arrive(q, window if q < chunks - 1 else last).start()
    copies[1].wait()
    wide[...] = values[...].astype(jnp.float32)
    spread = pltpu.make_async_copy(wide, weights, small.at[len(pairs)])
    spread.start()
    copies[0].wait()

    places = [SPB * start[m] - bands * me for m in range(count)]
    ranks = [jnp.int32(0)] * count
    for m in range(count):
        for n in range(m + 1, count):
            later = (places[n] < places[m]).astype(jnp.int32)
            ranks[m] = ranks[m] + later
            ranks[n] = ranks[n] + (1 - later)
    before = jnp.int32(0)
    until = jnp.int32(0)
    for m in range(count):
        order[ranks[m]] = jnp.int32(m)
        before = before + (places[m] <= -window).astype(jnp.int32)
        until = until + (places[m] < bands).astype(jnp.int32)

    def clear(n, carry):
        folded[order[n]] = jnp.zeros((lines, cols), jnp.float32)
        return carry

    lax.fori_loop(0, before, clear, 0)
    lax.fori_loop(until, count, clear, 0)
    for copy in copies[2:]:
        copy.wait()
    for r in range(2):
        for c in range(2):
            block = blocks[which(offsets, jnp.int32(r - c))].astype(jnp.float32).T
            for top in (0, cols):
                at = slice(top + r * half, top + (r + 1) * half)
                table[at, c * half : (c + 1) * half] = block.astype(jnp.bfloat16)
    step = side_step()
    for i, shift in enumerate((jnp.int32(0), step, -step)):
        picked[i] = along_blocks[which(along_offsets, shift)]
    spread.wait()

    def ready(q, carry):
        pl.when(q < chunks - 1)(lambda: arrive(q, window).wait())
        pl.when(q == chunks - 1)(lambda: arrive(chunks - 1, last).wait())
        return carry

    def one(n, arrived):
        m = order[n]
        low = SPB * start[m] - bands * me
        stop = jnp.minimum(low + window, bands)
        needed = lax.div(stop - 1, jnp.int32(window)) + 1
        lax.fori_loop(arrived, needed, ready, 0)
        whole = jnp.logical_and(low >= 0, low + window <= bands)

        def term(band, weight, r):
            return weight * cube[band, r : r + ROWS, :].astype(jnp.float32)

        @pl.when(whole)
        def _():
            for r in range(0, lines, ROWS):
                total = term(low, weights[m, 0], r)
                for j in range(1, window):
                    total = total + term(low + j, weights[m, j], r)
                folded[m, r : r + ROWS, :] = total

        @pl.when(jnp.logical_not(whole))
        def _():
            first = jnp.maximum(low, 0)
            for r in range(0, lines, ROWS):

                def some(t, total):
                    for i in range(group):
                        band = first + t * group + i
                        total = total + term(band, weights[m, band - low], r)
                    return total

                folded[m, r : r + ROWS, :] = lax.fori_loop(
                    0,
                    lax.div(stop - first, jnp.int32(group)),
                    some,
                    jnp.zeros((ROWS, cols), jnp.float32),
                )

        return jnp.maximum(arrived, needed)

    arrived = lax.fori_loop(before, until, one, jnp.int32(0))
    lax.fori_loop(arrived, chunks, ready, 0)

    side = table[...]
    planes, odd, units = ownership(count)

    def across(at, planes):
        value = folded[pl.ds(at, planes)].reshape(planes * lines, cols)
        both = jnp.concatenate(split(value), axis=1)
        made = jnp.dot(both, side, preferred_element_type=jnp.float32)
        return made.reshape(planes, lines, cols)

    for owner, out in ((me, keep), (1 - me, send)):
        made = across(owner * (planes + odd), planes)
        for i in range(planes):
            out[2 * i] = made[i, :, :half]
            out[2 * i + 1] = made[i, :, half:]
    if odd:
        made = across(planes, 1)[0]
        left, right = made[:, :half], made[:, half:]
        keep[units - 1] = jnp.where(me == 0, left, right)
        send[units - 1] = jnp.where(me == 0, right, left)


def coded_rows(count, lines):
    return count * lines + -(-count // 16) * 16


def encode(source, span, message):
    _, lines, half = source.shape
    units = span[1] - span[0]
    largest = jnp.max(jnp.abs(source[span[0] : span[1]]), axis=1)
    level = jnp.ceil(jnp.log2(jnp.maximum(largest, 1e-30)) * STEPS)
    factor = PEAK * jnp.exp2(level * (-1.0 / STEPS))
    for m in range(units):
        coded = jnp.floor(source[span[0] + m] * factor[m : m + 1, :] + 0.5).astype(jnp.int32)
        message[m * lines : (m + 1) * lines, :] = coded.astype(jnp.int16)
    spare = message.shape[0] - units * lines - units
    level = jnp.concatenate([level, jnp.zeros((spare, half), jnp.float32)], axis=0)
    message[units * lines :, :] = level.astype(jnp.int32).astype(jnp.int16)


def decode(message, span, lines, valid=True):
    units = span[1] - span[0]
    level = message[units * lines :, :].astype(jnp.int32).astype(jnp.float32)
    scale = jnp.where(valid, jnp.exp2(level * (1.0 / STEPS)) * (1.0 / PEAK), 0.0)

    def plane(m):
        coded = message[m * lines : (m + 1) * lines, :].astype(jnp.int32).astype(jnp.float32)
        return coded * scale[m : m + 1, :]

    return plane


def blurred(filters, count, plane, put):
    wide = jnp.concatenate([filters, filters], axis=1)
    for m in range(0, count, 2):
        parts = [split(plane(n)) for n in range(m, min(m + 2, count))]
        high = jnp.concatenate([p[0] for p in parts], axis=1)
        low = jnp.concatenate([p[1] for p in parts], axis=1)
        made = jnp.dot(
            wide, jnp.concatenate([high, low], axis=0), preferred_element_type=jnp.float32
        )
        half = made.shape[1] // len(parts)
        for i in range(len(parts)):
            put(m + i, made[:, i * half : (i + 1) * half])


def side_step():
    return jnp.where(lax.axis_index("line") % 2 == 0, jnp.int32(1), jnp.int32(-1))


def outside(*lines):
    return functools.reduce(jnp.logical_or, [lax.axis_index("line") == i for i in lines])


def by_core(zero, one):
    me = lax.axis_index("band")
    pl.when(me == 0)(zero)
    pl.when(me != 0)(one)


def share(spans, picked, keep, other, total, *rest):
    messages, product = rest[:-1], rest[-1]
    total[...] = keep[...] + other[...]

    def coding(source):
        for span, message in zip(spans, messages):
            encode(source, span, message)

    def summing():
        def put(m, value):
            product[m] = value

        blurred(picked[1], total.shape[0], lambda m: total[m], put)
        coding(product)

    by_core(lambda: coding(total), summing)


def centre(picked, total, other_total, base, other_base, term):
    units = total.shape[0]

    def into(out):
        def put(m, value):
            out[m] = value

        return put

    blurred(picked[0], units, lambda m: total[m], into(base))
    blurred(picked[0], units, lambda m: other_total[m], into(other_base))
    pl.when(lax.axis_index("band") != 0)(
        lambda: blurred(picked[2], units, lambda m: total[m], into(term))
    )


def relay(span, term, received, message, total):
    def forward():
        message[...] = received[...]

    def add():
        missing = outside(1, lax.axis_size("line") - 2)
        plane = decode(received, span, term.shape[1], jnp.logical_not(missing))
        for m in range(*span):
            total[m] = term[m] + plane(m - span[0])
        encode(total, span, message)

    by_core(forward, add)


def beside(span, picked, near, product):
    units, lines, _ = product.shape

    def put(m, value):
        product[m] = value

    plane = decode(near, span, lines)
    pl.when(lax.axis_index("band") == 0)(lambda: blurred(picked[1], units, plane, put))


def settle(span, picked, product, received, message, total):
    units, lines, _ = product.shape

    def put(m, value):
        total[m] = product[m] + value

    def add():
        missing = outside(0, lax.axis_size("line") - 1)
        plane = decode(received, span, lines, jnp.logical_not(missing))
        blurred(picked[2], units, plane, put)
        encode(total, (0, units), message)

    def forward():
        message[...] = received[...]

    by_core(add, forward)


def arccos(x):
    size = jnp.abs(x)
    big = size > 0.5
    z = jnp.where(big, 0.5 * (1.0 - size), size * size)
    root = jnp.where(big, jnp.sqrt(z), size)
    poly = 4.2163199048e-2
    for term in (2.4181311049e-2, 4.5470025998e-2, 7.4953002686e-2, 1.6666752422e-1):
        poly = poly * z + term
    arcsin = poly * z * root + root
    pi = 3.14159265358979
    inner = jnp.where(x < 0, 0.5 * pi + arcsin, 0.5 * pi - arcsin)
    outer = jnp.where(x < 0, pi - 2.0 * arcsin, 2.0 * arcsin)
    return jnp.where(big, outer, inner)


def finish(second, spans, observed, base, *rest):
    messages, rest = rest[: len(spans)], rest[len(spans) :]
    if second:
        sums, _, image, angles, angle, value, sems = rest
    else:
        image, sums, value, sems = rest
    units, lines, half = base.shape
    count = observed.shape[0]

    def work(core):
        places = [(m, slice(c * half, (c + 1) * half)) for m, c in units_of(core, count)]
        copies = [
            pltpu.make_async_copy(value.at[n], image.at[m, :, at], sems.at[n])
            for n, (m, at) in enumerate(places)
        ]
        for span, message in zip(spans, messages):
            plane = decode(message, span, lines)
            for n in range(*span):
                value[n] = base[n] + plane(n - span[0])
                copies[n].start()
        for c in range(2):
            at = slice(c * half, (c + 1) * half)
            inner = jnp.zeros((lines, half), jnp.float32)
            left = jnp.zeros((lines, half), jnp.float32)
            for n, (m, where) in enumerate(places):
                if where == at:
                    inner = inner + value[n] * observed[m, :, at].astype(jnp.float32)
                    left = left + value[n] * value[n]
            if second:
                bound = jnp.sqrt(left + sums[1, :, at]) * sums[2, :, at]
                ratio = (inner + sums[0, :, at]) / jnp.maximum(bound, 1.0)
                angle[:, at] = arccos(jnp.clip(ratio, -1.0, 1.0))
            else:
                right = jnp.zeros((lines, half), jnp.float32)
                for m in range(count):
                    seen = observed[m, :, at].astype(jnp.float32)
                    right = right + seen * seen
                sums[0, :, at] = inner
                sums[1, :, at] = left
                sums[2, :, at] = jnp.sqrt(right)
        if second:
            copies.append(pltpu.make_async_copy(angle, angles, sems.at[units]))
            copies[-1].start()
        for copy in copies:
            copy.wait()

    if second:
        by_core(lambda: work(1), lambda: work(0))
    else:
        by_core(lambda: work(0), lambda: work(1))


def on_device(
    cube,
    observed,
    along_kernels,
    along_offsets,
    across_kernels,
    across_offsets,
    resp_start,
    resp_values,
):
    f32, i16 = jnp.float32, jnp.int16
    size = lax.axis_size("line")
    bands, lines, cols = cube.shape
    count = resp_values.shape[0]
    half = cols // 2
    _, _, units = ownership(count)
    shape = jax.ShapeDtypeStruct
    swap = [(0, 1), (1, 0)]
    partner = [(i, i ^ 1) for i in range(size)]
    even_up = [(i, (i + 2 - 4 * (i % 2)) % size) for i in range(size)]
    odd_up = [(j, i) for i, j in even_up]

    def cores(zero, one):
        return [(2 * a, 2 * b) for a, b in zero] + [(2 * a + 1, 2 * b + 1) for a, b in one]

    part = shape((units, lines, half), f32)
    spans = [(0, (units + 1) // 2), ((units + 1) // 2, units)]
    coded = [shape((coded_rows(b - a, lines), half), i16) for a, b in spans]

    inputs = (
        resp_start,
        across_offsets,
        resp_values,
        across_kernels,
        along_offsets,
        along_kernels,
        cube,
    )
    keep, send, picked = call(
        fold,
        [pltpu.with_memory_space_constraint(x, pltpu.HBM) for x in inputs],
        [HBM] * len(inputs),
        [part, part, shape(along_kernels.shape, along_kernels.dtype)],
        scratch=[
            pltpu.SMEM(resp_start.shape, jnp.int32),
            pltpu.SMEM(across_offsets.shape, jnp.int32),
            pltpu.VMEM(resp_values.shape, resp_values.dtype),
            pltpu.VMEM(resp_values.shape, f32),
            pltpu.SMEM(resp_values.shape, f32),
            pltpu.VMEM(across_kernels.shape, across_kernels.dtype),
            pltpu.SMEM(along_offsets.shape, jnp.int32),
            pltpu.VMEM(along_kernels.shape, along_kernels.dtype),
            pltpu.VMEM(cube.shape, cube.dtype),
            pltpu.VMEM((count, lines, cols), f32),
            pltpu.VMEM((2 * cols, cols), across_kernels.dtype),
            pltpu.SMEM((count,), jnp.int32),
            pltpu.SemaphoreType.DMA((len(inputs),)),
            pltpu.SemaphoreType.DMA((-(-bands // resp_values.shape[1]),)),
        ],
    )
    work = [pltpu.VMEM(part.shape, f32)]
    other = lax.ppermute(send, "band", swap)
    total, *sent = call(
        functools.partial(share, spans),
        (picked, keep, other),
        [VMEM] * 3,
        [part, *coded],
        scratch=work,
    )
    near = [lax.ppermute(x, ("line", "band"), cores(partner, odd_up)) for x in sent]
    other_total = lax.ppermute(total, "band", swap)
    base, other_base, term = call(
        centre, (picked, total, other_total), [VMEM] * 3, [part] * 3
    )
    far, product = [], []
    for i, span in enumerate(spans):
        (message,) = call(
            functools.partial(relay, span), (term, near[i]), [VMEM] * 2, [coded[i]], scratch=work
        )
        message, near[i] = lax.optimization_barrier((message, near[i]))
        far.append(lax.ppermute(message, ("line", "band"), cores(even_up, partner)))
        planes = shape((span[1] - span[0], lines, half), f32)
        product += call(
            functools.partial(beside, span),
            (picked, near[i]),
            [VMEM] * 2,
            [planes],
        )
    messages, others = [], []
    for i, span in enumerate(spans):
        planes = product[i].shape
        messages += call(
            functools.partial(settle, span),
            (picked, product[i], far[i]),
            [VMEM] * 3,
            [coded[i]],
            scratch=[pltpu.VMEM(planes, f32)],
        )
        others.append(lax.ppermute(messages[i], "band", swap))
    image = shape((count, lines, cols), f32)
    some = 2 + len(spans)
    image, sums = call(
        functools.partial(finish, False, spans),
        (observed, base, *messages),
        [VMEM] * some,
        [image, shape((3, lines, cols), f32)],
        scratch=work + [pltpu.SemaphoreType.DMA((units,))],
        out_specs=[HBM, VMEM],
    )
    image, angles = call(
        functools.partial(finish, True, spans),
        (observed, other_base, *others, sums, image),
        [VMEM] * (some + 1) + [HBM],
        [image, shape((lines, cols), f32)],
        scratch=[pltpu.VMEM((lines, cols), f32), *work, pltpu.SemaphoreType.DMA((units + 1,))],
        out_specs=[HBM] * 2,
        aliases={some + 1: 0},
    )
    return image, angles


def solution(mesh):
    placed = (
        P("band", ("slab", "line"), None),
        P(None, ("slab", "line"), None),
        P(),
        P(),
        P(),
        P(),
        P(),
        P(),
    )
    return jax.shard_map(
        on_device,
        mesh=mesh,
        in_specs=placed,
        out_specs=(P(None, ("slab", "line"), None), P(("slab", "line"), None)),
        check_vma=False,
    )
```

```python
import functools
import math

import jax
import jax.numpy as jnp
from jax import lax
from jax.experimental import pallas as pl
from jax.experimental.pallas import tpu as pltpu
from jax.sharding import PartitionSpec as P

BLK = 128
SPB = 10
STEPS = 16.0
PEAK = 32000.0


def which(offsets, shift):
    return sum(
        jnp.where(offsets[k] == shift, jnp.int32(k), jnp.int32(0)) for k in range(offsets.shape[0])
    )


def split(value):
    high = value.astype(jnp.bfloat16)
    low = (value - high.astype(jnp.float32)).astype(jnp.bfloat16)
    return high, low


SMEM = pl.BlockSpec(memory_space=pltpu.SMEM)
VMEM = pl.BlockSpec(memory_space=pltpu.VMEM)
HBM = pl.BlockSpec(memory_space=pltpu.HBM)
ROWS = 64


def call(kernel, inputs, specs, outs, scratch=(), out_specs=None, aliases=None):
    return pl.pallas_call(
        kernel,
        in_specs=specs,
        out_specs=out_specs or [VMEM] * len(outs),
        out_shape=outs,
        scratch_shapes=scratch,
        input_output_aliases=aliases or {},
        compiler_params=pltpu.CompilerParams(vmem_limit_bytes=32 * 2**20),
        cost_estimate=pl.CostEstimate(flops=0, bytes_accessed=0, transcendentals=0),
        name=(kernel.func if isinstance(kernel, functools.partial) else kernel).__name__,
    )(*inputs)


def ownership(count):
    pairs = count // 2
    return pairs, count % 2, 2 * pairs + count % 2


def units_of(core, count):
    pairs, odd, _ = ownership(count)
    first = core * (pairs + odd)
    return [(first + i, c) for i in range(pairs) for c in range(2)] + [(pairs, core)] * odd


def fold(
    start_in,
    offsets_in,
    values_in,
    blocks_in,
    along_offsets_in,
    along_blocks_in,
    cube_in,
    keep,
    send,
    picked,
    start,
    offsets,
    values,
    wide,
    weights,
    blocks,
    along_offsets,
    along_blocks,
    cube,
    bands_out,
    folded,
    table,
    order,
    small,
    large,
):
    bands, lines, cols = cube.shape
    count, window = values.shape
    half = cols // 2
    group = math.gcd(SPB, bands)
    me = lax.axis_index("band")
    pairs = (
        (start_in, start),
        (values_in, values),
        (offsets_in, offsets),
        (blocks_in, blocks),
        (along_offsets_in, along_offsets),
        (along_blocks_in, along_blocks),
    )
    copies = [pltpu.make_async_copy(a, b, small.at[i]) for i, (a, b) in enumerate(pairs)]

    chunks = -(-bands // window)
    last = bands - (chunks - 1) * window

    def arrive(q, size):
        at = pl.ds(q * window, size)
        return pltpu.make_async_copy(cube_in.at[at], cube.at[at], large.at[q])

    for copy in copies:
        copy.start()
    for q in range(chunks):
        arrive(q, window if q < chunks - 1 else last).start()
    copies[1].wait()
    wide[...] = values[...].astype(jnp.float32)
    spread = pltpu.make_async_copy(wide, weights, small.at[len(pairs)])
    spread.start()
    copies[0].wait()

    places = [SPB * start[m] - bands * me for m in range(count)]
    ranks = [jnp.int32(0)] * count
    for m in range(count):
        for n in range(m + 1, count):
            later = (places[n] < places[m]).astype(jnp.int32)
            ranks[m] = ranks[m] + later
            ranks[n] = ranks[n] + (1 - later)
    before = jnp.int32(0)
    until = jnp.int32(0)
    for m in range(count):
        order[ranks[m]] = jnp.int32(m)
        before = before + (places[m] <= -window).astype(jnp.int32)
        until = until + (places[m] < bands).astype(jnp.int32)

    def clear(n, carry):
        folded[order[n]] = jnp.zeros((lines, cols), jnp.float32)
        return carry

    lax.fori_loop(0, before, clear, 0)
    lax.fori_loop(until, count, clear, 0)
    for copy in copies[2:]:
        copy.wait()
    for r in range(2):
        for c in range(2):
            block = blocks[which(offsets, jnp.int32(r - c))].astype(jnp.float32).T
            at = slice(r * half, (r + 1) * half)
            table[at, c * half : (c + 1) * half] = block.astype(jnp.bfloat16)
    step = side_step()
    for i, shift in enumerate((jnp.int32(0), step, -step)):
        picked[i] = along_blocks[which(along_offsets, shift)]
    spread.wait()

    side = table[...]

    def across(band, carry):
        value = cube[pl.ds(band, group)].reshape(group * lines, cols)
        made = jnp.dot(value, side, preferred_element_type=jnp.float32)
        bands_out[pl.ds(band, group)] = made.reshape(group, lines, cols)
        return carry

    def ready(q, used):
        def take(size):
            arrive(q, size).wait()

            @pl.when(used)
            def _():
                lax.fori_loop(0, size // group, lambda t, c: across(q * window + t * group, c), 0)

        pl.when(q < chunks - 1)(lambda: take(window))
        pl.when(q == chunks - 1)(lambda: take(last))
        return used

    def one(n, arrived):
        m = order[n]
        low = SPB * start[m] - bands * me
        stop = jnp.minimum(low + window, bands)
        needed = lax.div(stop - 1, jnp.int32(window)) + 1
        lax.fori_loop(arrived, needed, ready, True)
        whole = jnp.logical_and(low >= 0, low + window <= bands)

        def term(band, weight, r):
            return weight * bands_out[band, r : r + ROWS, :]

        @pl.when(whole)
        def _():
            for r in range(0, lines, ROWS):
                total = term(low, weights[m, 0], r)
                for j in range(1, window):
                    total = total + term(low + j, weights[m, j], r)
                folded[m, r : r + ROWS, :] = total

        @pl.when(jnp.logical_not(whole))
        def _():
            first = jnp.maximum(low, 0)
            for r in range(0, lines, ROWS):

                def some(t, total):
                    for i in range(group):
                        band = first + t * group + i
                        total = total + term(band, weights[m, band - low], r)
                    return total

                folded[m, r : r + ROWS, :] = lax.fori_loop(
                    0,
                    lax.div(stop - first, jnp.int32(group)),
                    some,
                    jnp.zeros((ROWS, cols), jnp.float32),
                )

        return jnp.maximum(arrived, needed)

    arrived = lax.fori_loop(before, until, one, jnp.int32(0))
    lax.fori_loop(arrived, chunks, ready, False)

    planes, odd, units = ownership(count)
    for owner, out in ((me, keep), (1 - me, send)):
        for i in range(planes):
            made = folded[owner * (planes + odd) + i]
            out[2 * i] = made[:, :half]
            out[2 * i + 1] = made[:, half:]
    if odd:
        left, right = folded[planes, :, :half], folded[planes, :, half:]
        keep[units - 1] = jnp.where(me == 0, left, right)
        send[units - 1] = jnp.where(me == 0, right, left)


def coded_rows(count, lines):
    return count * lines + -(-count // 16) * 16


def encode(source, span, message):
    _, lines, half = source.shape
    units = span[1] - span[0]
    largest = jnp.max(jnp.abs(source[span[0] : span[1]]), axis=1)
    level = jnp.ceil(jnp.log2(jnp.maximum(largest, 1e-30)) * STEPS)
    factor = PEAK * jnp.exp2(level * (-1.0 / STEPS))
    for m in range(units):
        coded = jnp.floor(source[span[0] + m] * factor[m : m + 1, :] + 0.5).astype(jnp.int32)
        message[m * lines : (m + 1) * lines, :] = coded.astype(jnp.int16)
    spare = message.shape[0] - units * lines - units
    level = jnp.concatenate([level, jnp.zeros((spare, half), jnp.float32)], axis=0)
    message[units * lines :, :] = level.astype(jnp.int32).astype(jnp.int16)


def decode(message, span, lines, valid=True):
    units = span[1] - span[0]
    level = message[units * lines :, :].astype(jnp.int32).astype(jnp.float32)
    scale = jnp.where(valid, jnp.exp2(level * (1.0 / STEPS)) * (1.0 / PEAK), 0.0)

    def plane(m):
        coded = message[m * lines : (m + 1) * lines, :].astype(jnp.int32).astype(jnp.float32)
        return coded * scale[m : m + 1, :]

    return plane


def blurred(filters, count, plane, put):
    wide = jnp.concatenate([filters, filters], axis=1)
    for m in range(0, count, 2):
        parts = [split(plane(n)) for n in range(m, min(m + 2, count))]
        high = jnp.concatenate([p[0] for p in parts], axis=1)
        low = jnp.concatenate([p[1] for p in parts], axis=1)
        made = jnp.dot(
            wide, jnp.concatenate([high, low], axis=0), preferred_element_type=jnp.float32
        )
        half = made.shape[1] // len(parts)
        for i in range(len(parts)):
            put(m + i, made[:, i * half : (i + 1) * half])


def side_step():
    return jnp.where(lax.axis_index("line") % 2 == 0, jnp.int32(1), jnp.int32(-1))


def outside(*lines):
    return functools.reduce(jnp.logical_or, [lax.axis_index("line") == i for i in lines])


def by_core(zero, one):
    me = lax.axis_index("band")
    pl.when(me == 0)(zero)
    pl.when(me != 0)(one)


def share(spans, picked, keep, other, total, *rest):
    messages, product = rest[:-1], rest[-1]
    total[...] = keep[...] + other[...]

    def coding(source):
        for span, message in zip(spans, messages):
            encode(source, span, message)

    def summing():
        def put(m, value):
            product[m] = value

        blurred(picked[1], total.shape[0], lambda m: total[m], put)
        coding(product)

    by_core(lambda: coding(total), summing)


def centre(picked, total, other_total, base, other_base, term):
    units = total.shape[0]

    def into(out):
        def put(m, value):
            out[m] = value

        return put

    blurred(picked[0], units, lambda m: total[m], into(base))
    blurred(picked[0], units, lambda m: other_total[m], into(other_base))
    pl.when(lax.axis_index("band") != 0)(
        lambda: blurred(picked[2], units, lambda m: total[m], into(term))
    )


def relay(span, term, received, message, total):
    def forward():
        message[...] = received[...]

    def add():
        missing = outside(1, lax.axis_size("line") - 2)
        plane = decode(received, span, term.shape[1], jnp.logical_not(missing))
        for m in range(*span):
            total[m] = term[m] + plane(m - span[0])
        encode(total, span, message)

    by_core(forward, add)


def beside(span, picked, near, product):
    units, lines, _ = product.shape

    def put(m, value):
        product[m] = value

    plane = decode(near, span, lines)
    pl.when(lax.axis_index("band") == 0)(lambda: blurred(picked[1], units, plane, put))


def settle(span, picked, product, received, message, total):
    units, lines, _ = product.shape

    def put(m, value):
        total[m] = product[m] + value

    def add():
        missing = outside(0, lax.axis_size("line") - 1)
        plane = decode(received, span, lines, jnp.logical_not(missing))
        blurred(picked[2], units, plane, put)
        encode(total, (0, units), message)

    def forward():
        message[...] = received[...]

    by_core(add, forward)


def arccos(x):
    size = jnp.abs(x)
    big = size > 0.5
    z = jnp.where(big, 0.5 * (1.0 - size), size * size)
    root = jnp.where(big, jnp.sqrt(z), size)
    poly = 4.2163199048e-2
    for term in (2.4181311049e-2, 4.5470025998e-2, 7.4953002686e-2, 1.6666752422e-1):
        poly = poly * z + term
    arcsin = poly * z * root + root
    pi = 3.14159265358979
    inner = jnp.where(x < 0, 0.5 * pi + arcsin, 0.5 * pi - arcsin)
    outer = jnp.where(x < 0, pi - 2.0 * arcsin, 2.0 * arcsin)
    return jnp.where(big, outer, inner)


def finish(second, spans, observed, base, *rest):
    messages, rest = rest[: len(spans)], rest[len(spans) :]
    if second:
        sums, _, image, angles, angle, value, sems = rest
    else:
        image, sums, value, sems = rest
    units, lines, half = base.shape
    count = observed.shape[0]

    def work(core):
        places = [(m, slice(c * half, (c + 1) * half)) for m, c in units_of(core, count)]
        copies = [
            pltpu.make_async_copy(value.at[n], image.at[m, :, at], sems.at[n])
            for n, (m, at) in enumerate(places)
        ]
        for span, message in zip(spans, messages):
            plane = decode(message, span, lines)
            for n in range(*span):
                value[n] = base[n] + plane(n - span[0])
                copies[n].start()
        for c in range(2):
            at = slice(c * half, (c + 1) * half)
            inner = jnp.zeros((lines, half), jnp.float32)
            left = jnp.zeros((lines, half), jnp.float32)
            for n, (m, where) in enumerate(places):
                if where == at:
                    inner = inner + value[n] * observed[m, :, at].astype(jnp.float32)
                    left = left + value[n] * value[n]
            if second:
                bound = jnp.sqrt(left + sums[1, :, at]) * sums[2, :, at]
                ratio = (inner + sums[0, :, at]) / jnp.maximum(bound, 1.0)
                angle[:, at] = arccos(jnp.clip(ratio, -1.0, 1.0))
            else:
                right = jnp.zeros((lines, half), jnp.float32)
                for m in range(count):
                    seen = observed[m, :, at].astype(jnp.float32)
                    right = right + seen * seen
                sums[0, :, at] = inner
                sums[1, :, at] = left
                sums[2, :, at] = jnp.sqrt(right)
        if second:
            copies.append(pltpu.make_async_copy(angle, angles, sems.at[units]))
            copies[-1].start()
        for copy in copies:
            copy.wait()

    if second:
        by_core(lambda: work(1), lambda: work(0))
    else:
        by_core(lambda: work(0), lambda: work(1))


def on_device(
    cube,
    observed,
    along_kernels,
    along_offsets,
    across_kernels,
    across_offsets,
    resp_start,
    resp_values,
):
    f32, i16 = jnp.float32, jnp.int16
    size = lax.axis_size("line")
    bands, lines, cols = cube.shape
    count = resp_values.shape[0]
    half = cols // 2
    _, _, units = ownership(count)
    shape = jax.ShapeDtypeStruct
    swap = [(0, 1), (1, 0)]
    partner = [(i, i ^ 1) for i in range(size)]
    even_up = [(i, (i + 2 - 4 * (i % 2)) % size) for i in range(size)]
    odd_up = [(j, i) for i, j in even_up]

    def cores(zero, one):
        return [(2 * a, 2 * b) for a, b in zero] + [(2 * a + 1, 2 * b + 1) for a, b in one]

    part = shape((units, lines, half), f32)
    spans = [(0, (units + 1) // 2), ((units + 1) // 2, units)]
    coded = [shape((coded_rows(b - a, lines), half), i16) for a, b in spans]

    inputs = (
        resp_start,
        across_offsets,
        resp_values,
        across_kernels,
        along_offsets,
        along_kernels,
        cube,
    )
    keep, send, picked = call(
        fold,
        [pltpu.with_memory_space_constraint(x, pltpu.HBM) for x in inputs],
        [HBM] * len(inputs),
        [part, part, shape(along_kernels.shape, along_kernels.dtype)],
        scratch=[
            pltpu.SMEM(resp_start.shape, jnp.int32),
            pltpu.SMEM(across_offsets.shape, jnp.int32),
            pltpu.VMEM(resp_values.shape, resp_values.dtype),
            pltpu.VMEM(resp_values.shape, f32),
            pltpu.SMEM(resp_values.shape, f32),
            pltpu.VMEM(across_kernels.shape, across_kernels.dtype),
            pltpu.SMEM(along_offsets.shape, jnp.int32),
            pltpu.VMEM(along_kernels.shape, along_kernels.dtype),
            pltpu.VMEM(cube.shape, cube.dtype),
            pltpu.VMEM(cube.shape, f32),
            pltpu.VMEM((count, lines, cols), f32),
            pltpu.VMEM((cols, cols), across_kernels.dtype),
            pltpu.SMEM((count,), jnp.int32),
            pltpu.SemaphoreType.DMA((len(inputs),)),
            pltpu.SemaphoreType.DMA((-(-bands // resp_values.shape[1]),)),
        ],
    )
    work = [pltpu.VMEM(part.shape, f32)]
    other = lax.ppermute(send, "band", swap)
    total, *sent = call(
        functools.partial(share, spans),
        (picked, keep, other),
        [VMEM] * 3,
        [part, *coded],
        scratch=work,
    )
    near = [lax.ppermute(x, ("line", "band"), cores(partner, odd_up)) for x in sent]
    other_total = lax.ppermute(total, "band", swap)
    base, other_base, term = call(
        centre, (picked, total, other_total), [VMEM] * 3, [part] * 3
    )
    far, product = [], []
    for i, span in enumerate(spans):
        (message,) = call(
            functools.partial(relay, span), (term, near[i]), [VMEM] * 2, [coded[i]], scratch=work
        )
        message, near[i] = lax.optimization_barrier((message, near[i]))
        far.append(lax.ppermute(message, ("line", "band"), cores(even_up, partner)))
        planes = shape((span[1] - span[0], lines, half), f32)
        product += call(
            functools.partial(beside, span),
            (picked, near[i]),
            [VMEM] * 2,
            [planes],
        )
    messages, others = [], []
    for i, span in enumerate(spans):
        planes = product[i].shape
        messages += call(
            functools.partial(settle, span),
            (picked, product[i], far[i]),
            [VMEM] * 3,
            [coded[i]],
            scratch=[pltpu.VMEM(planes, f32)],
        )
        others.append(lax.ppermute(messages[i], "band", swap))
    image = shape((count, lines, cols), f32)
    some = 2 + len(spans)
    image, sums = call(
        functools.partial(finish, False, spans),
        (observed, base, *messages),
        [VMEM] * some,
        [image, shape((3, lines, cols), f32)],
        scratch=work + [pltpu.SemaphoreType.DMA((units,))],
        out_specs=[HBM, VMEM],
    )
    image, angles = call(
        functools.partial(finish, True, spans),
        (observed, other_base, *others, sums, image),
        [VMEM] * (some + 1) + [HBM],
        [image, shape((lines, cols), f32)],
        scratch=[pltpu.VMEM((lines, cols), f32), *work, pltpu.SemaphoreType.DMA((units + 1,))],
        out_specs=[HBM] * 2,
        aliases={some + 1: 0},
    )
    return image, angles


def solution(mesh):
    placed = (
        P("band", ("slab", "line"), None),
        P(None, ("slab", "line"), None),
        P(),
        P(),
        P(),
        P(),
        P(),
        P(),
    )
    return jax.shard_map(
        on_device,
        mesh=mesh,
        in_specs=placed,
        out_specs=(P(None, ("slab", "line"), None), P(("slab", "line"), None)),
        check_vma=False,
    )
```

```python
import functools
import math

import jax
import jax.numpy as jnp
from jax import lax
from jax.experimental import pallas as pl
from jax.experimental.pallas import tpu as pltpu
from jax.sharding import PartitionSpec as P

BLK = 128
SPB = 10
STEPS = 16.0
PEAK = 32000.0


def which(offsets, shift):
    return sum(
        jnp.where(offsets[k] == shift, jnp.int32(k), jnp.int32(0)) for k in range(offsets.shape[0])
    )


def split(value):
    high = value.astype(jnp.bfloat16)
    low = (value - high.astype(jnp.float32)).astype(jnp.bfloat16)
    return high, low


SMEM = pl.BlockSpec(memory_space=pltpu.SMEM)
VMEM = pl.BlockSpec(memory_space=pltpu.VMEM)
HBM = pl.BlockSpec(memory_space=pltpu.HBM)
ROWS = 64


def call(kernel, inputs, specs, outs, scratch=(), out_specs=None, aliases=None):
    return pl.pallas_call(
        kernel,
        in_specs=specs,
        out_specs=out_specs or [VMEM] * len(outs),
        out_shape=[jax.ShapeDtypeStruct(x.shape, x.dtype) for x in outs],
        scratch_shapes=scratch,
        input_output_aliases=aliases or {},
        compiler_params=pltpu.CompilerParams(vmem_limit_bytes=32 * 2**20),
        cost_estimate=pl.CostEstimate(flops=0, bytes_accessed=0, transcendentals=0),
        name=(kernel.func if isinstance(kernel, functools.partial) else kernel).__name__,
    )(*inputs)


def ownership(count):
    pairs = count // 2
    return pairs, count % 2, 2 * pairs + count % 2


def units_of(core, count):
    pairs, odd, _ = ownership(count)
    first = core * (pairs + odd)
    return [(first + i, c) for i in range(pairs) for c in range(2)] + [(pairs, core)] * odd


def sum_windows(number, plane_of, start, weights, cube, folded, order, ready=None):
    bands, lines, cols = cube.shape
    window = weights.shape[1]
    group = math.gcd(SPB, bands)
    first = bands * lax.axis_index("band")
    places = [SPB * start[plane_of(i)] - first for i in range(number)]
    ranks = [jnp.int32(0)] * number
    for m in range(number):
        for n in range(m + 1, number):
            later = (places[n] < places[m]).astype(jnp.int32)
            ranks[m] = ranks[m] + later
            ranks[n] = ranks[n] + (1 - later)
    before = jnp.int32(0)
    until = jnp.int32(0)
    for m in range(number):
        order[ranks[m]] = jnp.int32(m)
        before = before + (places[m] <= -window).astype(jnp.int32)
        until = until + (places[m] < bands).astype(jnp.int32)

    def clear(n, carry):
        folded[order[n]] = jnp.zeros((lines, cols), jnp.float32)
        return carry

    lax.fori_loop(0, before, clear, 0)
    lax.fori_loop(until, number, clear, 0)

    def one(n, arrived):
        i = order[n]
        m = plane_of(i)
        low = SPB * start[m] - first
        stop = jnp.minimum(low + window, bands)
        needed = lax.div(stop - 1, jnp.int32(window)) + 1
        if ready is not None:
            ready(arrived, needed)
        whole = jnp.logical_and(low >= 0, low + window <= bands)

        def term(band, weight, r):
            return weight * cube[band, r : r + ROWS, :].astype(jnp.float32)

        @pl.when(whole)
        def _():
            for r in range(0, lines, ROWS):
                total = term(low, weights[m, 0], r)
                for j in range(1, window):
                    total = total + term(low + j, weights[m, j], r)
                folded[i, r : r + ROWS, :] = total

        @pl.when(jnp.logical_not(whole))
        def _():
            begin = jnp.maximum(low, 0)
            for r in range(0, lines, ROWS):

                def some(t, total):
                    for k in range(group):
                        band = begin + t * group + k
                        total = total + term(band, weights[m, band - low], r)
                    return total

                folded[i, r : r + ROWS, :] = lax.fori_loop(
                    0,
                    lax.div(stop - begin, jnp.int32(group)),
                    some,
                    jnp.zeros((ROWS, cols), jnp.float32),
                )

        return jnp.maximum(arrived, needed)

    return lax.fori_loop(before, until, one, jnp.int32(0))


def across(value, table):
    planes, lines, cols = value.shape
    both = jnp.concatenate(split(value.reshape(planes * lines, cols)), axis=1)
    made = jnp.dot(both, table, preferred_element_type=jnp.float32)
    return made.reshape(planes, lines, cols)


def spread_out(made, out):
    half = made.shape[2] // 2
    for i in range(made.shape[0]):
        out[2 * i] = made[i, :, :half]
        out[2 * i + 1] = made[i, :, half:]


def fold_other(
    start_in,
    offsets_in,
    values_in,
    blocks_in,
    along_offsets_in,
    along_blocks_in,
    cube_in,
    send,
    middle,
    cube,
    wide,
    table,
    picked,
    start,
    offsets,
    values,
    weights,
    blocks,
    along_offsets,
    along_blocks,
    folded,
    order,
    small,
    large,
):
    bands, lines, cols = cube.shape
    count, window = values.shape
    half = cols // 2
    planes, odd, units = ownership(count)
    me = lax.axis_index("band")
    pairs = (
        (start_in, start),
        (values_in, values),
        (offsets_in, offsets),
        (blocks_in, blocks),
        (along_offsets_in, along_offsets),
        (along_blocks_in, along_blocks),
    )
    copies = [pltpu.make_async_copy(a, b, small.at[i]) for i, (a, b) in enumerate(pairs)]
    chunks = -(-bands // window)
    last = bands - (chunks - 1) * window

    def arrive(q, size):
        at = pl.ds(q * window, size)
        return pltpu.make_async_copy(cube_in.at[at], cube.at[at], large.at[q])

    for copy in copies:
        copy.start()
    for q in range(chunks):
        arrive(q, window if q < chunks - 1 else last).start()
    copies[1].wait()
    wide[...] = values[...].astype(jnp.float32)
    spread = pltpu.make_async_copy(wide, weights, small.at[len(pairs)])
    spread.start()
    for copy in copies[:1] + copies[2:]:
        copy.wait()
    for r in range(2):
        for c in range(2):
            block = blocks[which(offsets, jnp.int32(r - c))].astype(jnp.float32).T
            for top in (0, cols):
                at = slice(top + r * half, top + (r + 1) * half)
                table[at, c * half : (c + 1) * half] = block.astype(jnp.bfloat16)
    step = side_step()
    for i, shift in enumerate((jnp.int32(0), step, -step)):
        picked[i] = along_blocks[which(along_offsets, shift)]
    spread.wait()

    def one(q, carry):
        pl.when(q < chunks - 1)(lambda: arrive(q, window).wait())
        pl.when(q == chunks - 1)(lambda: arrive(chunks - 1, last).wait())
        return carry

    def ready(a, b):
        lax.fori_loop(a, b, one, 0)

    base = (1 - me) * (planes + odd)

    def plane_of(i):
        return jnp.where(i == planes, planes, base + i) if odd else base + i

    arrived = sum_windows(planes + odd, plane_of, start, weights, cube, folded, order, ready)
    ready(arrived, chunks)
    made = across(folded[...], table[...])
    spread_out(made[:planes], send)
    if odd:
        left, right = made[planes, :, :half], made[planes, :, half:]
        middle[0] = jnp.where(me == 0, left, right)
        send[units - 1] = jnp.where(me == 0, right, left)


def fold_own(start_in, wide, cube, table, middle, keep, start, weights, folded, order, sems):
    planes, odd, units = ownership(wide.shape[0])
    copies = [
        pltpu.make_async_copy(start_in, start, sems.at[0]),
        pltpu.make_async_copy(wide, weights, sems.at[1]),
    ]
    for copy in copies:
        copy.start()
    for copy in copies:
        copy.wait()
    base = lax.axis_index("band") * (planes + odd)
    sum_windows(planes, lambda i: base + i, start, weights, cube, folded, order)
    spread_out(across(folded[...], table[...]), keep)
    if odd:
        keep[units - 1] = middle[0]


def coded_rows(count, lines):
    return count * lines + -(-count // 16) * 16


def encode(source, span, message):
    _, lines, half = source.shape
    units = span[1] - span[0]
    largest = jnp.max(jnp.abs(source[span[0] : span[1]]), axis=1)
    level = jnp.ceil(jnp.log2(jnp.maximum(largest, 1e-30)) * STEPS)
    factor = PEAK * jnp.exp2(level * (-1.0 / STEPS))
    for m in range(units):
        coded = jnp.floor(source[span[0] + m] * factor[m : m + 1, :] + 0.5).astype(jnp.int32)
        message[m * lines : (m + 1) * lines, :] = coded.astype(jnp.int16)
    spare = message.shape[0] - units * lines - units
    level = jnp.concatenate([level, jnp.zeros((spare, half), jnp.float32)], axis=0)
    message[units * lines :, :] = level.astype(jnp.int32).astype(jnp.int16)


def decode(message, span, lines, valid=True):
    units = span[1] - span[0]
    level = message[units * lines :, :].astype(jnp.int32).astype(jnp.float32)
    scale = jnp.where(valid, jnp.exp2(level * (1.0 / STEPS)) * (1.0 / PEAK), 0.0)

    def plane(m):
        coded = message[m * lines : (m + 1) * lines, :].astype(jnp.int32).astype(jnp.float32)
        return coded * scale[m : m + 1, :]

    return plane


def blurred(filters, count, plane, put):
    wide = jnp.concatenate([filters, filters], axis=1)
    for m in range(0, count, 2):
        parts = [split(plane(n)) for n in range(m, min(m + 2, count))]
        high = jnp.concatenate([p[0] for p in parts], axis=1)
        low = jnp.concatenate([p[1] for p in parts], axis=1)
        made = jnp.dot(
            wide, jnp.concatenate([high, low], axis=0), preferred_element_type=jnp.float32
        )
        half = made.shape[1] // len(parts)
        for i in range(len(parts)):
            put(m + i, made[:, i * half : (i + 1) * half])


def side_step():
    return jnp.where(lax.axis_index("line") % 2 == 0, jnp.int32(1), jnp.int32(-1))


def outside(*lines):
    return functools.reduce(jnp.logical_or, [lax.axis_index("line") == i for i in lines])


def by_core(zero, one):
    me = lax.axis_index("band")
    pl.when(me == 0)(zero)
    pl.when(me != 0)(one)


def share(spans, picked, keep, other, total, *rest):
    messages, product = rest[:-1], rest[-1]
    total[...] = keep[...] + other[...]

    def coding(source):
        for span, message in zip(spans, messages):
            encode(source, span, message)

    def summing():
        def put(m, value):
            product[m] = value

        blurred(picked[1], total.shape[0], lambda m: total[m], put)
        coding(product)

    by_core(lambda: coding(total), summing)


def centre(picked, total, other_total, base, other_base, term):
    units = total.shape[0]

    def into(out):
        def put(m, value):
            out[m] = value

        return put

    blurred(picked[0], units, lambda m: total[m], into(base))
    blurred(picked[0], units, lambda m: other_total[m], into(other_base))
    pl.when(lax.axis_index("band") != 0)(
        lambda: blurred(picked[2], units, lambda m: total[m], into(term))
    )


def relay(span, term, received, message, total):
    def forward():
        message[...] = received[...]

    def add():
        missing = outside(1, lax.axis_size("line") - 2)
        plane = decode(received, span, term.shape[1], jnp.logical_not(missing))
        for m in range(*span):
            total[m] = term[m] + plane(m - span[0])
        encode(total, span, message)

    by_core(forward, add)


def beside(span, picked, near, product):
    units, lines, _ = product.shape

    def put(m, value):
        product[m] = value

    plane = decode(near, span, lines)
    pl.when(lax.axis_index("band") == 0)(lambda: blurred(picked[1], units, plane, put))


def settle(span, picked, product, received, message, total):
    units, lines, _ = product.shape

    def put(m, value):
        total[m] = product[m] + value

    def add():
        missing = outside(0, lax.axis_size("line") - 1)
        plane = decode(received, span, lines, jnp.logical_not(missing))
        blurred(picked[2], units, plane, put)
        encode(total, (0, units), message)

    def forward():
        message[...] = received[...]

    by_core(add, forward)


def arccos(x):
    size = jnp.abs(x)
    big = size > 0.5
    z = jnp.where(big, 0.5 * (1.0 - size), size * size)
    root = jnp.where(big, jnp.sqrt(z), size)
    poly = 4.2163199048e-2
    for term in (2.4181311049e-2, 4.5470025998e-2, 7.4953002686e-2, 1.6666752422e-1):
        poly = poly * z + term
    arcsin = poly * z * root + root
    pi = 3.14159265358979
    inner = jnp.where(x < 0, 0.5 * pi + arcsin, 0.5 * pi - arcsin)
    outer = jnp.where(x < 0, pi - 2.0 * arcsin, 2.0 * arcsin)
    return jnp.where(big, outer, inner)


def finish(second, spans, observed, base, *rest):
    messages, rest = rest[: len(spans)], rest[len(spans) :]
    if second:
        sums, _, image, angles, angle, value, sems = rest
    else:
        image, sums, value, sems = rest
    units, lines, half = base.shape
    count = observed.shape[0]

    def work(core):
        places = [(m, slice(c * half, (c + 1) * half)) for m, c in units_of(core, count)]
        copies = [
            pltpu.make_async_copy(value.at[n], image.at[m, :, at], sems.at[n])
            for n, (m, at) in enumerate(places)
        ]
        for span, message in zip(spans, messages):
            plane = decode(message, span, lines)
            for n in range(*span):
                value[n] = base[n] + plane(n - span[0])
                copies[n].start()
        for c in range(2):
            at = slice(c * half, (c + 1) * half)
            inner = jnp.zeros((lines, half), jnp.float32)
            left = jnp.zeros((lines, half), jnp.float32)
            for n, (m, where) in enumerate(places):
                if where == at:
                    inner = inner + value[n] * observed[m, :, at].astype(jnp.float32)
                    left = left + value[n] * value[n]
            if second:
                bound = jnp.sqrt(left + sums[1, :, at]) * sums[2, :, at]
                ratio = (inner + sums[0, :, at]) / jnp.maximum(bound, 1.0)
                angle[:, at] = arccos(jnp.clip(ratio, -1.0, 1.0))
            else:
                right = jnp.zeros((lines, half), jnp.float32)
                for m in range(count):
                    seen = observed[m, :, at].astype(jnp.float32)
                    right = right + seen * seen
                sums[0, :, at] = inner
                sums[1, :, at] = left
                sums[2, :, at] = jnp.sqrt(right)
        if second:
            copies.append(pltpu.make_async_copy(angle, angles, sems.at[units]))
            copies[-1].start()
        for copy in copies:
            copy.wait()

    if second:
        by_core(lambda: work(1), lambda: work(0))
    else:
        by_core(lambda: work(0), lambda: work(1))


def on_device(
    cube,
    observed,
    along_kernels,
    along_offsets,
    across_kernels,
    across_offsets,
    resp_start,
    resp_values,
):
    f32, i16 = jnp.float32, jnp.int16
    size = lax.axis_size("line")
    bands, lines, cols = cube.shape
    count = resp_values.shape[0]
    half = cols // 2
    _, _, units = ownership(count)
    shape = jax.ShapeDtypeStruct
    swap = [(0, 1), (1, 0)]
    partner = [(i, i ^ 1) for i in range(size)]
    even_up = [(i, (i + 2 - 4 * (i % 2)) % size) for i in range(size)]
    odd_up = [(j, i) for i, j in even_up]

    def cores(zero, one):
        return [(2 * a, 2 * b) for a, b in zero] + [(2 * a + 1, 2 * b + 1) for a, b in one]

    part = shape((units, lines, half), f32)
    spans = [(0, (units + 1) // 2), ((units + 1) // 2, units)]
    coded = [shape((coded_rows(b - a, lines), half), i16) for a, b in spans]

    inputs = (
        resp_start,
        across_offsets,
        resp_values,
        across_kernels,
        along_offsets,
        along_kernels,
        cube,
    )
    inputs = [pltpu.with_memory_space_constraint(x, pltpu.HBM) for x in inputs]
    planes, odd, _ = ownership(count)
    wide = shape(resp_values.shape, f32)
    table = shape((2 * cols, cols), across_kernels.dtype)
    send, middle, local, wide, table, picked = call(
        fold_other,
        inputs,
        [HBM] * len(inputs),
        [part, shape((1, lines, half), f32), cube, wide, table, along_kernels],
        scratch=[
            pltpu.SMEM(resp_start.shape, jnp.int32),
            pltpu.SMEM(across_offsets.shape, jnp.int32),
            pltpu.VMEM(resp_values.shape, resp_values.dtype),
            pltpu.SMEM(resp_values.shape, f32),
            pltpu.VMEM(across_kernels.shape, across_kernels.dtype),
            pltpu.SMEM(along_offsets.shape, jnp.int32),
            pltpu.VMEM(along_kernels.shape, along_kernels.dtype),
            pltpu.VMEM((planes + odd, lines, cols), f32),
            pltpu.SMEM((count,), jnp.int32),
            pltpu.SemaphoreType.DMA((len(inputs),)),
            pltpu.SemaphoreType.DMA((-(-bands // resp_values.shape[1]),)),
        ],
    )
    (keep,) = call(
        fold_own,
        (inputs[0], wide, local, table, middle),
        [HBM] + [VMEM] * 4,
        [part],
        scratch=[
            pltpu.SMEM(resp_start.shape, jnp.int32),
            pltpu.SMEM(resp_values.shape, f32),
            pltpu.VMEM((planes, lines, cols), f32),
            pltpu.SMEM((count,), jnp.int32),
            pltpu.SemaphoreType.DMA((2,)),
        ],
    )
    work = [pltpu.VMEM(part.shape, f32)]
    other = lax.ppermute(send, "band", swap)
    total, *sent = call(
        functools.partial(share, spans),
        (picked, keep, other),
        [VMEM] * 3,
        [part, *coded],
        scratch=work,
    )
    near = [lax.ppermute(x, ("line", "band"), cores(partner, odd_up)) for x in sent]
    other_total = lax.ppermute(total, "band", swap)
    base, other_base, term = call(
        centre, (picked, total, other_total), [VMEM] * 3, [part] * 3
    )
    far, product = [], []
    for i, span in enumerate(spans):
        (message,) = call(
            functools.partial(relay, span), (term, near[i]), [VMEM] * 2, [coded[i]], scratch=work
        )
        message, near[i] = lax.optimization_barrier((message, near[i]))
        far.append(lax.ppermute(message, ("line", "band"), cores(even_up, partner)))
        planes = shape((span[1] - span[0], lines, half), f32)
        product += call(
            functools.partial(beside, span),
            (picked, near[i]),
            [VMEM] * 2,
            [planes],
        )
    messages, others = [], []
    for i, span in enumerate(spans):
        planes = product[i].shape
        messages += call(
            functools.partial(settle, span),
            (picked, product[i], far[i]),
            [VMEM] * 3,
            [coded[i]],
            scratch=[pltpu.VMEM(planes, f32)],
        )
        others.append(lax.ppermute(messages[i], "band", swap))
    image = shape((count, lines, cols), f32)
    some = 2 + len(spans)
    image, sums = call(
        functools.partial(finish, False, spans),
        (observed, base, *messages),
        [VMEM] * some,
        [image, shape((3, lines, cols), f32)],
        scratch=work + [pltpu.SemaphoreType.DMA((units,))],
        out_specs=[HBM, VMEM],
    )
    image, angles = call(
        functools.partial(finish, True, spans),
        (observed, other_base, *others, sums, image),
        [VMEM] * (some + 1) + [HBM],
        [image, shape((lines, cols), f32)],
        scratch=[pltpu.VMEM((lines, cols), f32), *work, pltpu.SemaphoreType.DMA((units + 1,))],
        out_specs=[HBM] * 2,
        aliases={some + 1: 0},
    )
    return image, angles


def solution(mesh):
    placed = (
        P("band", ("slab", "line"), None),
        P(None, ("slab", "line"), None),
        P(),
        P(),
        P(),
        P(),
        P(),
        P(),
    )
    return jax.shard_map(
        on_device,
        mesh=mesh,
        in_specs=placed,
        out_specs=(P(None, ("slab", "line"), None), P(("slab", "line"), None)),
        check_vma=False,
    )
```

```python
import functools
import math

import jax
import jax.numpy as jnp
from jax import lax
from jax.experimental import pallas as pl
from jax.experimental.pallas import tpu as pltpu
from jax.sharding import PartitionSpec as P

BLK = 128
SPB = 10
STEPS = 16.0
PEAK = 32000.0


def which(offsets, shift):
    return sum(
        jnp.where(offsets[k] == shift, jnp.int32(k), jnp.int32(0)) for k in range(offsets.shape[0])
    )


def split(value):
    high = value.astype(jnp.bfloat16)
    low = (value - high.astype(jnp.float32)).astype(jnp.bfloat16)
    return high, low


SMEM = pl.BlockSpec(memory_space=pltpu.SMEM)
VMEM = pl.BlockSpec(memory_space=pltpu.VMEM)
HBM = pl.BlockSpec(memory_space=pltpu.HBM)
ROWS = 64
CHUNKS = 3


def call(kernel, inputs, specs, outs, scratch=(), out_specs=None, aliases=None):
    return pl.pallas_call(
        kernel,
        in_specs=specs,
        out_specs=out_specs or [VMEM] * len(outs),
        out_shape=[jax.ShapeDtypeStruct(x.shape, x.dtype) for x in outs],
        scratch_shapes=scratch,
        input_output_aliases=aliases or {},
        compiler_params=pltpu.CompilerParams(vmem_limit_bytes=32 * 2**20),
        cost_estimate=pl.CostEstimate(flops=0, bytes_accessed=0, transcendentals=0),
        name=(kernel.func if isinstance(kernel, functools.partial) else kernel).__name__,
    )(*inputs)


def ownership(count):
    pairs = count // 2
    return pairs, count % 2, 2 * pairs + count % 2


def units_of(core, count):
    pairs, odd, _ = ownership(count)
    first = core * (pairs + odd)
    return [(first + i, c) for i in range(pairs) for c in range(2)] + [(pairs, core)] * odd


def sum_windows(number, plane_of, start, weights, cube, folded, order, ready=None):
    bands, lines, cols = cube.shape
    window = weights.shape[1]
    group = math.gcd(SPB, bands)
    first = bands * lax.axis_index("band")
    places = [SPB * start[plane_of(i)] - first for i in range(number)]
    ranks = [jnp.int32(0)] * number
    for m in range(number):
        for n in range(m + 1, number):
            later = (places[n] < places[m]).astype(jnp.int32)
            ranks[m] = ranks[m] + later
            ranks[n] = ranks[n] + (1 - later)
    before = jnp.int32(0)
    until = jnp.int32(0)
    for m in range(number):
        order[ranks[m]] = jnp.int32(m)
        before = before + (places[m] <= -window).astype(jnp.int32)
        until = until + (places[m] < bands).astype(jnp.int32)

    def clear(n, carry):
        folded[order[n]] = jnp.zeros((lines, cols), jnp.float32)
        return carry

    lax.fori_loop(0, before, clear, 0)
    lax.fori_loop(until, number, clear, 0)

    def one(n, arrived):
        i = order[n]
        m = plane_of(i)
        low = SPB * start[m] - first
        stop = jnp.minimum(low + window, bands)
        needed = lax.div(stop - 1, jnp.int32(window)) + 1
        if ready is not None:
            ready(arrived, needed)
        whole = jnp.logical_and(low >= 0, low + window <= bands)

        def term(band, weight, r):
            return weight * cube[band, r : r + ROWS, :].astype(jnp.float32)

        @pl.when(whole)
        def _():
            for r in range(0, lines, ROWS):
                total = term(low, weights[m, 0], r)
                for j in range(1, window):
                    total = total + term(low + j, weights[m, j], r)
                folded[i, r : r + ROWS, :] = total

        @pl.when(jnp.logical_not(whole))
        def _():
            begin = jnp.maximum(low, 0)
            for r in range(0, lines, ROWS):

                def some(t, total):
                    for k in range(group):
                        band = begin + t * group + k
                        total = total + term(band, weights[m, band - low], r)
                    return total

                folded[i, r : r + ROWS, :] = lax.fori_loop(
                    0,
                    lax.div(stop - begin, jnp.int32(group)),
                    some,
                    jnp.zeros((ROWS, cols), jnp.float32),
                )

        return jnp.maximum(arrived, needed)

    return lax.fori_loop(before, until, one, jnp.int32(0))


def across(value, table):
    planes, lines, cols = value.shape
    both = jnp.concatenate(split(value.reshape(planes * lines, cols)), axis=1)
    made = jnp.dot(both, table, preferred_element_type=jnp.float32)
    return made.reshape(planes, lines, cols)


def spread_out(made, out):
    half = made.shape[2] // 2
    for i in range(made.shape[0]):
        out[2 * i] = made[i, :, :half]
        out[2 * i + 1] = made[i, :, half:]


def fold_other(
    start_in,
    offsets_in,
    values_in,
    blocks_in,
    along_offsets_in,
    along_blocks_in,
    cube_in,
    send,
    middle,
    cube,
    wide,
    table,
    picked,
    start,
    offsets,
    values,
    weights,
    blocks,
    along_offsets,
    along_blocks,
    folded,
    order,
    small,
    large,
):
    bands, lines, cols = cube.shape
    count, window = values.shape
    half = cols // 2
    planes, odd, units = ownership(count)
    me = lax.axis_index("band")
    pairs = (
        (start_in, start),
        (values_in, values),
        (offsets_in, offsets),
        (blocks_in, blocks),
        (along_offsets_in, along_offsets),
        (along_blocks_in, along_blocks),
    )
    copies = [pltpu.make_async_copy(a, b, small.at[i]) for i, (a, b) in enumerate(pairs)]
    chunks = -(-bands // window)
    last = bands - (chunks - 1) * window

    def arrive(q, size):
        at = pl.ds(q * window, size)
        return pltpu.make_async_copy(cube_in.at[at], cube.at[at], large.at[q])

    for copy in copies:
        copy.start()
    for q in range(chunks):
        arrive(q, window if q < chunks - 1 else last).start()
    copies[1].wait()
    wide[...] = values[...].astype(jnp.float32)
    spread = pltpu.make_async_copy(wide, weights, small.at[len(pairs)])
    spread.start()
    for copy in copies[:1] + copies[2:]:
        copy.wait()
    for r in range(2):
        for c in range(2):
            block = blocks[which(offsets, jnp.int32(r - c))].astype(jnp.float32).T
            for top in (0, cols):
                at = slice(top + r * half, top + (r + 1) * half)
                table[at, c * half : (c + 1) * half] = block.astype(jnp.bfloat16)
    step = side_step()
    for i, shift in enumerate((jnp.int32(0), step, -step)):
        picked[i] = along_blocks[which(along_offsets, shift)]
    spread.wait()

    def one(q, carry):
        pl.when(q < chunks - 1)(lambda: arrive(q, window).wait())
        pl.when(q == chunks - 1)(lambda: arrive(chunks - 1, last).wait())
        return carry

    def ready(a, b):
        lax.fori_loop(a, b, one, 0)

    base = (1 - me) * (planes + odd)

    def plane_of(i):
        return jnp.where(i == planes, planes, base + i) if odd else base + i

    arrived = sum_windows(planes + odd, plane_of, start, weights, cube, folded, order, ready)
    ready(arrived, chunks)
    made = across(folded[...], table[...])
    spread_out(made[:planes], send)
    if odd:
        left, right = made[planes, :, :half], made[planes, :, half:]
        middle[0] = jnp.where(me == 0, left, right)
        send[units - 1] = jnp.where(me == 0, right, left)


def fold_own(start_in, wide, cube, table, middle, keep, start, weights, folded, order, sems):
    planes, odd, units = ownership(wide.shape[0])
    copies = [
        pltpu.make_async_copy(start_in, start, sems.at[0]),
        pltpu.make_async_copy(wide, weights, sems.at[1]),
    ]
    for copy in copies:
        copy.start()
    for copy in copies:
        copy.wait()
    base = lax.axis_index("band") * (planes + odd)
    sum_windows(planes, lambda i: base + i, start, weights, cube, folded, order)
    spread_out(across(folded[...], table[...]), keep)
    if odd:
        keep[units - 1] = middle[0]


def coded_rows(count, lines):
    return count * lines + -(-count // 16) * 16


def encode(source, span, message):
    _, lines, half = source.shape
    units = span[1] - span[0]
    largest = jnp.max(jnp.abs(source[span[0] : span[1]]), axis=1)
    level = jnp.ceil(jnp.log2(jnp.maximum(largest, 1e-30)) * STEPS)
    factor = PEAK * jnp.exp2(level * (-1.0 / STEPS))
    for m in range(units):
        coded = jnp.floor(source[span[0] + m] * factor[m : m + 1, :] + 0.5).astype(jnp.int32)
        message[m * lines : (m + 1) * lines, :] = coded.astype(jnp.int16)
    spare = message.shape[0] - units * lines - units
    level = jnp.concatenate([level, jnp.zeros((spare, half), jnp.float32)], axis=0)
    message[units * lines :, :] = level.astype(jnp.int32).astype(jnp.int16)


def decode(message, span, lines, valid=True):
    units = span[1] - span[0]
    level = message[units * lines :, :].astype(jnp.int32).astype(jnp.float32)
    scale = jnp.where(valid, jnp.exp2(level * (1.0 / STEPS)) * (1.0 / PEAK), 0.0)

    def plane(m):
        coded = message[m * lines : (m + 1) * lines, :].astype(jnp.int32).astype(jnp.float32)
        return coded * scale[m : m + 1, :]

    return plane


def blurred(filters, count, plane, put):
    wide = jnp.concatenate([filters, filters], axis=1)
    for m in range(0, count, 2):
        parts = [split(plane(n)) for n in range(m, min(m + 2, count))]
        high = jnp.concatenate([p[0] for p in parts], axis=1)
        low = jnp.concatenate([p[1] for p in parts], axis=1)
        made = jnp.dot(
            wide, jnp.concatenate([high, low], axis=0), preferred_element_type=jnp.float32
        )
        half = made.shape[1] // len(parts)
        for i in range(len(parts)):
            put(m + i, made[:, i * half : (i + 1) * half])


def side_step():
    return jnp.where(lax.axis_index("line") % 2 == 0, jnp.int32(1), jnp.int32(-1))


def outside(*lines):
    return functools.reduce(jnp.logical_or, [lax.axis_index("line") == i for i in lines])


def by_core(zero, one):
    me = lax.axis_index("band")
    pl.when(me == 0)(zero)
    pl.when(me != 0)(one)


def share(spans, picked, keep, other, total, *rest):
    messages, product = rest[:-1], rest[-1]
    total[...] = keep[...] + other[...]

    def coding(source):
        for span, message in zip(spans, messages):
            encode(source, span, message)

    def summing():
        def put(m, value):
            product[m] = value

        blurred(picked[1], total.shape[0], lambda m: total[m], put)
        coding(product)

    by_core(lambda: coding(total), summing)


def centre(picked, total, other_total, base, other_base, term):
    units = total.shape[0]

    def into(out):
        def put(m, value):
            out[m] = value

        return put

    blurred(picked[0], units, lambda m: total[m], into(base))
    blurred(picked[0], units, lambda m: other_total[m], into(other_base))
    pl.when(lax.axis_index("band") != 0)(
        lambda: blurred(picked[2], units, lambda m: total[m], into(term))
    )


def relay(span, term, received, message, total):
    def forward():
        message[...] = received[...]

    def add():
        missing = outside(1, lax.axis_size("line") - 2)
        plane = decode(received, span, term.shape[1], jnp.logical_not(missing))
        for m in range(*span):
            total[m] = term[m] + plane(m - span[0])
        encode(total, span, message)

    by_core(forward, add)


def beside(span, picked, near, product):
    units, lines, _ = product.shape

    def put(m, value):
        product[m] = value

    plane = decode(near, span, lines)
    pl.when(lax.axis_index("band") == 0)(lambda: blurred(picked[1], units, plane, put))


def settle(span, picked, product, received, message, total):
    units, lines, _ = product.shape

    def put(m, value):
        total[m] = product[m] + value

    def add():
        missing = outside(0, lax.axis_size("line") - 1)
        plane = decode(received, span, lines, jnp.logical_not(missing))
        blurred(picked[2], units, plane, put)
        encode(total, (0, units), message)

    def forward():
        message[...] = received[...]

    by_core(add, forward)


def arccos(x):
    size = jnp.abs(x)
    big = size > 0.5
    z = jnp.where(big, 0.5 * (1.0 - size), size * size)
    root = jnp.where(big, jnp.sqrt(z), size)
    poly = 4.2163199048e-2
    for term in (2.4181311049e-2, 4.5470025998e-2, 7.4953002686e-2, 1.6666752422e-1):
        poly = poly * z + term
    arcsin = poly * z * root + root
    pi = 3.14159265358979
    inner = jnp.where(x < 0, 0.5 * pi + arcsin, 0.5 * pi - arcsin)
    outer = jnp.where(x < 0, pi - 2.0 * arcsin, 2.0 * arcsin)
    return jnp.where(big, outer, inner)


def finish_units(core, parts, observed, base, value, image, sem, sums):
    _, lines, half = base.shape
    copies = []
    for span, message in parts:
        plane = decode(message, span, lines)
        for n in range(*span):
            m, c = units_of(core, observed.shape[0])[n]
            at = slice(c * half, (c + 1) * half)
            made = base[n] + plane(n - span[0])
            value[n] = made
            copies.append(pltpu.make_async_copy(value.at[n], image.at[m, :, at], sem(n)))
            copies[-1].start()
            seen = observed[m, :, at].astype(jnp.float32)
            sums[c] = (sums[c][0] + made * seen, sums[c][1] + made * made)
    return copies


def finish_most(spans, observed, base, other_base, *rest):
    chunks = len(spans)
    messages, others, rest = rest[:chunks], rest[chunks : 2 * chunks - 1], rest[2 * chunks - 1 :]
    image, own, theirs, value, other_value, sems = rest
    units, lines, half = base.shape
    zero = jnp.zeros((lines, half), jnp.float32)

    def work(core):
        sums, other_sums = [(zero, zero)] * 2, [(zero, zero)] * 2
        parts = list(zip(spans, messages))
        copies = finish_units(
            core, parts, observed, base, value, image, lambda n: sems.at[n], sums
        )
        parts = list(zip(spans[:-1], others))
        copies += finish_units(
            1 - core,
            parts,
            observed,
            other_base,
            other_value,
            image,
            lambda n: sems.at[units + n],
            other_sums,
        )
        for c in range(2):
            at = slice(c * half, (c + 1) * half)
            right = zero
            for m in range(observed.shape[0]):
                seen = observed[m, :, at].astype(jnp.float32)
                right = right + seen * seen
            own[0, :, at], own[1, :, at] = sums[c]
            own[2, :, at] = jnp.sqrt(right)
            theirs[0, :, at], theirs[1, :, at] = other_sums[c]
        for copy in copies:
            copy.wait()

    by_core(lambda: work(0), lambda: work(1))


def finish_last(span, observed, other_base, message, own, theirs, _, *rest):
    image, angles, angle, value, sems = rest
    units, lines, half = other_base.shape

    def work(core):
        columns = [slice(c * half, (c + 1) * half) for c in range(2)]
        sums = [(theirs[0, :, at], theirs[1, :, at]) for at in columns]
        copies = finish_units(
            core,
            [(span, message)],
            observed,
            other_base,
            value,
            image,
            lambda n: sems.at[n],
            sums,
        )
        for (inner, left), at in zip(sums, columns):
            bound = jnp.sqrt(left + own[1, :, at]) * own[2, :, at]
            ratio = (inner + own[0, :, at]) / jnp.maximum(bound, 1.0)
            angle[:, at] = arccos(jnp.clip(ratio, -1.0, 1.0))
        copies.append(pltpu.make_async_copy(angle, angles, sems.at[units]))
        copies[-1].start()
        for copy in copies:
            copy.wait()

    by_core(lambda: work(1), lambda: work(0))


def on_device(
    cube,
    observed,
    along_kernels,
    along_offsets,
    across_kernels,
    across_offsets,
    resp_start,
    resp_values,
):
    f32, i16 = jnp.float32, jnp.int16
    size = lax.axis_size("line")
    bands, lines, cols = cube.shape
    count = resp_values.shape[0]
    half = cols // 2
    _, _, units = ownership(count)
    shape = jax.ShapeDtypeStruct
    swap = [(0, 1), (1, 0)]
    partner = [(i, i ^ 1) for i in range(size)]
    even_up = [(i, (i + 2 - 4 * (i % 2)) % size) for i in range(size)]
    odd_up = [(j, i) for i, j in even_up]

    def cores(zero, one):
        return [(2 * a, 2 * b) for a, b in zero] + [(2 * a + 1, 2 * b + 1) for a, b in one]

    part = shape((units, lines, half), f32)
    edges = [-(-units * i // CHUNKS) for i in range(CHUNKS + 1)]
    spans = list(zip(edges[:-1], edges[1:]))
    coded = [shape((coded_rows(b - a, lines), half), i16) for a, b in spans]

    inputs = (
        resp_start,
        across_offsets,
        resp_values,
        across_kernels,
        along_offsets,
        along_kernels,
        cube,
    )
    inputs = [pltpu.with_memory_space_constraint(x, pltpu.HBM) for x in inputs]
    planes, odd, _ = ownership(count)
    wide = shape(resp_values.shape, f32)
    table = shape((2 * cols, cols), across_kernels.dtype)
    send, middle, local, wide, table, picked = call(
        fold_other,
        inputs,
        [HBM] * len(inputs),
        [part, shape((1, lines, half), f32), cube, wide, table, along_kernels],
        scratch=[
            pltpu.SMEM(resp_start.shape, jnp.int32),
            pltpu.SMEM(across_offsets.shape, jnp.int32),
            pltpu.VMEM(resp_values.shape, resp_values.dtype),
            pltpu.SMEM(resp_values.shape, f32),
            pltpu.VMEM(across_kernels.shape, across_kernels.dtype),
            pltpu.SMEM(along_offsets.shape, jnp.int32),
            pltpu.VMEM(along_kernels.shape, along_kernels.dtype),
            pltpu.VMEM((planes + odd, lines, cols), f32),
            pltpu.SMEM((count,), jnp.int32),
            pltpu.SemaphoreType.DMA((len(inputs),)),
            pltpu.SemaphoreType.DMA((-(-bands // resp_values.shape[1]),)),
        ],
    )
    (keep,) = call(
        fold_own,
        (inputs[0], wide, local, table, middle),
        [HBM] + [VMEM] * 4,
        [part],
        scratch=[
            pltpu.SMEM(resp_start.shape, jnp.int32),
            pltpu.SMEM(resp_values.shape, f32),
            pltpu.VMEM((planes, lines, cols), f32),
            pltpu.SMEM((count,), jnp.int32),
            pltpu.SemaphoreType.DMA((2,)),
        ],
    )
    work = [pltpu.VMEM(part.shape, f32)]
    other = lax.ppermute(send, "band", swap)
    total, *sent = call(
        functools.partial(share, spans),
        (picked, keep, other),
        [VMEM] * 3,
        [part, *coded],
        scratch=work,
    )
    near = [lax.ppermute(x, ("line", "band"), cores(partner, odd_up)) for x in sent]
    other_total = lax.ppermute(total, "band", swap)
    base, other_base, term = call(
        centre, (picked, total, other_total), [VMEM] * 3, [part] * 3
    )
    far, product = [], []
    for i, span in enumerate(spans):
        (message,) = call(
            functools.partial(relay, span), (term, near[i]), [VMEM] * 2, [coded[i]], scratch=work
        )
        message, near[i] = lax.optimization_barrier((message, near[i]))
        far.append(lax.ppermute(message, ("line", "band"), cores(even_up, partner)))
        planes = shape((span[1] - span[0], lines, half), f32)
        product += call(
            functools.partial(beside, span),
            (picked, near[i]),
            [VMEM] * 2,
            [planes],
        )
    messages, others = [], []
    for i, span in enumerate(spans):
        planes = product[i].shape
        messages += call(
            functools.partial(settle, span),
            (picked, product[i], far[i]),
            [VMEM] * 3,
            [coded[i]],
            scratch=[pltpu.VMEM(planes, f32)],
        )
        others.append(lax.ppermute(messages[i], "band", swap))
    image = shape((count, lines, cols), f32)
    three = shape((3, lines, cols), f32)
    inputs = [observed, base, other_base, *messages, *others[:-1]]
    image, own, theirs = call(
        functools.partial(finish_most, spans),
        inputs,
        [VMEM] * len(inputs),
        [image, three, three],
        scratch=work * 2 + [pltpu.SemaphoreType.DMA((2 * units,))],
        out_specs=[HBM, VMEM, VMEM],
    )
    image, angles = call(
        functools.partial(finish_last, spans[-1]),
        (observed, other_base, others[-1], own, theirs, image),
        [VMEM] * 5 + [HBM],
        [image, shape((lines, cols), f32)],
        scratch=[pltpu.VMEM((lines, cols), f32), *work, pltpu.SemaphoreType.DMA((units + 1,))],
        out_specs=[HBM] * 2,
        aliases={5: 0},
    )
    return image, angles


def solution(mesh):
    placed = (
        P("band", ("slab", "line"), None),
        P(None, ("slab", "line"), None),
        P(),
        P(),
        P(),
        P(),
        P(),
        P(),
    )
    return jax.shard_map(
        on_device,
        mesh=mesh,
        in_specs=placed,
        out_specs=(P(None, ("slab", "line"), None), P(("slab", "line"), None)),
        check_vma=False,
    )
```

```python
import functools
import math

import jax
import jax.numpy as jnp
from jax import lax
from jax.experimental import pallas as pl
from jax.experimental.pallas import tpu as pltpu
from jax.sharding import PartitionSpec as P

BLK = 128
SPB = 10
STEPS = 16.0
PEAK = 32000.0


def which(offsets, shift):
    return sum(
        jnp.where(offsets[k] == shift, jnp.int32(k), jnp.int32(0)) for k in range(offsets.shape[0])
    )


def split(value):
    high = value.astype(jnp.bfloat16)
    low = (value - high.astype(jnp.float32)).astype(jnp.bfloat16)
    return high, low


SMEM = pl.BlockSpec(memory_space=pltpu.SMEM)
VMEM = pl.BlockSpec(memory_space=pltpu.VMEM)
HBM = pl.BlockSpec(memory_space=pltpu.HBM)
ROWS = 64
CHUNKS = 3


def call(kernel, inputs, specs, outs, scratch=(), out_specs=None, aliases=None):
    return pl.pallas_call(
        kernel,
        in_specs=specs,
        out_specs=out_specs or [VMEM] * len(outs),
        out_shape=[jax.ShapeDtypeStruct(x.shape, x.dtype) for x in outs],
        scratch_shapes=scratch,
        input_output_aliases=aliases or {},
        compiler_params=pltpu.CompilerParams(vmem_limit_bytes=32 * 2**20),
        cost_estimate=pl.CostEstimate(flops=0, bytes_accessed=0, transcendentals=0),
        name=(kernel.func if isinstance(kernel, functools.partial) else kernel).__name__,
    )(*inputs)


def ownership(count):
    pairs = count // 2
    return pairs, count % 2, 2 * pairs + count % 2


def units_of(core, count):
    pairs, odd, _ = ownership(count)
    first = core * (pairs + odd)
    return [(first + i, c) for i in range(pairs) for c in range(2)] + [(pairs, core)] * odd


def sum_windows(number, plane_of, start, weights, cube, folded, order, ready=None):
    bands, lines, cols = cube.shape
    window = weights.shape[1]
    group = math.gcd(SPB, bands)
    first = bands * lax.axis_index("band")
    places = [SPB * start[plane_of(i)] - first for i in range(number)]
    ranks = [jnp.int32(0)] * number
    for m in range(number):
        for n in range(m + 1, number):
            later = (places[n] < places[m]).astype(jnp.int32)
            ranks[m] = ranks[m] + later
            ranks[n] = ranks[n] + (1 - later)
    before = jnp.int32(0)
    until = jnp.int32(0)
    for m in range(number):
        order[ranks[m]] = jnp.int32(m)
        before = before + (places[m] <= -window).astype(jnp.int32)
        until = until + (places[m] < bands).astype(jnp.int32)

    def clear(n, carry):
        folded[order[n]] = jnp.zeros((lines, cols), jnp.float32)
        return carry

    lax.fori_loop(0, before, clear, 0)
    lax.fori_loop(until, number, clear, 0)

    def one(n, arrived):
        i = order[n]
        m = plane_of(i)
        low = SPB * start[m] - first
        stop = jnp.minimum(low + window, bands)
        needed = lax.div(stop - 1, jnp.int32(window)) + 1
        if ready is not None:
            ready(arrived, needed)
        whole = jnp.logical_and(low >= 0, low + window <= bands)

        def term(band, weight, r):
            return weight * cube[band, r : r + ROWS, :].astype(jnp.float32)

        @pl.when(whole)
        def _():
            for r in range(0, lines, ROWS):
                total = term(low, weights[m, 0], r)
                for j in range(1, window):
                    total = total + term(low + j, weights[m, j], r)
                folded[i, r : r + ROWS, :] = total

        @pl.when(jnp.logical_not(whole))
        def _():
            begin = jnp.maximum(low, 0)
            for r in range(0, lines, ROWS):

                def some(t, total):
                    for k in range(group):
                        band = begin + t * group + k
                        total = total + term(band, weights[m, band - low], r)
                    return total

                folded[i, r : r + ROWS, :] = lax.fori_loop(
                    0,
                    lax.div(stop - begin, jnp.int32(group)),
                    some,
                    jnp.zeros((ROWS, cols), jnp.float32),
                )

        return jnp.maximum(arrived, needed)

    return lax.fori_loop(before, until, one, jnp.int32(0))


def across(value, table):
    planes, lines, cols = value.shape
    both = jnp.concatenate(split(value.reshape(planes * lines, cols)), axis=1)
    made = jnp.dot(both, table, preferred_element_type=jnp.float32)
    return made.reshape(planes, lines, cols)


def spread_out(made, out):
    half = made.shape[2] // 2
    for i in range(made.shape[0]):
        out[2 * i] = made[i, :, :half]
        out[2 * i + 1] = made[i, :, half:]


def fold_other(
    start_in,
    offsets_in,
    values_in,
    blocks_in,
    along_offsets_in,
    along_blocks_in,
    cube_in,
    send,
    middle,
    cube,
    wide,
    table,
    picked,
    start,
    offsets,
    values,
    weights,
    blocks,
    along_offsets,
    along_blocks,
    folded,
    order,
    small,
    large,
):
    bands, lines, cols = cube.shape
    count, window = values.shape
    half = cols // 2
    planes, odd, units = ownership(count)
    me = lax.axis_index("band")
    pairs = (
        (start_in, start),
        (values_in, values),
        (offsets_in, offsets),
        (blocks_in, blocks),
        (along_offsets_in, along_offsets),
        (along_blocks_in, along_blocks),
    )
    copies = [pltpu.make_async_copy(a, b, small.at[i]) for i, (a, b) in enumerate(pairs)]
    chunks = -(-bands // window)
    last = bands - (chunks - 1) * window

    def arrive(q, size):
        at = pl.ds(q * window, size)
        return pltpu.make_async_copy(cube_in.at[at], cube.at[at], large.at[q])

    for copy in copies:
        copy.start()
    for q in range(chunks):
        arrive(q, window if q < chunks - 1 else last).start()
    copies[1].wait()
    wide[...] = values[...].astype(jnp.float32)
    spread = pltpu.make_async_copy(wide, weights, small.at[len(pairs)])
    spread.start()
    for copy in copies[:1] + copies[2:]:
        copy.wait()
    for r in range(2):
        for c in range(2):
            block = blocks[which(offsets, jnp.int32(r - c))].astype(jnp.float32).T
            for top in (0, cols):
                at = slice(top + r * half, top + (r + 1) * half)
                table[at, c * half : (c + 1) * half] = block.astype(jnp.bfloat16)
    step = side_step()
    for i, shift in enumerate((jnp.int32(0), step, -step)):
        picked[i] = along_blocks[which(along_offsets, shift)]
    spread.wait()

    def one(q, carry):
        pl.when(q < chunks - 1)(lambda: arrive(q, window).wait())
        pl.when(q == chunks - 1)(lambda: arrive(chunks - 1, last).wait())
        return carry

    def ready(a, b):
        lax.fori_loop(a, b, one, 0)

    base = (1 - me) * (planes + odd)

    def plane_of(i):
        return jnp.where(i == planes, planes, base + i) if odd else base + i

    arrived = sum_windows(planes + odd, plane_of, start, weights, cube, folded, order, ready)
    ready(arrived, chunks)
    made = across(folded[...], table[...])
    spread_out(made[:planes], send)
    if odd:
        left, right = made[planes, :, :half], made[planes, :, half:]
        middle[0] = jnp.where(me == 0, left, right)
        send[units - 1] = jnp.where(me == 0, right, left)


def fold_own(start_in, wide, cube, table, middle, keep, start, weights, folded, order, sems):
    planes, odd, units = ownership(wide.shape[0])
    copies = [
        pltpu.make_async_copy(start_in, start, sems.at[0]),
        pltpu.make_async_copy(wide, weights, sems.at[1]),
    ]
    for copy in copies:
        copy.start()
    for copy in copies:
        copy.wait()
    base = lax.axis_index("band") * (planes + odd)
    sum_windows(planes, lambda i: base + i, start, weights, cube, folded, order)
    spread_out(across(folded[...], table[...]), keep)
    if odd:
        keep[units - 1] = middle[0]


def coded_rows(count, lines):
    return count * lines + -(-count // 16) * 16


def encode(source, span, message):
    _, lines, half = source.shape
    units = span[1] - span[0]
    largest = jnp.max(jnp.abs(source[span[0] : span[1]]), axis=1)
    level = jnp.ceil(jnp.log2(jnp.maximum(largest, 1e-30)) * STEPS)
    factor = PEAK * jnp.exp2(level * (-1.0 / STEPS))
    for m in range(units):
        coded = jnp.floor(source[span[0] + m] * factor[m : m + 1, :] + 0.5).astype(jnp.int32)
        message[m * lines : (m + 1) * lines, :] = coded.astype(jnp.int16)
    spare = message.shape[0] - units * lines - units
    level = jnp.concatenate([level, jnp.zeros((spare, half), jnp.float32)], axis=0)
    message[units * lines :, :] = level.astype(jnp.int32).astype(jnp.int16)


def decode(message, span, lines, valid=True):
    units = span[1] - span[0]
    level = message[units * lines :, :].astype(jnp.int32).astype(jnp.float32)
    scale = jnp.where(valid, jnp.exp2(level * (1.0 / STEPS)) * (1.0 / PEAK), 0.0)

    def plane(m):
        coded = message[m * lines : (m + 1) * lines, :].astype(jnp.int32).astype(jnp.float32)
        return coded * scale[m : m + 1, :]

    return plane


def blurred(filters, count, plane, put):
    wide = jnp.concatenate([filters, filters], axis=1)
    for m in range(0, count, 2):
        parts = [split(plane(n)) for n in range(m, min(m + 2, count))]
        high = jnp.concatenate([p[0] for p in parts], axis=1)
        low = jnp.concatenate([p[1] for p in parts], axis=1)
        made = jnp.dot(
            wide, jnp.concatenate([high, low], axis=0), preferred_element_type=jnp.float32
        )
        half = made.shape[1] // len(parts)
        for i in range(len(parts)):
            put(m + i, made[:, i * half : (i + 1) * half])


def side_step():
    return jnp.where(lax.axis_index("line") % 2 == 0, jnp.int32(1), jnp.int32(-1))


def outside(*lines):
    return functools.reduce(jnp.logical_or, [lax.axis_index("line") == i for i in lines])


def by_core(zero, one):
    me = lax.axis_index("band")
    pl.when(me == 0)(zero)
    pl.when(me != 0)(one)


def share(spans, picked, keep, other, total, *rest):
    messages, product = rest[:-1], rest[-1]
    total[...] = keep[...] + other[...]

    def coding(source):
        for span, message in zip(spans, messages):
            encode(source, span, message)

    def summing():
        def put(m, value):
            product[m] = value

        blurred(picked[1], total.shape[0], lambda m: total[m], put)
        coding(product)

    by_core(lambda: coding(total), summing)


def centre(picked, total, other_total, base, other_base, term):
    units = total.shape[0]

    def into(out):
        def put(m, value):
            out[m] = value

        return put

    blurred(picked[0], units, lambda m: total[m], into(base))
    blurred(picked[0], units, lambda m: other_total[m], into(other_base))
    pl.when(lax.axis_index("band") != 0)(
        lambda: blurred(picked[2], units, lambda m: total[m], into(term))
    )


def relay(span, term, received, message, total):
    def forward():
        message[...] = received[...]

    def add():
        missing = outside(1, lax.axis_size("line") - 2)
        plane = decode(received, span, term.shape[1], jnp.logical_not(missing))
        for m in range(*span):
            total[m] = term[m] + plane(m - span[0])
        encode(total, span, message)

    by_core(forward, add)


def beside(span, picked, near, product):
    units, lines, _ = product.shape

    def put(m, value):
        product[m] = value

    plane = decode(near, span, lines)
    pl.when(lax.axis_index("band") == 0)(lambda: blurred(picked[1], units, plane, put))


def settle(span, picked, product, received, message, total):
    units, lines, _ = product.shape

    def put(m, value):
        total[m] = product[m] + value

    def add():
        missing = outside(0, lax.axis_size("line") - 1)
        plane = decode(received, span, lines, jnp.logical_not(missing))
        blurred(picked[2], units, plane, put)
        encode(total, (0, units), message)

    def forward():
        message[...] = received[...]

    by_core(add, forward)


def arccos(x):
    size = jnp.abs(x)
    big = size > 0.5
    z = jnp.where(big, 0.5 * (1.0 - size), size * size)
    root = jnp.where(big, jnp.sqrt(z), size)
    poly = 4.2163199048e-2
    for term in (2.4181311049e-2, 4.5470025998e-2, 7.4953002686e-2, 1.6666752422e-1):
        poly = poly * z + term
    arcsin = poly * z * root + root
    pi = 3.14159265358979
    inner = jnp.where(x < 0, 0.5 * pi + arcsin, 0.5 * pi - arcsin)
    outer = jnp.where(x < 0, pi - 2.0 * arcsin, 2.0 * arcsin)
    return jnp.where(big, outer, inner)


def finish_units(core, parts, observed, base, value, image, sem, sums):
    _, lines, half = base.shape
    copies = []
    for span, message in parts:
        plane = decode(message, span, lines)
        for n in range(*span):
            m, c = units_of(core, observed.shape[0])[n]
            at = slice(c * half, (c + 1) * half)
            made = base[n] + plane(n - span[0])
            value[n] = made
            copies.append(pltpu.make_async_copy(value.at[n], image.at[m, :, at], sem(n)))
            copies[-1].start()
            seen = observed[m, :, at].astype(jnp.float32)
            sums[c] = (sums[c][0] + made * seen, sums[c][1] + made * made)
    return copies


def finish_most(spans, observed, base, other_base, *rest):
    chunks = len(spans)
    messages, others, rest = rest[:chunks], rest[chunks : 2 * chunks - 1], rest[2 * chunks - 1 :]
    image, own, theirs, value, other_value, sems = rest
    units, lines, half = base.shape
    zero = jnp.zeros((lines, half), jnp.float32)

    def work(core):
        sums, other_sums = [(zero, zero)] * 2, [(zero, zero)] * 2
        parts = list(zip(spans, messages))
        copies = finish_units(
            core, parts, observed, base, value, image, lambda n: sems.at[n], sums
        )
        parts = list(zip(spans[:-1], others))
        copies += finish_units(
            1 - core,
            parts,
            observed,
            other_base,
            other_value,
            image,
            lambda n: sems.at[units + n],
            other_sums,
        )
        for c in range(2):
            at = slice(c * half, (c + 1) * half)
            right = zero
            for m in range(observed.shape[0]):
                seen = observed[m, :, at].astype(jnp.float32)
                right = right + seen * seen
            own[0, :, at], own[1, :, at] = sums[c]
            own[2, :, at] = jnp.sqrt(right)
            theirs[0, :, at], theirs[1, :, at] = other_sums[c]
        for copy in copies:
            copy.wait()

    by_core(lambda: work(0), lambda: work(1))


def finish_last(span, observed, other_base, message, own, theirs, _, *rest):
    image, angles, angle, value, sems = rest
    units, lines, half = other_base.shape

    def work(core):
        columns = [slice(c * half, (c + 1) * half) for c in range(2)]
        sums = [(theirs[0, :, at], theirs[1, :, at]) for at in columns]
        copies = finish_units(
            core,
            [(span, message)],
            observed,
            other_base,
            value,
            image,
            lambda n: sems.at[n],
            sums,
        )
        for (inner, left), at in zip(sums, columns):
            bound = jnp.sqrt(left + own[1, :, at]) * own[2, :, at]
            ratio = (inner + own[0, :, at]) / jnp.maximum(bound, 1.0)
            angle[:, at] = arccos(jnp.clip(ratio, -1.0, 1.0))
        copies.append(pltpu.make_async_copy(angle, angles, sems.at[units]))
        copies[-1].start()
        for copy in copies:
            copy.wait()

    by_core(lambda: work(1), lambda: work(0))


def on_device(
    cube,
    observed,
    along_kernels,
    along_offsets,
    across_kernels,
    across_offsets,
    resp_start,
    resp_values,
):
    f32, i16 = jnp.float32, jnp.int16
    slabs, size = lax.axis_size("slab"), lax.axis_size("line")
    bands, lines, cols = cube.shape
    count = resp_values.shape[0]
    half = cols // 2
    _, _, units = ownership(count)
    shape = jax.ShapeDtypeStruct
    swap = [(0, 1), (1, 0)]
    blocks = [(s, i) for s in range(slabs) for i in range(size)]
    partner = [((s, i), (s, i ^ 1)) for s, i in blocks]

    def two_on(s, i):
        i = i + 2 - 4 * (i % 2)
        return (s, i) if 0 <= i < size else ((s + 1) % slabs, i % size)

    even_up = [(block, two_on(*block)) for block in blocks]
    odd_up = [(j, i) for i, j in even_up]
    everywhere = ("slab", "line", "band")

    def cores(*pairs):
        return [
            ((a * size + b) * 2 + core, (c * size + d) * 2 + core)
            for core in range(2)
            for (a, b), (c, d) in pairs[core]
        ]

    part = shape((units, lines, half), f32)
    edges = [-(-units * i // CHUNKS) for i in range(CHUNKS + 1)]
    spans = list(zip(edges[:-1], edges[1:]))
    coded = [shape((coded_rows(b - a, lines), half), i16) for a, b in spans]

    inputs = (
        resp_start,
        across_offsets,
        resp_values,
        across_kernels,
        along_offsets,
        along_kernels,
        cube,
    )
    inputs = [pltpu.with_memory_space_constraint(x, pltpu.HBM) for x in inputs]
    planes, odd, _ = ownership(count)
    wide = shape(resp_values.shape, f32)
    table = shape((2 * cols, cols), across_kernels.dtype)
    send, middle, local, wide, table, picked = call(
        fold_other,
        inputs,
        [HBM] * len(inputs),
        [part, shape((1, lines, half), f32), cube, wide, table, along_kernels],
        scratch=[
            pltpu.SMEM(resp_start.shape, jnp.int32),
            pltpu.SMEM(across_offsets.shape, jnp.int32),
            pltpu.VMEM(resp_values.shape, resp_values.dtype),
            pltpu.SMEM(resp_values.shape, f32),
            pltpu.VMEM(across_kernels.shape, across_kernels.dtype),
            pltpu.SMEM(along_offsets.shape, jnp.int32),
            pltpu.VMEM(along_kernels.shape, along_kernels.dtype),
            pltpu.VMEM((planes + odd, lines, cols), f32),
            pltpu.SMEM((count,), jnp.int32),
            pltpu.SemaphoreType.DMA((len(inputs),)),
            pltpu.SemaphoreType.DMA((-(-bands // resp_values.shape[1]),)),
        ],
    )
    (keep,) = call(
        fold_own,
        (inputs[0], wide, local, table, middle),
        [HBM] + [VMEM] * 4,
        [part],
        scratch=[
            pltpu.SMEM(resp_start.shape, jnp.int32),
            pltpu.SMEM(resp_values.shape, f32),
            pltpu.VMEM((planes, lines, cols), f32),
            pltpu.SMEM((count,), jnp.int32),
            pltpu.SemaphoreType.DMA((2,)),
        ],
    )
    work = [pltpu.VMEM(part.shape, f32)]
    other = lax.ppermute(send, "band", swap)
    total, *sent = call(
        functools.partial(share, spans),
        (picked, keep, other),
        [VMEM] * 3,
        [part, *coded],
        scratch=work,
    )
    near = [lax.ppermute(x, everywhere, cores(partner, odd_up)) for x in sent]
    other_total = lax.ppermute(total, "band", swap)
    base, other_base, term = call(
        centre, (picked, total, other_total), [VMEM] * 3, [part] * 3
    )
    far, product = [], []
    for i, span in enumerate(spans):
        (message,) = call(
            functools.partial(relay, span), (term, near[i]), [VMEM] * 2, [coded[i]], scratch=work
        )
        message, near[i] = lax.optimization_barrier((message, near[i]))
        far.append(lax.ppermute(message, everywhere, cores(even_up, partner)))
        planes = shape((span[1] - span[0], lines, half), f32)
        product += call(
            functools.partial(beside, span),
            (picked, near[i]),
            [VMEM] * 2,
            [planes],
        )
    messages, others = [], []
    for i, span in enumerate(spans):
        planes = product[i].shape
        messages += call(
            functools.partial(settle, span),
            (picked, product[i], far[i]),
            [VMEM] * 3,
            [coded[i]],
            scratch=[pltpu.VMEM(planes, f32)],
        )
        others.append(lax.ppermute(messages[i], "band", swap))
    image = shape((count, lines, cols), f32)
    three = shape((3, lines, cols), f32)
    inputs = [observed, base, other_base, *messages, *others[:-1]]
    image, own, theirs = call(
        functools.partial(finish_most, spans),
        inputs,
        [VMEM] * len(inputs),
        [image, three, three],
        scratch=work * 2 + [pltpu.SemaphoreType.DMA((2 * units,))],
        out_specs=[HBM, VMEM, VMEM],
    )
    image, angles = call(
        functools.partial(finish_last, spans[-1]),
        (observed, other_base, others[-1], own, theirs, image),
        [VMEM] * 5 + [HBM],
        [image, shape((lines, cols), f32)],
        scratch=[pltpu.VMEM((lines, cols), f32), *work, pltpu.SemaphoreType.DMA((units + 1,))],
        out_specs=[HBM] * 2,
        aliases={5: 0},
    )
    return image, angles


def solution(mesh):
    placed = (
        P("band", ("slab", "line"), None),
        P(None, ("slab", "line"), None),
        P(),
        P(),
        P(),
        P(),
        P(),
        P(),
    )
    return jax.shard_map(
        on_device,
        mesh=mesh,
        in_specs=placed,
        out_specs=(P(None, ("slab", "line"), None), P(("slab", "line"), None)),
        check_vma=False,
    )
```

```python
import functools
import math

import jax
import jax.numpy as jnp
from jax import lax
from jax.experimental import pallas as pl
from jax.experimental.pallas import tpu as pltpu
from jax.sharding import PartitionSpec as P

BLK = 128
SPB = 10
STEPS = 16.0
PEAK = 32000.0


def which(offsets, shift):
    return sum(
        jnp.where(offsets[k] == shift, jnp.int32(k), jnp.int32(0)) for k in range(offsets.shape[0])
    )


def split(value):
    high = value.astype(jnp.bfloat16)
    low = (value - high.astype(jnp.float32)).astype(jnp.bfloat16)
    return high, low


SMEM = pl.BlockSpec(memory_space=pltpu.SMEM)
VMEM = pl.BlockSpec(memory_space=pltpu.VMEM)
HBM = pl.BlockSpec(memory_space=pltpu.HBM)
ROWS = 64
CHUNKS = 3


def call(kernel, inputs, specs, outs, scratch=(), out_specs=None, aliases=None):
    return pl.pallas_call(
        kernel,
        in_specs=specs,
        out_specs=out_specs or [VMEM] * len(outs),
        out_shape=[jax.ShapeDtypeStruct(x.shape, x.dtype) for x in outs],
        scratch_shapes=scratch,
        input_output_aliases=aliases or {},
        compiler_params=pltpu.CompilerParams(vmem_limit_bytes=32 * 2**20),
        cost_estimate=pl.CostEstimate(flops=0, bytes_accessed=0, transcendentals=0),
        name=(kernel.func if isinstance(kernel, functools.partial) else kernel).__name__,
    )(*inputs)


def ownership(count):
    pairs = count // 2
    return pairs, count % 2, 2 * pairs + count % 2


def units_of(core, count):
    pairs, odd, _ = ownership(count)
    first = core * (pairs + odd)
    return [(first + i, c) for i in range(pairs) for c in range(2)] + [(pairs, core)] * odd


def sum_windows(number, plane_of, start, weights, cube, folded, order, ready=None):
    bands, lines, cols = cube.shape
    window = weights.shape[1]
    group = math.gcd(SPB, bands)
    first = bands * lax.axis_index("band")
    places = [SPB * start[plane_of(i)] - first for i in range(number)]
    ranks = [jnp.int32(0)] * number
    for m in range(number):
        for n in range(m + 1, number):
            later = (places[n] < places[m]).astype(jnp.int32)
            ranks[m] = ranks[m] + later
            ranks[n] = ranks[n] + (1 - later)
    before = jnp.int32(0)
    until = jnp.int32(0)
    for m in range(number):
        order[ranks[m]] = jnp.int32(m)
        before = before + (places[m] <= -window).astype(jnp.int32)
        until = until + (places[m] < bands).astype(jnp.int32)

    def clear(n, carry):
        folded[order[n]] = jnp.zeros((lines, cols), jnp.float32)
        return carry

    lax.fori_loop(0, before, clear, 0)
    lax.fori_loop(until, number, clear, 0)

    def one(n, arrived):
        i = order[n]
        m = plane_of(i)
        low = SPB * start[m] - first
        stop = jnp.minimum(low + window, bands)
        needed = lax.div(stop - 1, jnp.int32(window)) + 1
        if ready is not None:
            ready(arrived, needed)
        whole = jnp.logical_and(low >= 0, low + window <= bands)

        def term(band, weight, r):
            return weight * cube[band, r : r + ROWS, :].astype(jnp.float32)

        @pl.when(whole)
        def _():
            for r in range(0, lines, ROWS):
                total = term(low, weights[m, 0], r)
                for j in range(1, window):
                    total = total + term(low + j, weights[m, j], r)
                folded[i, r : r + ROWS, :] = total

        @pl.when(jnp.logical_not(whole))
        def _():
            begin = jnp.maximum(low, 0)
            for r in range(0, lines, ROWS):

                def some(t, total):
                    for k in range(group):
                        band = begin + t * group + k
                        total = total + term(band, weights[m, band - low], r)
                    return total

                folded[i, r : r + ROWS, :] = lax.fori_loop(
                    0,
                    lax.div(stop - begin, jnp.int32(group)),
                    some,
                    jnp.zeros((ROWS, cols), jnp.float32),
                )

        return jnp.maximum(arrived, needed)

    return lax.fori_loop(before, until, one, jnp.int32(0))


def across(value, table):
    planes, lines, cols = value.shape
    both = jnp.concatenate(split(value.reshape(planes * lines, cols)), axis=1)
    made = jnp.dot(both, table, preferred_element_type=jnp.float32)
    return made.reshape(planes, lines, cols)


def spread_out(made, out):
    half = made.shape[2] // 2
    for i in range(made.shape[0]):
        out[2 * i] = made[i, :, :half]
        out[2 * i + 1] = made[i, :, half:]


def fold_other(
    start_in,
    offsets_in,
    values_in,
    blocks_in,
    along_offsets_in,
    along_blocks_in,
    cube_in,
    send,
    middle,
    cube,
    wide,
    table,
    picked,
    start,
    offsets,
    values,
    weights,
    blocks,
    along_offsets,
    along_blocks,
    folded,
    order,
    small,
    large,
):
    bands, lines, cols = cube.shape
    count, window = values.shape
    half = cols // 2
    planes, odd, units = ownership(count)
    me = lax.axis_index("band")
    pairs = (
        (start_in, start),
        (values_in, values),
        (offsets_in, offsets),
        (blocks_in, blocks),
        (along_offsets_in, along_offsets),
        (along_blocks_in, along_blocks),
    )
    copies = [pltpu.make_async_copy(a, b, small.at[i]) for i, (a, b) in enumerate(pairs)]
    chunks = -(-bands // window)
    last = bands - (chunks - 1) * window

    def arrive(q, size):
        at = pl.ds(q * window, size)
        return pltpu.make_async_copy(cube_in.at[at], cube.at[at], large.at[q])

    for copy in copies:
        copy.start()
    for q in range(chunks):
        arrive(q, window if q < chunks - 1 else last).start()
    copies[1].wait()
    wide[...] = values[...].astype(jnp.float32)
    spread = pltpu.make_async_copy(wide, weights, small.at[len(pairs)])
    spread.start()
    for copy in copies[:1] + copies[2:]:
        copy.wait()
    for r in range(2):
        for c in range(2):
            block = blocks[which(offsets, jnp.int32(r - c))].astype(jnp.float32).T
            for top in (0, cols):
                at = slice(top + r * half, top + (r + 1) * half)
                table[at, c * half : (c + 1) * half] = block.astype(jnp.bfloat16)
    step = side_step()
    for i, shift in enumerate((jnp.int32(0), step, -step)):
        picked[i] = along_blocks[which(along_offsets, shift)]
    spread.wait()

    def one(q, carry):
        pl.when(q < chunks - 1)(lambda: arrive(q, window).wait())
        pl.when(q == chunks - 1)(lambda: arrive(chunks - 1, last).wait())
        return carry

    def ready(a, b):
        lax.fori_loop(a, b, one, 0)

    base = (1 - me) * (planes + odd)

    def plane_of(i):
        return jnp.where(i == planes, planes, base + i) if odd else base + i

    arrived = sum_windows(planes + odd, plane_of, start, weights, cube, folded, order, ready)
    ready(arrived, chunks)
    made = across(folded[...], table[...])
    spread_out(made[:planes], send)
    if odd:
        left, right = made[planes, :, :half], made[planes, :, half:]
        middle[0] = jnp.where(me == 0, left, right)
        send[units - 1] = jnp.where(me == 0, right, left)


def fold_own(start_in, wide, cube, table, middle, keep, start, weights, folded, order, sems):
    planes, odd, units = ownership(wide.shape[0])
    copies = [
        pltpu.make_async_copy(start_in, start, sems.at[0]),
        pltpu.make_async_copy(wide, weights, sems.at[1]),
    ]
    for copy in copies:
        copy.start()
    for copy in copies:
        copy.wait()
    base = lax.axis_index("band") * (planes + odd)
    sum_windows(planes, lambda i: base + i, start, weights, cube, folded, order)
    spread_out(across(folded[...], table[...]), keep)
    if odd:
        keep[units - 1] = middle[0]


def coded_rows(count, lines):
    return count * lines + -(-count // 16) * 16


def encode(source, span, message):
    _, lines, half = source.shape
    units = span[1] - span[0]
    largest = jnp.max(jnp.abs(source[span[0] : span[1]]), axis=1)
    level = jnp.ceil(jnp.log2(jnp.maximum(largest, 1e-30)) * STEPS)
    factor = PEAK * jnp.exp2(level * (-1.0 / STEPS))
    for m in range(units):
        coded = jnp.floor(source[span[0] + m] * factor[m : m + 1, :] + 0.5).astype(jnp.int32)
        message[m * lines : (m + 1) * lines, :] = coded.astype(jnp.int16)
    spare = message.shape[0] - units * lines - units
    level = jnp.concatenate([level, jnp.zeros((spare, half), jnp.float32)], axis=0)
    message[units * lines :, :] = level.astype(jnp.int32).astype(jnp.int16)


def decode(message, span, lines, valid=True):
    units = span[1] - span[0]
    level = message[units * lines :, :].astype(jnp.int32).astype(jnp.float32)
    scale = jnp.where(valid, jnp.exp2(level * (1.0 / STEPS)) * (1.0 / PEAK), 0.0)

    def plane(m):
        coded = message[m * lines : (m + 1) * lines, :].astype(jnp.int32).astype(jnp.float32)
        return coded * scale[m : m + 1, :]

    return plane


def blurred(filters, count, plane, put):
    wide = jnp.concatenate([filters, filters], axis=1)
    for m in range(0, count, 2):
        parts = [split(plane(n)) for n in range(m, min(m + 2, count))]
        high = jnp.concatenate([p[0] for p in parts], axis=1)
        low = jnp.concatenate([p[1] for p in parts], axis=1)
        made = jnp.dot(
            wide, jnp.concatenate([high, low], axis=0), preferred_element_type=jnp.float32
        )
        half = made.shape[1] // len(parts)
        for i in range(len(parts)):
            put(m + i, made[:, i * half : (i + 1) * half])


def side_step():
    return jnp.where(lax.axis_index("line") % 2 == 0, jnp.int32(1), jnp.int32(-1))


def outside(*lines):
    return functools.reduce(jnp.logical_or, [lax.axis_index("line") == i for i in lines])


def by_core(zero, one):
    me = lax.axis_index("band")
    pl.when(me == 0)(zero)
    pl.when(me != 0)(one)


def share(spans, picked, keep, other, total, *rest):
    messages, product = rest[:-1], rest[-1]
    total[...] = keep[...] + other[...]

    def coding(source):
        for span, message in zip(spans, messages):
            encode(source, span, message)

    def summing():
        def put(m, value):
            product[m] = value

        blurred(picked[1], total.shape[0], lambda m: total[m], put)
        coding(product)

    by_core(lambda: coding(total), summing)


def centre(picked, total, base, term):
    def into(out):
        def put(m, value):
            out[m] = value

        return put

    blurred(picked[0], total.shape[0], lambda m: total[m], into(base))
    pl.when(lax.axis_index("band") != 0)(
        lambda: blurred(picked[2], total.shape[0], lambda m: total[m], into(term))
    )


def relay(span, term, received, message, total):
    def forward():
        message[...] = received[...]

    def add():
        missing = outside(1, lax.axis_size("line") - 2)
        plane = decode(received, span, term.shape[1], jnp.logical_not(missing))
        for m in range(*span):
            total[m] = term[m] + plane(m - span[0])
        encode(total, span, message)

    by_core(forward, add)


def beside(span, picked, base, near, product):
    units, lines, _ = product.shape

    def put(m, value):
        product[m] = base[span[0] + m] + value

    plane = decode(near, span, lines)
    pl.when(lax.axis_index("band") == 0)(lambda: blurred(picked[1], units, plane, put))


def settle(span, picked, base, product, received, message, total):
    units, lines, _ = product.shape

    def put(m, value):
        total[m] = product[m] + value

    def spreading():
        missing = outside(0, lax.axis_size("line") - 1)
        plane = decode(received, span, lines, jnp.logical_not(missing))
        blurred(picked[2], units, plane, put)

    def summing():
        plane = decode(received, span, lines)
        for m in range(units):
            total[m] = base[span[0] + m] + plane(m)

    by_core(spreading, summing)
    encode(total, (0, units), message)


def arccos(x):
    size = jnp.abs(x)
    big = size > 0.5
    z = jnp.where(big, 0.5 * (1.0 - size), size * size)
    root = jnp.where(big, jnp.sqrt(z), size)
    poly = 4.2163199048e-2
    for term in (2.4181311049e-2, 4.5470025998e-2, 7.4953002686e-2, 1.6666752422e-1):
        poly = poly * z + term
    arcsin = poly * z * root + root
    pi = 3.14159265358979
    inner = jnp.where(x < 0, 0.5 * pi + arcsin, 0.5 * pi - arcsin)
    outer = jnp.where(x < 0, pi - 2.0 * arcsin, 2.0 * arcsin)
    return jnp.where(big, outer, inner)


def finish_units(core, parts, observed, value, image, sem, sums):
    _, lines, half = value.shape
    copies = []
    for span, message in parts:
        plane = decode(message, span, lines)
        for n in range(*span):
            m, c = units_of(core, observed.shape[0])[n]
            at = slice(c * half, (c + 1) * half)
            made = plane(n - span[0])
            value[n] = made
            copies.append(pltpu.make_async_copy(value.at[n], image.at[m, :, at], sem(n)))
            copies[-1].start()
            seen = observed[m, :, at].astype(jnp.float32)
            sums[c] = (sums[c][0] + made * seen, sums[c][1] + made * made)
    return copies


def finish_most(spans, observed, *rest):
    chunks = len(spans)
    messages, others, rest = rest[:chunks], rest[chunks : 2 * chunks - 1], rest[2 * chunks - 1 :]
    image, own, theirs, value, other_value, sems = rest
    units, lines, half = value.shape
    zero = jnp.zeros((lines, half), jnp.float32)

    def work(core):
        sums, other_sums = [(zero, zero)] * 2, [(zero, zero)] * 2
        parts = list(zip(spans, messages))
        copies = finish_units(
            core, parts, observed, value, image, lambda n: sems.at[n], sums
        )
        parts = list(zip(spans[:-1], others))
        copies += finish_units(
            1 - core,
            parts,
            observed,
            other_value,
            image,
            lambda n: sems.at[units + n],
            other_sums,
        )
        for c in range(2):
            at = slice(c * half, (c + 1) * half)
            right = zero
            for m in range(observed.shape[0]):
                seen = observed[m, :, at].astype(jnp.float32)
                right = right + seen * seen
            own[0, :, at], own[1, :, at] = sums[c]
            own[2, :, at] = jnp.sqrt(right)
            theirs[0, :, at], theirs[1, :, at] = other_sums[c]
        for copy in copies:
            copy.wait()

    by_core(lambda: work(0), lambda: work(1))


def finish_last(span, observed, message, own, theirs, _, *rest):
    image, angles, angle, value, sems = rest
    units, lines, half = value.shape

    def work(core):
        columns = [slice(c * half, (c + 1) * half) for c in range(2)]
        sums = [(theirs[0, :, at], theirs[1, :, at]) for at in columns]
        copies = finish_units(
            core,
            [(span, message)],
            observed,
            value,
            image,
            lambda n: sems.at[n],
            sums,
        )
        for (inner, left), at in zip(sums, columns):
            bound = jnp.sqrt(left + own[1, :, at]) * own[2, :, at]
            ratio = (inner + own[0, :, at]) / jnp.maximum(bound, 1.0)
            angle[:, at] = arccos(jnp.clip(ratio, -1.0, 1.0))
        copies.append(pltpu.make_async_copy(angle, angles, sems.at[units]))
        copies[-1].start()
        for copy in copies:
            copy.wait()

    by_core(lambda: work(1), lambda: work(0))


def on_device(
    cube,
    observed,
    along_kernels,
    along_offsets,
    across_kernels,
    across_offsets,
    resp_start,
    resp_values,
):
    f32, i16 = jnp.float32, jnp.int16
    size = lax.axis_size("line")
    bands, lines, cols = cube.shape
    count = resp_values.shape[0]
    half = cols // 2
    _, _, units = ownership(count)
    shape = jax.ShapeDtypeStruct
    swap = [(0, 1), (1, 0)]
    partner = [(i, i ^ 1) for i in range(size)]
    even_up = [(i, (i + 2 - 4 * (i % 2)) % size) for i in range(size)]
    odd_up = [(j, i) for i, j in even_up]

    def cores(zero, one):
        return [(2 * a, 2 * b) for a, b in zero] + [(2 * a + 1, 2 * b + 1) for a, b in one]

    part = shape((units, lines, half), f32)
    edges = [-(-units * i // CHUNKS) for i in range(CHUNKS + 1)]
    spans = list(zip(edges[:-1], edges[1:]))
    coded = [shape((coded_rows(b - a, lines), half), i16) for a, b in spans]

    inputs = (
        resp_start,
        across_offsets,
        resp_values,
        across_kernels,
        along_offsets,
        along_kernels,
        cube,
    )
    inputs = [pltpu.with_memory_space_constraint(x, pltpu.HBM) for x in inputs]
    planes, odd, _ = ownership(count)
    wide = shape(resp_values.shape, f32)
    table = shape((2 * cols, cols), across_kernels.dtype)
    send, middle, local, wide, table, picked = call(
        fold_other,
        inputs,
        [HBM] * len(inputs),
        [part, shape((1, lines, half), f32), cube, wide, table, along_kernels],
        scratch=[
            pltpu.SMEM(resp_start.shape, jnp.int32),
            pltpu.SMEM(across_offsets.shape, jnp.int32),
            pltpu.VMEM(resp_values.shape, resp_values.dtype),
            pltpu.SMEM(resp_values.shape, f32),
            pltpu.VMEM(across_kernels.shape, across_kernels.dtype),
            pltpu.SMEM(along_offsets.shape, jnp.int32),
            pltpu.VMEM(along_kernels.shape, along_kernels.dtype),
            pltpu.VMEM((planes + odd, lines, cols), f32),
            pltpu.SMEM((count,), jnp.int32),
            pltpu.SemaphoreType.DMA((len(inputs),)),
            pltpu.SemaphoreType.DMA((-(-bands // resp_values.shape[1]),)),
        ],
    )
    (keep,) = call(
        fold_own,
        (inputs[0], wide, local, table, middle),
        [HBM] + [VMEM] * 4,
        [part],
        scratch=[
            pltpu.SMEM(resp_start.shape, jnp.int32),
            pltpu.SMEM(resp_values.shape, f32),
            pltpu.VMEM((planes, lines, cols), f32),
            pltpu.SMEM((count,), jnp.int32),
            pltpu.SemaphoreType.DMA((2,)),
        ],
    )
    work = [pltpu.VMEM(part.shape, f32)]
    other = lax.ppermute(send, "band", swap)
    total, *sent = call(
        functools.partial(share, spans),
        (picked, keep, other),
        [VMEM] * 3,
        [part, *coded],
        scratch=work,
    )
    near = [lax.ppermute(x, ("line", "band"), cores(partner, odd_up)) for x in sent]
    base, term = call(centre, (picked, total), [VMEM] * 2, [part] * 2)
    far, product = [], []
    for i, span in enumerate(spans):
        (message,) = call(
            functools.partial(relay, span), (term, near[i]), [VMEM] * 2, [coded[i]], scratch=work
        )
        message, near[i] = lax.optimization_barrier((message, near[i]))
        far.append(lax.ppermute(message, ("line", "band"), cores(even_up, partner)))
        planes = shape((span[1] - span[0], lines, half), f32)
        product += call(
            functools.partial(beside, span),
            (picked, base, near[i]),
            [VMEM] * 3,
            [planes],
        )
    messages, others = [], []
    for i, span in enumerate(spans):
        planes = product[i].shape
        messages += call(
            functools.partial(settle, span),
            (picked, base, product[i], far[i]),
            [VMEM] * 4,
            [coded[i]],
            scratch=[pltpu.VMEM(planes, f32)],
        )
        others.append(lax.ppermute(messages[i], "band", swap))
    image = shape((count, lines, cols), f32)
    three = shape((3, lines, cols), f32)
    inputs = [observed, *messages, *others[:-1]]
    image, own, theirs = call(
        functools.partial(finish_most, spans),
        inputs,
        [VMEM] * len(inputs),
        [image, three, three],
        scratch=work * 2 + [pltpu.SemaphoreType.DMA((2 * units,))],
        out_specs=[HBM, VMEM, VMEM],
    )
    image, angles = call(
        functools.partial(finish_last, spans[-1]),
        (observed, others[-1], own, theirs, image),
        [VMEM] * 4 + [HBM],
        [image, shape((lines, cols), f32)],
        scratch=[pltpu.VMEM((lines, cols), f32), *work, pltpu.SemaphoreType.DMA((units + 1,))],
        out_specs=[HBM] * 2,
        aliases={4: 0},
    )
    return image, angles


def solution(mesh):
    placed = (
        P("band", ("slab", "line"), None),
        P(None, ("slab", "line"), None),
        P(),
        P(),
        P(),
        P(),
        P(),
        P(),
    )
    return jax.shard_map(
        on_device,
        mesh=mesh,
        in_specs=placed,
        out_specs=(P(None, ("slab", "line"), None), P(("slab", "line"), None)),
        check_vma=False,
    )
```

```python
import functools
import math

import jax
import jax.numpy as jnp
from jax import lax
from jax.experimental import pallas as pl
from jax.experimental.pallas import tpu as pltpu
from jax.sharding import PartitionSpec as P

BLK = 128
SPB = 10
STEPS = 16.0
PEAK = 32000.0


def which(offsets, shift):
    return sum(
        jnp.where(offsets[k] == shift, jnp.int32(k), jnp.int32(0)) for k in range(offsets.shape[0])
    )


def split(value):
    high = value.astype(jnp.bfloat16)
    low = (value - high.astype(jnp.float32)).astype(jnp.bfloat16)
    return high, low


SMEM = pl.BlockSpec(memory_space=pltpu.SMEM)
VMEM = pl.BlockSpec(memory_space=pltpu.VMEM)
HBM = pl.BlockSpec(memory_space=pltpu.HBM)
ROWS = 128
CHUNKS = 3


def call(kernel, inputs, specs, outs, scratch=(), out_specs=None, aliases=None):
    return pl.pallas_call(
        kernel,
        in_specs=specs,
        out_specs=out_specs or [VMEM] * len(outs),
        out_shape=[jax.ShapeDtypeStruct(x.shape, x.dtype) for x in outs],
        scratch_shapes=scratch,
        input_output_aliases=aliases or {},
        compiler_params=pltpu.CompilerParams(vmem_limit_bytes=32 * 2**20),
        cost_estimate=pl.CostEstimate(flops=0, bytes_accessed=0, transcendentals=0),
        name=(kernel.func if isinstance(kernel, functools.partial) else kernel).__name__,
    )(*inputs)


def ownership(count):
    pairs = count // 2
    return pairs, count % 2, 2 * pairs + count % 2


def units_of(core, count):
    pairs, odd, _ = ownership(count)
    first = core * (pairs + odd)
    return [(first + i, c) for i in range(pairs) for c in range(2)] + [(pairs, core)] * odd


def sum_windows(number, plane_of, start, weights, cube, folded, order, ready=None):
    bands, lines, cols = cube.shape
    window = weights.shape[1]
    group = math.gcd(SPB, bands)
    first = bands * lax.axis_index("band")
    places = [SPB * start[plane_of(i)] - first for i in range(number)]
    ranks = [jnp.int32(0)] * number
    for m in range(number):
        for n in range(m + 1, number):
            later = (places[n] < places[m]).astype(jnp.int32)
            ranks[m] = ranks[m] + later
            ranks[n] = ranks[n] + (1 - later)
    before = jnp.int32(0)
    until = jnp.int32(0)
    for m in range(number):
        order[ranks[m]] = jnp.int32(m)
        before = before + (places[m] <= -window).astype(jnp.int32)
        until = until + (places[m] < bands).astype(jnp.int32)

    def clear(n, carry):
        folded[order[n]] = jnp.zeros((lines, cols), jnp.float32)
        return carry

    lax.fori_loop(0, before, clear, 0)
    lax.fori_loop(until, number, clear, 0)

    def one(n, arrived):
        i = order[n]
        m = plane_of(i)
        low = SPB * start[m] - first
        stop = jnp.minimum(low + window, bands)
        needed = lax.div(stop - 1, jnp.int32(window)) + 1
        if ready is not None:
            ready(arrived, needed)
        whole = jnp.logical_and(low >= 0, low + window <= bands)

        def term(band, weight, r):
            return weight * cube[band, r : r + ROWS, :].astype(jnp.float32)

        @pl.when(whole)
        def _():
            for r in range(0, lines, ROWS):
                total = term(low, weights[m, 0], r)
                for j in range(1, window):
                    total = total + term(low + j, weights[m, j], r)
                folded[i, r : r + ROWS, :] = total

        @pl.when(jnp.logical_not(whole))
        def _():
            begin = jnp.maximum(low, 0)
            for r in range(0, lines, ROWS):

                def some(t, total):
                    for k in range(group):
                        band = begin + t * group + k
                        total = total + term(band, weights[m, band - low], r)
                    return total

                folded[i, r : r + ROWS, :] = lax.fori_loop(
                    0,
                    lax.div(stop - begin, jnp.int32(group)),
                    some,
                    jnp.zeros((ROWS, cols), jnp.float32),
                )

        return jnp.maximum(arrived, needed)

    return lax.fori_loop(before, until, one, jnp.int32(0))


def across(value, table):
    planes, lines, cols = value.shape
    both = jnp.concatenate(split(value.reshape(planes * lines, cols)), axis=1)
    made = jnp.dot(both, table, preferred_element_type=jnp.float32)
    return made.reshape(planes, lines, cols)


def spread_out(made, out):
    half = made.shape[2] // 2
    for i in range(made.shape[0]):
        out[2 * i] = made[i, :, :half]
        out[2 * i + 1] = made[i, :, half:]


def fold_other(
    start_in,
    offsets_in,
    values_in,
    blocks_in,
    along_offsets_in,
    along_blocks_in,
    cube_in,
    send,
    middle,
    cube,
    wide,
    table,
    picked,
    start,
    offsets,
    values,
    weights,
    blocks,
    along_offsets,
    along_blocks,
    folded,
    order,
    small,
    large,
):
    bands, lines, cols = cube.shape
    count, window = values.shape
    half = cols // 2
    planes, odd, units = ownership(count)
    me = lax.axis_index("band")
    pairs = (
        (start_in, start),
        (values_in, values),
        (offsets_in, offsets),
        (blocks_in, blocks),
        (along_offsets_in, along_offsets),
        (along_blocks_in, along_blocks),
    )
    copies = [pltpu.make_async_copy(a, b, small.at[i]) for i, (a, b) in enumerate(pairs)]
    chunks = -(-bands // window)
    last = bands - (chunks - 1) * window

    def arrive(q, size):
        at = pl.ds(q * window, size)
        return pltpu.make_async_copy(cube_in.at[at], cube.at[at], large.at[q])

    for copy in copies:
        copy.start()
    for q in range(chunks):
        arrive(q, window if q < chunks - 1 else last).start()
    copies[1].wait()
    wide[...] = values[...].astype(jnp.float32)
    spread = pltpu.make_async_copy(wide, weights, small.at[len(pairs)])
    spread.start()
    for copy in copies[:1] + copies[2:]:
        copy.wait()
    for r in range(2):
        for c in range(2):
            block = blocks[which(offsets, jnp.int32(r - c))].astype(jnp.float32).T
            for top in (0, cols):
                at = slice(top + r * half, top + (r + 1) * half)
                table[at, c * half : (c + 1) * half] = block.astype(jnp.bfloat16)
    step = side_step()
    for i, shift in enumerate((jnp.int32(0), step, -step)):
        picked[i] = along_blocks[which(along_offsets, shift)]
    spread.wait()

    def one(q, carry):
        pl.when(q < chunks - 1)(lambda: arrive(q, window).wait())
        pl.when(q == chunks - 1)(lambda: arrive(chunks - 1, last).wait())
        return carry

    def ready(a, b):
        lax.fori_loop(a, b, one, 0)

    base = (1 - me) * (planes + odd)

    def plane_of(i):
        return jnp.where(i == planes, planes, base + i) if odd else base + i

    arrived = sum_windows(planes + odd, plane_of, start, weights, cube, folded, order, ready)
    ready(arrived, chunks)
    made = across(folded[...], table[...])
    spread_out(made[:planes], send)
    if odd:
        left, right = made[planes, :, :half], made[planes, :, half:]
        middle[0] = jnp.where(me == 0, left, right)
        send[units - 1] = jnp.where(me == 0, right, left)


def fold_own(start_in, wide, cube, table, middle, keep, start, weights, folded, order, sems):
    planes, odd, units = ownership(wide.shape[0])
    copies = [
        pltpu.make_async_copy(start_in, start, sems.at[0]),
        pltpu.make_async_copy(wide, weights, sems.at[1]),
    ]
    for copy in copies:
        copy.start()
    for copy in copies:
        copy.wait()
    base = lax.axis_index("band") * (planes + odd)
    sum_windows(planes, lambda i: base + i, start, weights, cube, folded, order)
    spread_out(across(folded[...], table[...]), keep)
    if odd:
        keep[units - 1] = middle[0]


def coded_rows(count, lines):
    return count * lines + -(-count // 16) * 16


def encode(source, span, message):
    _, lines, half = source.shape
    units = span[1] - span[0]
    largest = jnp.max(jnp.abs(source[span[0] : span[1]]), axis=1)
    level = jnp.ceil(jnp.log2(jnp.maximum(largest, 1e-30)) * STEPS)
    factor = PEAK * jnp.exp2(level * (-1.0 / STEPS))
    for m in range(units):
        coded = jnp.floor(source[span[0] + m] * factor[m : m + 1, :] + 0.5).astype(jnp.int32)
        message[m * lines : (m + 1) * lines, :] = coded.astype(jnp.int16)
    spare = message.shape[0] - units * lines - units
    level = jnp.concatenate([level, jnp.zeros((spare, half), jnp.float32)], axis=0)
    message[units * lines :, :] = level.astype(jnp.int32).astype(jnp.int16)


def decode(message, span, lines, valid=True):
    units = span[1] - span[0]
    level = message[units * lines :, :].astype(jnp.int32).astype(jnp.float32)
    scale = jnp.where(valid, jnp.exp2(level * (1.0 / STEPS)) * (1.0 / PEAK), 0.0)

    def plane(m):
        coded = message[m * lines : (m + 1) * lines, :].astype(jnp.int32).astype(jnp.float32)
        return coded * scale[m : m + 1, :]

    return plane


def blurred(filters, count, plane, put):
    wide = jnp.concatenate([filters, filters], axis=1)
    for m in range(0, count, 2):
        parts = [split(plane(n)) for n in range(m, min(m + 2, count))]
        high = jnp.concatenate([p[0] for p in parts], axis=1)
        low = jnp.concatenate([p[1] for p in parts], axis=1)
        made = jnp.dot(
            wide, jnp.concatenate([high, low], axis=0), preferred_element_type=jnp.float32
        )
        half = made.shape[1] // len(parts)
        for i in range(len(parts)):
            put(m + i, made[:, i * half : (i + 1) * half])


def side_step():
    return jnp.where(lax.axis_index("line") % 2 == 0, jnp.int32(1), jnp.int32(-1))


def outside(*lines):
    return functools.reduce(jnp.logical_or, [lax.axis_index("line") == i for i in lines])


def by_core(zero, one):
    me = lax.axis_index("band")
    pl.when(me == 0)(zero)
    pl.when(me != 0)(one)


def share(spans, picked, keep, other, total, *rest):
    messages, product = rest[:-1], rest[-1]
    total[...] = keep[...] + other[...]

    def coding(source):
        for span, message in zip(spans, messages):
            encode(source, span, message)

    def summing():
        def put(m, value):
            product[m] = value

        blurred(picked[1], total.shape[0], lambda m: total[m], put)
        coding(product)

    by_core(lambda: coding(total), summing)


def centre(picked, total, observed, base, term, norm):
    def into(out):
        def put(m, value):
            out[m] = value

        return put

    blurred(picked[0], total.shape[0], lambda m: total[m], into(base))
    pl.when(lax.axis_index("band") != 0)(
        lambda: blurred(picked[2], total.shape[0], lambda m: total[m], into(term))
    )
    right = jnp.zeros(norm.shape, jnp.float32)
    for m in range(observed.shape[0]):
        seen = observed[m].astype(jnp.float32)
        right = right + seen * seen
    norm[...] = jnp.sqrt(right)


def relay(span, term, received, message, total):
    def forward():
        message[...] = received[...]

    def add():
        missing = outside(1, lax.axis_size("line") - 2)
        plane = decode(received, span, term.shape[1], jnp.logical_not(missing))
        for m in range(*span):
            total[m] = term[m] + plane(m - span[0])
        encode(total, span, message)

    by_core(forward, add)


def beside(span, picked, base, near, product):
    units, lines, _ = product.shape

    def put(m, value):
        product[m] = base[span[0] + m] + value

    plane = decode(near, span, lines)
    pl.when(lax.axis_index("band") == 0)(lambda: blurred(picked[1], units, plane, put))


def settle(span, picked, base, product, received, message, total):
    units, lines, _ = product.shape

    def put(m, value):
        total[m] = product[m] + value

    def spreading():
        missing = outside(0, lax.axis_size("line") - 1)
        plane = decode(received, span, lines, jnp.logical_not(missing))
        blurred(picked[2], units, plane, put)

    def summing():
        plane = decode(received, span, lines)
        for m in range(units):
            total[m] = base[span[0] + m] + plane(m)

    by_core(spreading, summing)
    encode(total, (0, units), message)


def arccos(x):
    size = jnp.abs(x)
    big = size > 0.5
    z = jnp.where(big, 0.5 * (1.0 - size), size * size)
    root = jnp.where(big, jnp.sqrt(z), size)
    poly = 4.2163199048e-2
    for term in (2.4181311049e-2, 4.5470025998e-2, 7.4953002686e-2, 1.6666752422e-1):
        poly = poly * z + term
    arcsin = poly * z * root + root
    pi = 3.14159265358979
    inner = jnp.where(x < 0, 0.5 * pi + arcsin, 0.5 * pi - arcsin)
    outer = jnp.where(x < 0, pi - 2.0 * arcsin, 2.0 * arcsin)
    return jnp.where(big, outer, inner)


def finish_units(core, parts, observed, value, image, sem, sums):
    _, lines, half = value.shape
    copies = []
    for span, message in parts:
        plane = decode(message, span, lines)
        for n in range(*span):
            m, c = units_of(core, observed.shape[0])[n]
            at = slice(c * half, (c + 1) * half)
            made = plane(n - span[0])
            value[n] = made
            copies.append(pltpu.make_async_copy(value.at[n], image.at[m, :, at], sem(n)))
            copies[-1].start()
            seen = observed[m, :, at].astype(jnp.float32)
            sums[c] = (sums[c][0] + made * seen, sums[c][1] + made * made)
    return copies


def finish_most(spans, observed, *rest):
    chunks = len(spans)
    messages, others, rest = rest[:chunks], rest[chunks : 2 * chunks - 1], rest[2 * chunks - 1 :]
    image, own, theirs, value, other_value, sems = rest
    units, lines, half = value.shape
    zero = jnp.zeros((lines, half), jnp.float32)

    def work(core):
        sums, other_sums = [(zero, zero)] * 2, [(zero, zero)] * 2
        parts = list(zip(spans, messages))
        copies = finish_units(
            core, parts, observed, value, image, lambda n: sems.at[n], sums
        )
        parts = list(zip(spans[:-1], others))
        copies += finish_units(
            1 - core,
            parts,
            observed,
            other_value,
            image,
            lambda n: sems.at[units + n],
            other_sums,
        )
        for c in range(2):
            at = slice(c * half, (c + 1) * half)
            own[0, :, at], own[1, :, at] = sums[c]
            theirs[0, :, at], theirs[1, :, at] = other_sums[c]
        for copy in copies:
            copy.wait()

    by_core(lambda: work(0), lambda: work(1))


def finish_last(span, observed, message, norm, own, theirs, _, *rest):
    image, angles, angle, value, sems = rest
    units, lines, half = value.shape

    def work(core):
        columns = [slice(c * half, (c + 1) * half) for c in range(2)]
        sums = [(theirs[0, :, at], theirs[1, :, at]) for at in columns]
        copies = finish_units(
            core,
            [(span, message)],
            observed,
            value,
            image,
            lambda n: sems.at[n],
            sums,
        )
        for (inner, left), at in zip(sums, columns):
            bound = jnp.sqrt(left + own[1, :, at]) * norm[:, at]
            ratio = (inner + own[0, :, at]) / jnp.maximum(bound, 1.0)
            angle[:, at] = arccos(jnp.clip(ratio, -1.0, 1.0))
        copies.append(pltpu.make_async_copy(angle, angles, sems.at[units]))
        copies[-1].start()
        for copy in copies:
            copy.wait()

    by_core(lambda: work(1), lambda: work(0))


def on_device(
    cube,
    observed,
    along_kernels,
    along_offsets,
    across_kernels,
    across_offsets,
    resp_start,
    resp_values,
):
    f32, i16 = jnp.float32, jnp.int16
    size = lax.axis_size("line")
    bands, lines, cols = cube.shape
    count = resp_values.shape[0]
    half = cols // 2
    _, _, units = ownership(count)
    shape = jax.ShapeDtypeStruct
    swap = [(0, 1), (1, 0)]
    partner = [(i, i ^ 1) for i in range(size)]
    even_up = [(i, (i + 2 - 4 * (i % 2)) % size) for i in range(size)]
    odd_up = [(j, i) for i, j in even_up]

    def cores(zero, one):
        return [(2 * a, 2 * b) for a, b in zero] + [(2 * a + 1, 2 * b + 1) for a, b in one]

    part = shape((units, lines, half), f32)
    edges = [-(-units * i // CHUNKS) for i in range(CHUNKS + 1)]
    spans = list(zip(edges[:-1], edges[1:]))
    coded = [shape((coded_rows(b - a, lines), half), i16) for a, b in spans]

    inputs = (
        resp_start,
        across_offsets,
        resp_values,
        across_kernels,
        along_offsets,
        along_kernels,
        cube,
    )
    inputs = [pltpu.with_memory_space_constraint(x, pltpu.HBM) for x in inputs]
    planes, odd, _ = ownership(count)
    wide = shape(resp_values.shape, f32)
    table = shape((2 * cols, cols), across_kernels.dtype)
    send, middle, local, wide, table, picked = call(
        fold_other,
        inputs,
        [HBM] * len(inputs),
        [part, shape((1, lines, half), f32), cube, wide, table, along_kernels],
        scratch=[
            pltpu.SMEM(resp_start.shape, jnp.int32),
            pltpu.SMEM(across_offsets.shape, jnp.int32),
            pltpu.VMEM(resp_values.shape, resp_values.dtype),
            pltpu.SMEM(resp_values.shape, f32),
            pltpu.VMEM(across_kernels.shape, across_kernels.dtype),
            pltpu.SMEM(along_offsets.shape, jnp.int32),
            pltpu.VMEM(along_kernels.shape, along_kernels.dtype),
            pltpu.VMEM((planes + odd, lines, cols), f32),
            pltpu.SMEM((count,), jnp.int32),
            pltpu.SemaphoreType.DMA((len(inputs),)),
            pltpu.SemaphoreType.DMA((-(-bands // resp_values.shape[1]),)),
        ],
    )
    (keep,) = call(
        fold_own,
        (inputs[0], wide, local, table, middle),
        [HBM] + [VMEM] * 4,
        [part],
        scratch=[
            pltpu.SMEM(resp_start.shape, jnp.int32),
            pltpu.SMEM(resp_values.shape, f32),
            pltpu.VMEM((planes, lines, cols), f32),
            pltpu.SMEM((count,), jnp.int32),
            pltpu.SemaphoreType.DMA((2,)),
        ],
    )
    work = [pltpu.VMEM(part.shape, f32)]
    other = lax.ppermute(send, "band", swap)
    total, *sent = call(
        functools.partial(share, spans),
        (picked, keep, other),
        [VMEM] * 3,
        [part, *coded],
        scratch=work,
    )
    near = [lax.ppermute(x, ("line", "band"), cores(partner, odd_up)) for x in sent]
    base, term, norm = call(
        centre, (picked, total, observed), [VMEM] * 3, [part, part, shape((lines, cols), f32)]
    )
    far, product = [], []
    for i, span in enumerate(spans):
        (message,) = call(
            functools.partial(relay, span), (term, near[i]), [VMEM] * 2, [coded[i]], scratch=work
        )
        message, near[i] = lax.optimization_barrier((message, near[i]))
        far.append(lax.ppermute(message, ("line", "band"), cores(even_up, partner)))
        planes = shape((span[1] - span[0], lines, half), f32)
        product += call(
            functools.partial(beside, span),
            (picked, base, near[i]),
            [VMEM] * 3,
            [planes],
        )
    messages, others = [], []
    for i, span in enumerate(spans):
        planes = product[i].shape
        messages += call(
            functools.partial(settle, span),
            (picked, base, product[i], far[i]),
            [VMEM] * 4,
            [coded[i]],
            scratch=[pltpu.VMEM(planes, f32)],
        )
        others.append(lax.ppermute(messages[i], "band", swap))
    image = shape((count, lines, cols), f32)
    pair = shape((2, lines, cols), f32)
    inputs = [observed, *messages, *others[:-1]]
    image, own, theirs = call(
        functools.partial(finish_most, spans),
        inputs,
        [VMEM] * len(inputs),
        [image, pair, pair],
        scratch=work * 2 + [pltpu.SemaphoreType.DMA((2 * units,))],
        out_specs=[HBM, VMEM, VMEM],
    )
    image, angles = call(
        functools.partial(finish_last, spans[-1]),
        (observed, others[-1], norm, own, theirs, image),
        [VMEM] * 5 + [HBM],
        [image, shape((lines, cols), f32)],
        scratch=[pltpu.VMEM((lines, cols), f32), *work, pltpu.SemaphoreType.DMA((units + 1,))],
        out_specs=[HBM] * 2,
        aliases={5: 0},
    )
    return image, angles


def solution(mesh):
    placed = (
        P("band", ("slab", "line"), None),
        P(None, ("slab", "line"), None),
        P(),
        P(),
        P(),
        P(),
        P(),
        P(),
    )
    return jax.shard_map(
        on_device,
        mesh=mesh,
        in_specs=placed,
        out_specs=(P(None, ("slab", "line"), None), P(("slab", "line"), None)),
        check_vma=False,
    )
```

```python
import functools
import math

import jax
import jax.numpy as jnp
from jax import lax
from jax.experimental import pallas as pl
from jax.experimental.pallas import tpu as pltpu
from jax.sharding import PartitionSpec as P

BLK = 128
SPB = 10
STEPS = 16.0
PEAK = 32000.0


def which(offsets, shift):
    return sum(
        jnp.where(offsets[k] == shift, jnp.int32(k), jnp.int32(0)) for k in range(offsets.shape[0])
    )


def split(value):
    high = value.astype(jnp.bfloat16)
    low = (value - high.astype(jnp.float32)).astype(jnp.bfloat16)
    return high, low


SMEM = pl.BlockSpec(memory_space=pltpu.SMEM)
VMEM = pl.BlockSpec(memory_space=pltpu.VMEM)
HBM = pl.BlockSpec(memory_space=pltpu.HBM)
ROWS = 64
CHUNKS = 3


def call(kernel, inputs, specs, outs, scratch=(), out_specs=None, aliases=None):
    return pl.pallas_call(
        kernel,
        in_specs=specs,
        out_specs=out_specs or [VMEM] * len(outs),
        out_shape=[jax.ShapeDtypeStruct(x.shape, x.dtype) for x in outs],
        scratch_shapes=scratch,
        input_output_aliases=aliases or {},
        compiler_params=pltpu.CompilerParams(vmem_limit_bytes=32 * 2**20),
        cost_estimate=pl.CostEstimate(flops=0, bytes_accessed=0, transcendentals=0),
        name=(kernel.func if isinstance(kernel, functools.partial) else kernel).__name__,
    )(*inputs)


def ownership(count):
    pairs = count // 2
    return pairs, count % 2, 2 * pairs + count % 2


def units_of(core, count):
    pairs, odd, _ = ownership(count)
    first = core * (pairs + odd)
    return [(first + i, c) for i in range(pairs) for c in range(2)] + [(pairs, core)] * odd


def sum_windows(number, plane_of, start, weights, cube, folded, order, ready=None):
    bands, lines, cols = cube.shape
    window = weights.shape[1]
    group = math.gcd(SPB, bands)
    first = bands * lax.axis_index("band")
    places = [SPB * start[plane_of(i)] - first for i in range(number)]
    ranks = [jnp.int32(0)] * number
    for m in range(number):
        for n in range(m + 1, number):
            later = (places[n] < places[m]).astype(jnp.int32)
            ranks[m] = ranks[m] + later
            ranks[n] = ranks[n] + (1 - later)
    before = jnp.int32(0)
    until = jnp.int32(0)
    for m in range(number):
        order[ranks[m]] = jnp.int32(m)
        before = before + (places[m] <= -window).astype(jnp.int32)
        until = until + (places[m] < bands).astype(jnp.int32)

    def clear(n, carry):
        folded[order[n]] = jnp.zeros((lines, cols), jnp.float32)
        return carry

    lax.fori_loop(0, before, clear, 0)
    lax.fori_loop(until, number, clear, 0)

    def one(n, arrived):
        i = order[n]
        m = plane_of(i)
        low = SPB * start[m] - first
        stop = jnp.minimum(low + window, bands)
        needed = lax.div(stop - 1, jnp.int32(window)) + 1
        if ready is not None:
            ready(arrived, needed)
        whole = jnp.logical_and(low >= 0, low + window <= bands)

        def term(band, weight, r):
            return weight * cube[band, r : r + ROWS, :].astype(jnp.float32)

        @pl.when(whole)
        def _():
            for r in range(0, lines, ROWS):
                total = term(low, weights[m, 0], r)
                for j in range(1, window):
                    total = total + term(low + j, weights[m, j], r)
                folded[i, r : r + ROWS, :] = total

        @pl.when(jnp.logical_not(whole))
        def _():
            begin = jnp.maximum(low, 0)
            for r in range(0, lines, ROWS):

                def some(t, total):
                    for k in range(group):
                        band = begin + t * group + k
                        total = total + term(band, weights[m, band - low], r)
                    return total

                folded[i, r : r + ROWS, :] = lax.fori_loop(
                    0,
                    lax.div(stop - begin, jnp.int32(group)),
                    some,
                    jnp.zeros((ROWS, cols), jnp.float32),
                )

        return jnp.maximum(arrived, needed)

    return lax.fori_loop(before, until, one, jnp.int32(0))


def across(value, table):
    planes, lines, cols = value.shape
    both = jnp.concatenate(split(value.reshape(planes * lines, cols)), axis=1)
    made = jnp.dot(both, table, preferred_element_type=jnp.float32)
    return made.reshape(planes, lines, cols)


def spread_out(made, out):
    half = made.shape[2] // 2
    for i in range(made.shape[0]):
        out[2 * i] = made[i, :, :half]
        out[2 * i + 1] = made[i, :, half:]


def fold_other(
    start_in,
    offsets_in,
    values_in,
    blocks_in,
    along_offsets_in,
    along_blocks_in,
    cube_in,
    send,
    middle,
    cube,
    wide,
    table,
    picked,
    start,
    offsets,
    values,
    weights,
    blocks,
    along_offsets,
    along_blocks,
    folded,
    order,
    small,
    large,
):
    bands, lines, cols = cube.shape
    count, window = values.shape
    half = cols // 2
    planes, odd, units = ownership(count)
    me = lax.axis_index("band")
    pairs = (
        (start_in, start),
        (values_in, values),
        (offsets_in, offsets),
        (blocks_in, blocks),
        (along_offsets_in, along_offsets),
        (along_blocks_in, along_blocks),
    )
    copies = [pltpu.make_async_copy(a, b, small.at[i]) for i, (a, b) in enumerate(pairs)]
    chunks = -(-bands // window)
    last = bands - (chunks - 1) * window

    def arrive(q, size):
        at = pl.ds(q * window, size)
        return pltpu.make_async_copy(cube_in.at[at], cube.at[at], large.at[q])

    for copy in copies:
        copy.start()
    for q in range(chunks):
        arrive(q, window if q < chunks - 1 else last).start()
    copies[1].wait()
    wide[...] = values[...].astype(jnp.float32)
    spread = pltpu.make_async_copy(wide, weights, small.at[len(pairs)])
    spread.start()
    for copy in copies[:1] + copies[2:]:
        copy.wait()
    for r in range(2):
        for c in range(2):
            block = blocks[which(offsets, jnp.int32(r - c))].astype(jnp.float32).T
            for top in (0, cols):
                at = slice(top + r * half, top + (r + 1) * half)
                table[at, c * half : (c + 1) * half] = block.astype(jnp.bfloat16)
    step = side_step()
    for i, shift in enumerate((jnp.int32(0), step, -step)):
        picked[i] = along_blocks[which(along_offsets, shift)]
    spread.wait()

    def one(q, carry):
        pl.when(q < chunks - 1)(lambda: arrive(q, window).wait())
        pl.when(q == chunks - 1)(lambda: arrive(chunks - 1, last).wait())
        return carry

    def ready(a, b):
        lax.fori_loop(a, b, one, 0)

    base = (1 - me) * (planes + odd)

    def plane_of(i):
        return jnp.where(i == planes, planes, base + i) if odd else base + i

    arrived = sum_windows(planes + odd, plane_of, start, weights, cube, folded, order, ready)
    ready(arrived, chunks)
    made = across(folded[...], table[...])
    spread_out(made[:planes], send)
    if odd:
        left, right = made[planes, :, :half], made[planes, :, half:]
        middle[0] = jnp.where(me == 0, left, right)
        send[units - 1] = jnp.where(me == 0, right, left)


def fold_own(start_in, wide, cube, table, middle, keep, start, weights, folded, order, sems):
    planes, odd, units = ownership(wide.shape[0])
    copies = [
        pltpu.make_async_copy(start_in, start, sems.at[0]),
        pltpu.make_async_copy(wide, weights, sems.at[1]),
    ]
    for copy in copies:
        copy.start()
    for copy in copies:
        copy.wait()
    base = lax.axis_index("band") * (planes + odd)
    sum_windows(planes, lambda i: base + i, start, weights, cube, folded, order)
    spread_out(across(folded[...], table[...]), keep)
    if odd:
        keep[units - 1] = middle[0]


def coded_rows(count, lines):
    return count * lines + -(-count // 16) * 16


def encode(source, span, message):
    _, lines, half = source.shape
    units = span[1] - span[0]
    largest = jnp.max(jnp.abs(source[span[0] : span[1]]), axis=1)
    level = jnp.ceil(jnp.log2(jnp.maximum(largest, 1e-30)) * STEPS)
    factor = PEAK * jnp.exp2(level * (-1.0 / STEPS))
    for m in range(units):
        coded = jnp.floor(source[span[0] + m] * factor[m : m + 1, :] + 0.5).astype(jnp.int32)
        message[m * lines : (m + 1) * lines, :] = coded.astype(jnp.int16)
    spare = message.shape[0] - units * lines - units
    level = jnp.concatenate([level, jnp.zeros((spare, half), jnp.float32)], axis=0)
    message[units * lines :, :] = level.astype(jnp.int32).astype(jnp.int16)


def decode(message, span, lines, valid=True):
    units = span[1] - span[0]
    level = message[units * lines :, :].astype(jnp.int32).astype(jnp.float32)
    scale = jnp.where(valid, jnp.exp2(level * (1.0 / STEPS)) * (1.0 / PEAK), 0.0)

    def plane(m):
        coded = message[m * lines : (m + 1) * lines, :].astype(jnp.int32).astype(jnp.float32)
        return coded * scale[m : m + 1, :]

    return plane


def blurred(filters, count, plane, put):
    wide = jnp.concatenate([filters, filters], axis=1)
    for m in range(0, count, 2):
        parts = [split(plane(n)) for n in range(m, min(m + 2, count))]
        high = jnp.concatenate([p[0] for p in parts], axis=1)
        low = jnp.concatenate([p[1] for p in parts], axis=1)
        made = jnp.dot(
            wide, jnp.concatenate([high, low], axis=0), preferred_element_type=jnp.float32
        )
        half = made.shape[1] // len(parts)
        for i in range(len(parts)):
            put(m + i, made[:, i * half : (i + 1) * half])


def side_step():
    return jnp.where(lax.axis_index("line") % 2 == 0, jnp.int32(1), jnp.int32(-1))


def outside(*lines):
    return functools.reduce(jnp.logical_or, [lax.axis_index("line") == i for i in lines])


def by_core(zero, one):
    me = lax.axis_index("band")
    pl.when(me == 0)(zero)
    pl.when(me != 0)(one)


def share(span, picked, keep, other, total, message, product):
    units = span[1] - span[0]
    total[...] = keep[slice(*span)] + other[slice(*span)]

    def summing():
        def put(m, value):
            product[m] = value

        blurred(picked[1], units, lambda m: total[m], put)
        encode(product, (0, units), message)

    by_core(lambda: encode(total, (0, units), message), summing)


def centre(spans, picked, *rest):
    totals, (base, term) = rest[:-2], rest[-2:]

    def work(block, out):
        for span, total in zip(spans, totals):

            def put(m, value):
                out[span[0] + m] = value

            blurred(block, span[1] - span[0], lambda m: total[m], put)

    work(picked[0], base)
    pl.when(lax.axis_index("band") != 0)(lambda: work(picked[2], term))


def relay(span, term, received, message, total):
    def forward():
        message[...] = received[...]

    def add():
        missing = outside(1, lax.axis_size("line") - 2)
        plane = decode(received, span, term.shape[1], jnp.logical_not(missing))
        for m in range(*span):
            total[m] = term[m] + plane(m - span[0])
        encode(total, span, message)

    by_core(forward, add)


def beside(span, picked, base, near, product):
    units, lines, _ = product.shape

    def put(m, value):
        product[m] = base[span[0] + m] + value

    plane = decode(near, span, lines)
    pl.when(lax.axis_index("band") == 0)(lambda: blurred(picked[1], units, plane, put))


def settle(span, picked, base, product, received, message, total):
    units, lines, _ = product.shape

    def put(m, value):
        total[m] = product[m] + value

    def spreading():
        missing = outside(0, lax.axis_size("line") - 1)
        plane = decode(received, span, lines, jnp.logical_not(missing))
        blurred(picked[2], units, plane, put)

    def summing():
        plane = decode(received, span, lines)
        for m in range(units):
            total[m] = base[span[0] + m] + plane(m)

    by_core(spreading, summing)
    encode(total, (0, units), message)


def arccos(x):
    size = jnp.abs(x)
    big = size > 0.5
    z = jnp.where(big, 0.5 * (1.0 - size), size * size)
    root = jnp.where(big, jnp.sqrt(z), size)
    poly = 4.2163199048e-2
    for term in (2.4181311049e-2, 4.5470025998e-2, 7.4953002686e-2, 1.6666752422e-1):
        poly = poly * z + term
    arcsin = poly * z * root + root
    pi = 3.14159265358979
    inner = jnp.where(x < 0, 0.5 * pi + arcsin, 0.5 * pi - arcsin)
    outer = jnp.where(x < 0, pi - 2.0 * arcsin, 2.0 * arcsin)
    return jnp.where(big, outer, inner)


def finish_units(core, parts, observed, value, image, sem, sums):
    _, lines, half = value.shape
    copies = []
    for span, message in parts:
        plane = decode(message, span, lines)
        for n in range(*span):
            m, c = units_of(core, observed.shape[0])[n]
            at = slice(c * half, (c + 1) * half)
            made = plane(n - span[0])
            value[n] = made
            copies.append(pltpu.make_async_copy(value.at[n], image.at[m, :, at], sem(n)))
            copies[-1].start()
            seen = observed[m, :, at].astype(jnp.float32)
            sums[c] = (sums[c][0] + made * seen, sums[c][1] + made * made)
    return copies


def finish_most(spans, observed, *rest):
    chunks = len(spans)
    messages, others, rest = rest[:chunks], rest[chunks : 2 * chunks - 1], rest[2 * chunks - 1 :]
    image, own, theirs, value, other_value, sems = rest
    units, lines, half = value.shape
    zero = jnp.zeros((lines, half), jnp.float32)

    def work(core):
        sums, other_sums = [(zero, zero)] * 2, [(zero, zero)] * 2
        parts = list(zip(spans, messages))
        copies = finish_units(
            core, parts, observed, value, image, lambda n: sems.at[n], sums
        )
        parts = list(zip(spans[:-1], others))
        copies += finish_units(
            1 - core,
            parts,
            observed,
            other_value,
            image,
            lambda n: sems.at[units + n],
            other_sums,
        )
        for c in range(2):
            at = slice(c * half, (c + 1) * half)
            right = zero
            for m in range(observed.shape[0]):
                seen = observed[m, :, at].astype(jnp.float32)
                right = right + seen * seen
            own[0, :, at], own[1, :, at] = sums[c]
            own[2, :, at] = jnp.sqrt(right)
            theirs[0, :, at], theirs[1, :, at] = other_sums[c]
        for copy in copies:
            copy.wait()

    by_core(lambda: work(0), lambda: work(1))


def finish_last(span, observed, message, own, theirs, _, *rest):
    image, angles, angle, value, sems = rest
    units, lines, half = value.shape

    def work(core):
        columns = [slice(c * half, (c + 1) * half) for c in range(2)]
        sums = [(theirs[0, :, at], theirs[1, :, at]) for at in columns]
        copies = finish_units(
            core,
            [(span, message)],
            observed,
            value,
            image,
            lambda n: sems.at[n],
            sums,
        )
        for (inner, left), at in zip(sums, columns):
            bound = jnp.sqrt(left + own[1, :, at]) * own[2, :, at]
            ratio = (inner + own[0, :, at]) / jnp.maximum(bound, 1.0)
            angle[:, at] = arccos(jnp.clip(ratio, -1.0, 1.0))
        copies.append(pltpu.make_async_copy(angle, angles, sems.at[units]))
        copies[-1].start()
        for copy in copies:
            copy.wait()

    by_core(lambda: work(1), lambda: work(0))


def on_device(
    cube,
    observed,
    along_kernels,
    along_offsets,
    across_kernels,
    across_offsets,
    resp_start,
    resp_values,
):
    f32, i16 = jnp.float32, jnp.int16
    size = lax.axis_size("line")
    bands, lines, cols = cube.shape
    count = resp_values.shape[0]
    half = cols // 2
    _, _, units = ownership(count)
    shape = jax.ShapeDtypeStruct
    swap = [(0, 1), (1, 0)]
    partner = [(i, i ^ 1) for i in range(size)]
    even_up = [(i, (i + 2 - 4 * (i % 2)) % size) for i in range(size)]
    odd_up = [(j, i) for i, j in even_up]

    def cores(zero, one):
        return [(2 * a, 2 * b) for a, b in zero] + [(2 * a + 1, 2 * b + 1) for a, b in one]

    part = shape((units, lines, half), f32)
    edges = [-(-units * i // CHUNKS) for i in range(CHUNKS + 1)]
    spans = list(zip(edges[:-1], edges[1:]))
    coded = [shape((coded_rows(b - a, lines), half), i16) for a, b in spans]

    inputs = (
        resp_start,
        across_offsets,
        resp_values,
        across_kernels,
        along_offsets,
        along_kernels,
        cube,
    )
    inputs = [pltpu.with_memory_space_constraint(x, pltpu.HBM) for x in inputs]
    planes, odd, _ = ownership(count)
    wide = shape(resp_values.shape, f32)
    table = shape((2 * cols, cols), across_kernels.dtype)
    send, middle, local, wide, table, picked = call(
        fold_other,
        inputs,
        [HBM] * len(inputs),
        [part, shape((1, lines, half), f32), cube, wide, table, along_kernels],
        scratch=[
            pltpu.SMEM(resp_start.shape, jnp.int32),
            pltpu.SMEM(across_offsets.shape, jnp.int32),
            pltpu.VMEM(resp_values.shape, resp_values.dtype),
            pltpu.SMEM(resp_values.shape, f32),
            pltpu.VMEM(across_kernels.shape, across_kernels.dtype),
            pltpu.SMEM(along_offsets.shape, jnp.int32),
            pltpu.VMEM(along_kernels.shape, along_kernels.dtype),
            pltpu.VMEM((planes + odd, lines, cols), f32),
            pltpu.SMEM((count,), jnp.int32),
            pltpu.SemaphoreType.DMA((len(inputs),)),
            pltpu.SemaphoreType.DMA((-(-bands // resp_values.shape[1]),)),
        ],
    )
    (keep,) = call(
        fold_own,
        (inputs[0], wide, local, table, middle),
        [HBM] + [VMEM] * 4,
        [part],
        scratch=[
            pltpu.SMEM(resp_start.shape, jnp.int32),
            pltpu.SMEM(resp_values.shape, f32),
            pltpu.VMEM((planes, lines, cols), f32),
            pltpu.SMEM((count,), jnp.int32),
            pltpu.SemaphoreType.DMA((2,)),
        ],
    )
    work = [pltpu.VMEM(part.shape, f32)]
    other = lax.ppermute(send, "band", swap)
    totals, near = [], []
    for i, span in enumerate(spans):
        planes = shape((span[1] - span[0], lines, half), f32)
        total, message = call(
            functools.partial(share, span),
            (picked, keep, other),
            [VMEM] * 3,
            [planes, coded[i]],
            scratch=[pltpu.VMEM(planes.shape, f32)],
        )
        totals.append(total)
        near.append(lax.ppermute(message, ("line", "band"), cores(partner, odd_up)))
    base, term = call(
        functools.partial(centre, spans),
        (picked, *totals),
        [VMEM] * (1 + len(spans)),
        [part] * 2,
    )
    far, product = [], []
    for i, span in enumerate(spans):
        (message,) = call(
            functools.partial(relay, span), (term, near[i]), [VMEM] * 2, [coded[i]], scratch=work
        )
        message, near[i] = lax.optimization_barrier((message, near[i]))
        far.append(lax.ppermute(message, ("line", "band"), cores(even_up, partner)))
        planes = shape((span[1] - span[0], lines, half), f32)
        product += call(
            functools.partial(beside, span),
            (picked, base, near[i]),
            [VMEM] * 3,
            [planes],
        )
    messages, others = [], []
    for i, span in enumerate(spans):
        planes = product[i].shape
        messages += call(
            functools.partial(settle, span),
            (picked, base, product[i], far[i]),
            [VMEM] * 4,
            [coded[i]],
            scratch=[pltpu.VMEM(planes, f32)],
        )
        others.append(lax.ppermute(messages[i], "band", swap))
    image = shape((count, lines, cols), f32)
    three = shape((3, lines, cols), f32)
    inputs = [observed, *messages, *others[:-1]]
    image, own, theirs = call(
        functools.partial(finish_most, spans),
        inputs,
        [VMEM] * len(inputs),
        [image, three, three],
        scratch=work * 2 + [pltpu.SemaphoreType.DMA((2 * units,))],
        out_specs=[HBM, VMEM, VMEM],
    )
    image, angles = call(
        functools.partial(finish_last, spans[-1]),
        (observed, others[-1], own, theirs, image),
        [VMEM] * 4 + [HBM],
        [image, shape((lines, cols), f32)],
        scratch=[pltpu.VMEM((lines, cols), f32), *work, pltpu.SemaphoreType.DMA((units + 1,))],
        out_specs=[HBM] * 2,
        aliases={4: 0},
    )
    return image, angles


def solution(mesh):
    placed = (
        P("band", ("slab", "line"), None),
        P(None, ("slab", "line"), None),
        P(),
        P(),
        P(),
        P(),
        P(),
        P(),
    )
    return jax.shard_map(
        on_device,
        mesh=mesh,
        in_specs=placed,
        out_specs=(P(None, ("slab", "line"), None), P(("slab", "line"), None)),
        check_vma=False,
    )
```

```python
import functools
import math

import jax
import jax.numpy as jnp
from jax import lax
from jax.experimental import pallas as pl
from jax.experimental.pallas import tpu as pltpu
from jax.sharding import PartitionSpec as P

BLK = 128
SPB = 10
STEPS = 16.0
PEAK = 32000.0


def which(offsets, shift):
    return sum(
        jnp.where(offsets[k] == shift, jnp.int32(k), jnp.int32(0)) for k in range(offsets.shape[0])
    )


def split(value):
    high = value.astype(jnp.bfloat16)
    low = (value - high.astype(jnp.float32)).astype(jnp.bfloat16)
    return high, low


SMEM = pl.BlockSpec(memory_space=pltpu.SMEM)
VMEM = pl.BlockSpec(memory_space=pltpu.VMEM)
HBM = pl.BlockSpec(memory_space=pltpu.HBM)
ROWS = 64
CHUNKS = 3


def call(kernel, inputs, specs, outs, scratch=(), out_specs=None, aliases=None):
    return pl.pallas_call(
        kernel,
        in_specs=specs,
        out_specs=out_specs or [VMEM] * len(outs),
        out_shape=[jax.ShapeDtypeStruct(x.shape, x.dtype) for x in outs],
        scratch_shapes=scratch,
        input_output_aliases=aliases or {},
        compiler_params=pltpu.CompilerParams(vmem_limit_bytes=32 * 2**20),
        cost_estimate=pl.CostEstimate(flops=0, bytes_accessed=0, transcendentals=0),
        name=(kernel.func if isinstance(kernel, functools.partial) else kernel).__name__,
    )(*inputs)


def ownership(count):
    pairs = count // 2
    return pairs, count % 2, 2 * pairs + count % 2


def units_of(core, count):
    pairs, odd, _ = ownership(count)
    first = core * (pairs + odd)
    return [(first + i, c) for i in range(pairs) for c in range(2)] + [(pairs, core)] * odd


def sum_windows(number, plane_of, start, weights, cube, folded, order, ready=None):
    bands, lines, cols = cube.shape
    window = weights.shape[1]
    group = math.gcd(SPB, bands)
    first = bands * lax.axis_index("band")
    places = [SPB * start[plane_of(i)] - first for i in range(number)]
    ranks = [jnp.int32(0)] * number
    for m in range(number):
        for n in range(m + 1, number):
            later = (places[n] < places[m]).astype(jnp.int32)
            ranks[m] = ranks[m] + later
            ranks[n] = ranks[n] + (1 - later)
    before = jnp.int32(0)
    until = jnp.int32(0)
    for m in range(number):
        order[ranks[m]] = jnp.int32(m)
        before = before + (places[m] <= -window).astype(jnp.int32)
        until = until + (places[m] < bands).astype(jnp.int32)

    def clear(n, carry):
        folded[order[n]] = jnp.zeros((lines, cols), jnp.float32)
        return carry

    lax.fori_loop(0, before, clear, 0)
    lax.fori_loop(until, number, clear, 0)

    def one(n, arrived):
        i = order[n]
        m = plane_of(i)
        low = SPB * start[m] - first
        stop = jnp.minimum(low + window, bands)
        needed = lax.div(stop - 1, jnp.int32(window)) + 1
        if ready is not None:
            ready(arrived, needed)
        whole = jnp.logical_and(low >= 0, low + window <= bands)

        def term(band, weight, r):
            return weight * cube[band, r : r + ROWS, :].astype(jnp.float32)

        @pl.when(whole)
        def _():
            for r in range(0, lines, ROWS):
                total = term(low, weights[m, 0], r)
                for j in range(1, window):
                    total = total + term(low + j, weights[m, j], r)
                folded[i, r : r + ROWS, :] = total

        @pl.when(jnp.logical_not(whole))
        def _():
            begin = jnp.maximum(low, 0)
            for r in range(0, lines, ROWS):

                def some(t, total):
                    for k in range(group):
                        band = begin + t * group + k
                        total = total + term(band, weights[m, band - low], r)
                    return total

                folded[i, r : r + ROWS, :] = lax.fori_loop(
                    0,
                    lax.div(stop - begin, jnp.int32(group)),
                    some,
                    jnp.zeros((ROWS, cols), jnp.float32),
                )

        return jnp.maximum(arrived, needed)

    return lax.fori_loop(before, until, one, jnp.int32(0))


def across(value, table):
    planes, lines, cols = value.shape
    both = jnp.concatenate(split(value.reshape(planes * lines, cols)), axis=1)
    made = jnp.dot(both, table, preferred_element_type=jnp.float32)
    return made.reshape(planes, lines, cols)


def spread_out(made, put):
    half = made.shape[2] // 2
    for i in range(made.shape[0]):
        put(2 * i, made[i, :, :half])
        put(2 * i + 1, made[i, :, half:])


def fold_other(
    start_in,
    offsets_in,
    values_in,
    blocks_in,
    along_offsets_in,
    along_blocks_in,
    cube_in,
    send,
    send_rest,
    middle,
    cube,
    wide,
    table,
    picked,
    start,
    offsets,
    values,
    weights,
    blocks,
    along_offsets,
    along_blocks,
    folded,
    order,
    small,
    large,
):
    bands, lines, cols = cube.shape
    count, window = values.shape
    half = cols // 2
    planes, odd, units = ownership(count)
    me = lax.axis_index("band")
    pairs = (
        (start_in, start),
        (values_in, values),
        (offsets_in, offsets),
        (blocks_in, blocks),
        (along_offsets_in, along_offsets),
        (along_blocks_in, along_blocks),
    )
    copies = [pltpu.make_async_copy(a, b, small.at[i]) for i, (a, b) in enumerate(pairs)]
    chunks = -(-bands // window)
    last = bands - (chunks - 1) * window

    def arrive(q, size):
        at = pl.ds(q * window, size)
        return pltpu.make_async_copy(cube_in.at[at], cube.at[at], large.at[q])

    for copy in copies:
        copy.start()
    for q in range(chunks):
        arrive(q, window if q < chunks - 1 else last).start()
    copies[1].wait()
    wide[...] = values[...].astype(jnp.float32)
    spread = pltpu.make_async_copy(wide, weights, small.at[len(pairs)])
    spread.start()
    for copy in copies[:1] + copies[2:]:
        copy.wait()
    for r in range(2):
        for c in range(2):
            block = blocks[which(offsets, jnp.int32(r - c))].astype(jnp.float32).T
            for top in (0, cols):
                at = slice(top + r * half, top + (r + 1) * half)
                table[at, c * half : (c + 1) * half] = block.astype(jnp.bfloat16)
    step = side_step()
    for i, shift in enumerate((jnp.int32(0), step, -step)):
        picked[i] = along_blocks[which(along_offsets, shift)]
    spread.wait()

    def one(q, carry):
        pl.when(q < chunks - 1)(lambda: arrive(q, window).wait())
        pl.when(q == chunks - 1)(lambda: arrive(chunks - 1, last).wait())
        return carry

    def ready(a, b):
        lax.fori_loop(a, b, one, 0)

    base = (1 - me) * (planes + odd)

    def plane_of(i):
        return jnp.where(i == planes, planes, base + i) if odd else base + i

    arrived = sum_windows(planes + odd, plane_of, start, weights, cube, folded, order, ready)
    ready(arrived, chunks)
    made = across(folded[...], table[...])

    def put(n, value):
        if n < send.shape[0]:
            send[n] = value
        else:
            send_rest[n - send.shape[0]] = value

    spread_out(made[:planes], put)
    if odd:
        left, right = made[planes, :, :half], made[planes, :, half:]
        middle[0] = jnp.where(me == 0, left, right)
        put(units - 1, jnp.where(me == 0, right, left))


def fold_own(start_in, wide, cube, table, middle, keep, start, weights, folded, order, sems):
    planes, odd, units = ownership(wide.shape[0])
    copies = [
        pltpu.make_async_copy(start_in, start, sems.at[0]),
        pltpu.make_async_copy(wide, weights, sems.at[1]),
    ]
    for copy in copies:
        copy.start()
    for copy in copies:
        copy.wait()
    base = lax.axis_index("band") * (planes + odd)
    sum_windows(planes, lambda i: base + i, start, weights, cube, folded, order)

    def put(n, value):
        keep[n] = value

    spread_out(across(folded[...], table[...]), put)
    if odd:
        keep[units - 1] = middle[0]


def coded_rows(count, lines):
    return count * lines + -(-count // 16) * 16


def encode(source, span, message):
    _, lines, half = source.shape
    units = span[1] - span[0]
    largest = jnp.max(jnp.abs(source[span[0] : span[1]]), axis=1)
    level = jnp.ceil(jnp.log2(jnp.maximum(largest, 1e-30)) * STEPS)
    factor = PEAK * jnp.exp2(level * (-1.0 / STEPS))
    for m in range(units):
        coded = jnp.floor(source[span[0] + m] * factor[m : m + 1, :] + 0.5).astype(jnp.int32)
        message[m * lines : (m + 1) * lines, :] = coded.astype(jnp.int16)
    spare = message.shape[0] - units * lines - units
    level = jnp.concatenate([level, jnp.zeros((spare, half), jnp.float32)], axis=0)
    message[units * lines :, :] = level.astype(jnp.int32).astype(jnp.int16)


def decode(message, span, lines, valid=True):
    units = span[1] - span[0]
    level = message[units * lines :, :].astype(jnp.int32).astype(jnp.float32)
    scale = jnp.where(valid, jnp.exp2(level * (1.0 / STEPS)) * (1.0 / PEAK), 0.0)

    def plane(m):
        coded = message[m * lines : (m + 1) * lines, :].astype(jnp.int32).astype(jnp.float32)
        return coded * scale[m : m + 1, :]

    return plane


def blurred(filters, count, plane, put):
    wide = jnp.concatenate([filters, filters], axis=1)
    for m in range(0, count, 2):
        parts = [split(plane(n)) for n in range(m, min(m + 2, count))]
        high = jnp.concatenate([p[0] for p in parts], axis=1)
        low = jnp.concatenate([p[1] for p in parts], axis=1)
        made = jnp.dot(
            wide, jnp.concatenate([high, low], axis=0), preferred_element_type=jnp.float32
        )
        half = made.shape[1] // len(parts)
        for i in range(len(parts)):
            put(m + i, made[:, i * half : (i + 1) * half])


def side_step():
    return jnp.where(lax.axis_index("line") % 2 == 0, jnp.int32(1), jnp.int32(-1))


def outside(*lines):
    return functools.reduce(jnp.logical_or, [lax.axis_index("line") == i for i in lines])


def by_core(zero, one):
    me = lax.axis_index("band")
    pl.when(me == 0)(zero)
    pl.when(me != 0)(one)


def share(span, begin, picked, keep, other, total, message, product):
    units = span[1] - span[0]
    total[...] = keep[slice(*span)] + other[span[0] - begin : span[1] - begin]

    def summing():
        def put(m, value):
            product[m] = value

        blurred(picked[1], units, lambda m: total[m], put)
        encode(product, (0, units), message)

    by_core(lambda: encode(total, (0, units), message), summing)


def centre(spans, picked, *rest):
    totals, (base, term) = rest[:-2], rest[-2:]

    def work(block, out):
        for span, total in zip(spans, totals):

            def put(m, value):
                out[span[0] + m] = value

            blurred(block, span[1] - span[0], lambda m: total[m], put)

    work(picked[0], base)
    pl.when(lax.axis_index("band") != 0)(lambda: work(picked[2], term))


def relay(span, term, received, message, total):
    def forward():
        message[...] = received[...]

    def add():
        missing = outside(1, lax.axis_size("line") - 2)
        plane = decode(received, span, term.shape[1], jnp.logical_not(missing))
        for m in range(*span):
            total[m] = term[m] + plane(m - span[0])
        encode(total, span, message)

    by_core(forward, add)


def beside(span, picked, base, near, product):
    units, lines, _ = product.shape

    def put(m, value):
        product[m] = base[span[0] + m] + value

    plane = decode(near, span, lines)
    pl.when(lax.axis_index("band") == 0)(lambda: blurred(picked[1], units, plane, put))


def settle(span, picked, base, product, received, message, total):
    units, lines, _ = product.shape

    def put(m, value):
        total[m] = product[m] + value

    def spreading():
        missing = outside(0, lax.axis_size("line") - 1)
        plane = decode(received, span, lines, jnp.logical_not(missing))
        blurred(picked[2], units, plane, put)

    def summing():
        plane = decode(received, span, lines)
        for m in range(units):
            total[m] = base[span[0] + m] + plane(m)

    by_core(spreading, summing)
    encode(total, (0, units), message)


def arccos(x):
    size = jnp.abs(x)
    big = size > 0.5
    z = jnp.where(big, 0.5 * (1.0 - size), size * size)
    root = jnp.where(big, jnp.sqrt(z), size)
    poly = 4.2163199048e-2
    for term in (2.4181311049e-2, 4.5470025998e-2, 7.4953002686e-2, 1.6666752422e-1):
        poly = poly * z + term
    arcsin = poly * z * root + root
    pi = 3.14159265358979
    inner = jnp.where(x < 0, 0.5 * pi + arcsin, 0.5 * pi - arcsin)
    outer = jnp.where(x < 0, pi - 2.0 * arcsin, 2.0 * arcsin)
    return jnp.where(big, outer, inner)


def finish_units(core, parts, observed, value, image, sem, sums):
    _, lines, half = value.shape
    copies = []
    for span, message in parts:
        plane = decode(message, span, lines)
        for n in range(*span):
            m, c = units_of(core, observed.shape[0])[n]
            at = slice(c * half, (c + 1) * half)
            made = plane(n - span[0])
            value[n] = made
            copies.append(pltpu.make_async_copy(value.at[n], image.at[m, :, at], sem(n)))
            copies[-1].start()
            seen = observed[m, :, at].astype(jnp.float32)
            sums[c] = (sums[c][0] + made * seen, sums[c][1] + made * made)
    return copies


def finish_most(spans, observed, *rest):
    chunks = len(spans)
    messages, others, rest = rest[:chunks], rest[chunks : 2 * chunks - 1], rest[2 * chunks - 1 :]
    image, own, theirs, value, other_value, sems = rest
    units, lines, half = value.shape
    zero = jnp.zeros((lines, half), jnp.float32)

    def work(core):
        sums, other_sums = [(zero, zero)] * 2, [(zero, zero)] * 2
        parts = list(zip(spans, messages))
        copies = finish_units(
            core, parts, observed, value, image, lambda n: sems.at[n], sums
        )
        parts = list(zip(spans[:-1], others))
        copies += finish_units(
            1 - core,
            parts,
            observed,
            other_value,
            image,
            lambda n: sems.at[units + n],
            other_sums,
        )
        for c in range(2):
            at = slice(c * half, (c + 1) * half)
            right = zero
            for m in range(observed.shape[0]):
                seen = observed[m, :, at].astype(jnp.float32)
                right = right + seen * seen
            own[0, :, at], own[1, :, at] = sums[c]
            own[2, :, at] = jnp.sqrt(right)
            theirs[0, :, at], theirs[1, :, at] = other_sums[c]
        for copy in copies:
            copy.wait()

    by_core(lambda: work(0), lambda: work(1))


def finish_last(span, observed, message, own, theirs, _, *rest):
    image, angles, angle, value, sems = rest
    units, lines, half = value.shape

    def work(core):
        columns = [slice(c * half, (c + 1) * half) for c in range(2)]
        sums = [(theirs[0, :, at], theirs[1, :, at]) for at in columns]
        copies = finish_units(
            core,
            [(span, message)],
            observed,
            value,
            image,
            lambda n: sems.at[n],
            sums,
        )
        for (inner, left), at in zip(sums, columns):
            bound = jnp.sqrt(left + own[1, :, at]) * own[2, :, at]
            ratio = (inner + own[0, :, at]) / jnp.maximum(bound, 1.0)
            angle[:, at] = arccos(jnp.clip(ratio, -1.0, 1.0))
        copies.append(pltpu.make_async_copy(angle, angles, sems.at[units]))
        copies[-1].start()
        for copy in copies:
            copy.wait()

    by_core(lambda: work(1), lambda: work(0))


def on_device(
    cube,
    observed,
    along_kernels,
    along_offsets,
    across_kernels,
    across_offsets,
    resp_start,
    resp_values,
):
    f32, i16 = jnp.float32, jnp.int16
    size = lax.axis_size("line")
    bands, lines, cols = cube.shape
    count = resp_values.shape[0]
    half = cols // 2
    _, _, units = ownership(count)
    shape = jax.ShapeDtypeStruct
    swap = [(0, 1), (1, 0)]
    partner = [(i, i ^ 1) for i in range(size)]
    even_up = [(i, (i + 2 - 4 * (i % 2)) % size) for i in range(size)]
    odd_up = [(j, i) for i, j in even_up]

    def cores(zero, one):
        return [(2 * a, 2 * b) for a, b in zero] + [(2 * a + 1, 2 * b + 1) for a, b in one]

    part = shape((units, lines, half), f32)
    edges = [-(-units * i // CHUNKS) for i in range(CHUNKS + 1)]
    spans = list(zip(edges[:-1], edges[1:]))
    coded = [shape((coded_rows(b - a, lines), half), i16) for a, b in spans]

    inputs = (
        resp_start,
        across_offsets,
        resp_values,
        across_kernels,
        along_offsets,
        along_kernels,
        cube,
    )
    inputs = [pltpu.with_memory_space_constraint(x, pltpu.HBM) for x in inputs]
    planes, odd, _ = ownership(count)
    wide = shape(resp_values.shape, f32)
    table = shape((2 * cols, cols), across_kernels.dtype)
    first = spans[-1][0]
    parts = [shape((n, lines, half), f32) for n in (first, units - first)]
    *sent, middle, local, wide, table, picked = call(
        fold_other,
        inputs,
        [HBM] * len(inputs),
        [*parts, shape((1, lines, half), f32), cube, wide, table, along_kernels],
        scratch=[
            pltpu.SMEM(resp_start.shape, jnp.int32),
            pltpu.SMEM(across_offsets.shape, jnp.int32),
            pltpu.VMEM(resp_values.shape, resp_values.dtype),
            pltpu.SMEM(resp_values.shape, f32),
            pltpu.VMEM(across_kernels.shape, across_kernels.dtype),
            pltpu.SMEM(along_offsets.shape, jnp.int32),
            pltpu.VMEM(along_kernels.shape, along_kernels.dtype),
            pltpu.VMEM((planes + odd, lines, cols), f32),
            pltpu.SMEM((count,), jnp.int32),
            pltpu.SemaphoreType.DMA((len(inputs),)),
            pltpu.SemaphoreType.DMA((-(-bands // resp_values.shape[1]),)),
        ],
    )
    (keep,) = call(
        fold_own,
        (inputs[0], wide, local, table, middle),
        [HBM] + [VMEM] * 4,
        [part],
        scratch=[
            pltpu.SMEM(resp_start.shape, jnp.int32),
            pltpu.SMEM(resp_values.shape, f32),
            pltpu.VMEM((planes, lines, cols), f32),
            pltpu.SMEM((count,), jnp.int32),
            pltpu.SemaphoreType.DMA((2,)),
        ],
    )
    work = [pltpu.VMEM(part.shape, f32)]
    other = [lax.ppermute(x, "band", swap) for x in sent]
    totals, near = [], []
    for i, span in enumerate(spans):
        planes = shape((span[1] - span[0], lines, half), f32)
        total, message = call(
            functools.partial(share, span, first * (span[0] >= first)),
            (picked, keep, other[span[0] >= first]),
            [VMEM] * 3,
            [planes, coded[i]],
            scratch=[pltpu.VMEM(planes.shape, f32)],
        )
        totals.append(total)
        near.append(lax.ppermute(message, ("line", "band"), cores(partner, odd_up)))
    base, term = call(
        functools.partial(centre, spans),
        (picked, *totals),
        [VMEM] * (1 + len(spans)),
        [part] * 2,
    )
    far, product = [], []
    for i, span in enumerate(spans):
        (message,) = call(
            functools.partial(relay, span), (term, near[i]), [VMEM] * 2, [coded[i]], scratch=work
        )
        message, near[i] = lax.optimization_barrier((message, near[i]))
        far.append(lax.ppermute(message, ("line", "band"), cores(even_up, partner)))
        planes = shape((span[1] - span[0], lines, half), f32)
        product += call(
            functools.partial(beside, span),
            (picked, base, near[i]),
            [VMEM] * 3,
            [planes],
        )
    messages, others = [], []
    for i, span in enumerate(spans):
        planes = product[i].shape
        messages += call(
            functools.partial(settle, span),
            (picked, base, product[i], far[i]),
            [VMEM] * 4,
            [coded[i]],
            scratch=[pltpu.VMEM(planes, f32)],
        )
        others.append(lax.ppermute(messages[i], "band", swap))
    image = shape((count, lines, cols), f32)
    three = shape((3, lines, cols), f32)
    inputs = [observed, *messages, *others[:-1]]
    image, own, theirs = call(
        functools.partial(finish_most, spans),
        inputs,
        [VMEM] * len(inputs),
        [image, three, three],
        scratch=work * 2 + [pltpu.SemaphoreType.DMA((2 * units,))],
        out_specs=[HBM, VMEM, VMEM],
    )
    image, angles = call(
        functools.partial(finish_last, spans[-1]),
        (observed, others[-1], own, theirs, image),
        [VMEM] * 4 + [HBM],
        [image, shape((lines, cols), f32)],
        scratch=[pltpu.VMEM((lines, cols), f32), *work, pltpu.SemaphoreType.DMA((units + 1,))],
        out_specs=[HBM] * 2,
        aliases={4: 0},
    )
    return image, angles


def solution(mesh):
    placed = (
        P("band", ("slab", "line"), None),
        P(None, ("slab", "line"), None),
        P(),
        P(),
        P(),
        P(),
        P(),
        P(),
    )
    return jax.shard_map(
        on_device,
        mesh=mesh,
        in_specs=placed,
        out_specs=(P(None, ("slab", "line"), None), P(("slab", "line"), None)),
        check_vma=False,
    )
```

```python
import functools
import math

import jax
import jax.numpy as jnp
from jax import lax
from jax.experimental import pallas as pl
from jax.experimental.pallas import tpu as pltpu
from jax.sharding import PartitionSpec as P

BLK = 128
SPB = 10
STEPS = 16.0
PEAK = 32000.0


def which(offsets, shift):
    return sum(
        jnp.where(offsets[k] == shift, jnp.int32(k), jnp.int32(0)) for k in range(offsets.shape[0])
    )


def split(value):
    high = value.astype(jnp.bfloat16)
    low = (value - high.astype(jnp.float32)).astype(jnp.bfloat16)
    return high, low


SMEM = pl.BlockSpec(memory_space=pltpu.SMEM)
VMEM = pl.BlockSpec(memory_space=pltpu.VMEM)
HBM = pl.BlockSpec(memory_space=pltpu.HBM)
ROWS = 64
CHUNKS = 3


def call(kernel, inputs, specs, outs, scratch=(), out_specs=None, aliases=None):
    return pl.pallas_call(
        kernel,
        in_specs=specs,
        out_specs=out_specs or [VMEM] * len(outs),
        out_shape=[jax.ShapeDtypeStruct(x.shape, x.dtype) for x in outs],
        scratch_shapes=scratch,
        input_output_aliases=aliases or {},
        compiler_params=pltpu.CompilerParams(vmem_limit_bytes=32 * 2**20),
        cost_estimate=pl.CostEstimate(flops=0, bytes_accessed=0, transcendentals=0),
        name=(kernel.func if isinstance(kernel, functools.partial) else kernel).__name__,
    )(*inputs)


def ownership(count):
    pairs = count // 2
    return pairs, count % 2, 2 * pairs + count % 2


def units_of(core, count):
    pairs, odd, _ = ownership(count)
    first = core * (pairs + odd)
    return [(first + i, c) for i in range(pairs) for c in range(2)] + [(pairs, core)] * odd


def sum_windows(number, plane_of, start, weights, cube, folded, order, ready=None):
    bands, lines, cols = cube.shape
    window = weights.shape[1]
    group = math.gcd(SPB, bands)
    first = bands * lax.axis_index("band")
    places = [SPB * start[plane_of(i)] - first for i in range(number)]
    ranks = [jnp.int32(0)] * number
    for m in range(number):
        for n in range(m + 1, number):
            later = (places[n] < places[m]).astype(jnp.int32)
            ranks[m] = ranks[m] + later
            ranks[n] = ranks[n] + (1 - later)
    before = jnp.int32(0)
    until = jnp.int32(0)
    for m in range(number):
        order[ranks[m]] = jnp.int32(m)
        before = before + (places[m] <= -window).astype(jnp.int32)
        until = until + (places[m] < bands).astype(jnp.int32)

    def clear(n, carry):
        folded[order[n]] = jnp.zeros((lines, cols), jnp.float32)
        return carry

    lax.fori_loop(0, before, clear, 0)
    lax.fori_loop(until, number, clear, 0)

    def one(n, arrived):
        i = order[n]
        m = plane_of(i)
        low = SPB * start[m] - first
        stop = jnp.minimum(low + window, bands)
        needed = lax.div(stop - 1, jnp.int32(window)) + 1
        if ready is not None:
            ready(arrived, needed)
        whole = jnp.logical_and(low >= 0, low + window <= bands)

        def term(band, weight, r):
            return weight * cube[band, r : r + ROWS, :].astype(jnp.float32)

        @pl.when(whole)
        def _():
            for r in range(0, lines, ROWS):
                total = term(low, weights[m, 0], r)
                for j in range(1, window):
                    total = total + term(low + j, weights[m, j], r)
                folded[i, r : r + ROWS, :] = total

        @pl.when(jnp.logical_not(whole))
        def _():
            begin = jnp.maximum(low, 0)
            for r in range(0, lines, ROWS):

                def some(t, total):
                    for k in range(group):
                        band = begin + t * group + k
                        total = total + term(band, weights[m, band - low], r)
                    return total

                folded[i, r : r + ROWS, :] = lax.fori_loop(
                    0,
                    lax.div(stop - begin, jnp.int32(group)),
                    some,
                    jnp.zeros((ROWS, cols), jnp.float32),
                )

        return jnp.maximum(arrived, needed)

    return lax.fori_loop(before, until, one, jnp.int32(0))


def across(value, table):
    planes, lines, cols = value.shape
    both = jnp.concatenate(split(value.reshape(planes * lines, cols)), axis=1)
    made = jnp.dot(both, table, preferred_element_type=jnp.float32)
    return made.reshape(planes, lines, cols)


def spread_out(made, out):
    half = made.shape[2] // 2
    for i in range(made.shape[0]):
        out[2 * i] = made[i, :, :half]
        out[2 * i + 1] = made[i, :, half:]


def fold_other(
    start_in,
    offsets_in,
    values_in,
    blocks_in,
    along_offsets_in,
    along_blocks_in,
    cube_in,
    send,
    middle,
    cube,
    wide,
    table,
    picked,
    start,
    offsets,
    values,
    weights,
    blocks,
    along_offsets,
    along_blocks,
    folded,
    order,
    small,
    large,
):
    bands, lines, cols = cube.shape
    count, window = values.shape
    half = cols // 2
    planes, odd, units = ownership(count)
    me = lax.axis_index("band")
    pairs = (
        (start_in, start),
        (values_in, values),
        (offsets_in, offsets),
        (blocks_in, blocks),
        (along_offsets_in, along_offsets),
        (along_blocks_in, along_blocks),
    )
    copies = [pltpu.make_async_copy(a, b, small.at[i]) for i, (a, b) in enumerate(pairs)]
    chunks = -(-bands // window)
    last = bands - (chunks - 1) * window

    def arrive(q, size):
        at = pl.ds(q * window, size)
        return pltpu.make_async_copy(cube_in.at[at], cube.at[at], large.at[q])

    for copy in copies:
        copy.start()
    for q in range(chunks):
        arrive(q, window if q < chunks - 1 else last).start()
    copies[1].wait()
    wide[...] = values[...].astype(jnp.float32)
    spread = pltpu.make_async_copy(wide, weights, small.at[len(pairs)])
    spread.start()
    for copy in copies[:1] + copies[2:]:
        copy.wait()
    for r in range(2):
        for c in range(2):
            block = blocks[which(offsets, jnp.int32(r - c))].astype(jnp.float32).T
            for top in (0, cols):
                at = slice(top + r * half, top + (r + 1) * half)
                table[at, c * half : (c + 1) * half] = block.astype(jnp.bfloat16)
    step = side_step()
    for i, shift in enumerate((jnp.int32(0), step, -step)):
        picked[i] = along_blocks[which(along_offsets, shift)]
    spread.wait()

    def one(q, carry):
        pl.when(q < chunks - 1)(lambda: arrive(q, window).wait())
        pl.when(q == chunks - 1)(lambda: arrive(chunks - 1, last).wait())
        return carry

    def ready(a, b):
        lax.fori_loop(a, b, one, 0)

    base = (1 - me) * (planes + odd)

    def plane_of(i):
        return jnp.where(i == planes, planes, base + i) if odd else base + i

    arrived = sum_windows(planes + odd, plane_of, start, weights, cube, folded, order, ready)
    ready(arrived, chunks)
    made = across(folded[...], table[...])
    spread_out(made[:planes], send)
    if odd:
        left, right = made[planes, :, :half], made[planes, :, half:]
        middle[0] = jnp.where(me == 0, left, right)
        send[units - 1] = jnp.where(me == 0, right, left)


def fold_own(start_in, wide, cube, table, middle, keep, start, weights, folded, order, sems):
    planes, odd, units = ownership(wide.shape[0])
    copies = [
        pltpu.make_async_copy(start_in, start, sems.at[0]),
        pltpu.make_async_copy(wide, weights, sems.at[1]),
    ]
    for copy in copies:
        copy.start()
    for copy in copies:
        copy.wait()
    base = lax.axis_index("band") * (planes + odd)
    sum_windows(planes, lambda i: base + i, start, weights, cube, folded, order)
    spread_out(across(folded[...], table[...]), keep)
    if odd:
        keep[units - 1] = middle[0]


def coded_rows(count, lines):
    return count * lines + -(-count // 16) * 16


def encode(source, span, message):
    _, lines, half = source.shape
    units = span[1] - span[0]
    largest = jnp.max(jnp.abs(source[span[0] : span[1]]), axis=1)
    level = jnp.ceil(jnp.log2(jnp.maximum(largest, 1e-30)) * STEPS)
    factor = PEAK * jnp.exp2(level * (-1.0 / STEPS))
    for m in range(units):
        coded = jnp.floor(source[span[0] + m] * factor[m : m + 1, :] + 0.5).astype(jnp.int32)
        message[m * lines : (m + 1) * lines, :] = coded.astype(jnp.int16)
    spare = message.shape[0] - units * lines - units
    level = jnp.concatenate([level, jnp.zeros((spare, half), jnp.float32)], axis=0)
    message[units * lines :, :] = level.astype(jnp.int32).astype(jnp.int16)


def decode(message, span, lines, valid=True):
    units = span[1] - span[0]
    level = message[units * lines :, :].astype(jnp.int32).astype(jnp.float32)
    scale = jnp.where(valid, jnp.exp2(level * (1.0 / STEPS)) * (1.0 / PEAK), 0.0)

    def plane(m):
        coded = message[m * lines : (m + 1) * lines, :].astype(jnp.int32).astype(jnp.float32)
        return coded * scale[m : m + 1, :]

    return plane


def blurred(filters, count, plane, put):
    wide = jnp.concatenate([filters, filters], axis=1)
    for m in range(0, count, 2):
        parts = [split(plane(n)) for n in range(m, min(m + 2, count))]
        high = jnp.concatenate([p[0] for p in parts], axis=1)
        low = jnp.concatenate([p[1] for p in parts], axis=1)
        made = jnp.dot(
            wide, jnp.concatenate([high, low], axis=0), preferred_element_type=jnp.float32
        )
        half = made.shape[1] // len(parts)
        for i in range(len(parts)):
            put(m + i, made[:, i * half : (i + 1) * half])


def side_step():
    return jnp.where(lax.axis_index("line") % 2 == 0, jnp.int32(1), jnp.int32(-1))


def outside(*lines):
    return functools.reduce(jnp.logical_or, [lax.axis_index("line") == i for i in lines])


def by_core(zero, one):
    me = lax.axis_index("band")
    pl.when(me == 0)(zero)
    pl.when(me != 0)(one)


def share(span, picked, keep, other, total, message, product):
    units = span[1] - span[0]
    total[...] = keep[slice(*span)] + other[slice(*span)]

    def summing():
        def put(m, value):
            product[m] = value

        blurred(picked[1], units, lambda m: total[m], put)
        encode(product, (0, units), message)

    by_core(lambda: encode(total, (0, units), message), summing)


def centre(spans, picked, *rest):
    totals, (base, term) = rest[:-2], rest[-2:]

    def work(block, out):
        for span, total in zip(spans, totals):

            def put(m, value):
                out[span[0] + m] = value

            blurred(block, span[1] - span[0], lambda m: total[m], put)

    work(picked[0], base)
    pl.when(lax.axis_index("band") != 0)(lambda: work(picked[2], term))


def relay(span, term, received, message, total):
    def forward():
        message[...] = received[...]

    def add():
        missing = outside(1, lax.axis_size("line") - 2)
        plane = decode(received, span, term.shape[1], jnp.logical_not(missing))
        for m in range(*span):
            total[m] = term[m] + plane(m - span[0])
        encode(total, span, message)

    by_core(forward, add)


def beside(span, picked, base, near, product):
    units, lines, _ = product.shape

    def put(m, value):
        product[m] = base[span[0] + m] + value

    plane = decode(near, span, lines)
    pl.when(lax.axis_index("band") == 0)(lambda: blurred(picked[1], units, plane, put))


def settle(span, picked, base, product, received, message, total):
    units, lines, _ = product.shape

    def put(m, value):
        total[m] = product[m] + value

    def spreading():
        missing = outside(0, lax.axis_size("line") - 1)
        plane = decode(received, span, lines, jnp.logical_not(missing))
        blurred(picked[2], units, plane, put)

    def summing():
        plane = decode(received, span, lines)
        for m in range(units):
            total[m] = base[span[0] + m] + plane(m)

    by_core(spreading, summing)
    encode(total, (0, units), message)


def arccos(x):
    size = jnp.abs(x)
    big = size > 0.5
    z = jnp.where(big, 0.5 * (1.0 - size), size * size)
    root = jnp.where(big, jnp.sqrt(z), size)
    poly = 4.2163199048e-2
    for term in (2.4181311049e-2, 4.5470025998e-2, 7.4953002686e-2, 1.6666752422e-1):
        poly = poly * z + term
    arcsin = poly * z * root + root
    pi = 3.14159265358979
    inner = jnp.where(x < 0, 0.5 * pi + arcsin, 0.5 * pi - arcsin)
    outer = jnp.where(x < 0, pi - 2.0 * arcsin, 2.0 * arcsin)
    return jnp.where(big, outer, inner)


def finish_units(core, parts, observed, value, image, sem, sums):
    _, lines, half = value.shape
    copies = []
    for span, message in parts:
        plane = decode(message, span, lines)
        for n in range(*span):
            m, c = units_of(core, observed.shape[0])[n]
            at = slice(c * half, (c + 1) * half)
            made = plane(n - span[0])
            value[n] = made
            copies.append(pltpu.make_async_copy(value.at[n], image.at[m, :, at], sem(n)))
            copies[-1].start()
            seen = observed[m, :, at].astype(jnp.float32)
            sums[c] = (sums[c][0] + made * seen, sums[c][1] + made * made)
    return copies


def finish_most(spans, observed, *rest):
    chunks = len(spans)
    messages, others, rest = rest[:chunks], rest[chunks : 2 * chunks - 1], rest[2 * chunks - 1 :]
    image, own, theirs, value, other_value, sems = rest
    units, lines, half = value.shape
    zero = jnp.zeros((lines, half), jnp.float32)

    def work(core):
        sums, other_sums = [(zero, zero)] * 2, [(zero, zero)] * 2
        parts = list(zip(spans, messages))
        copies = finish_units(
            core, parts, observed, value, image, lambda n: sems.at[n], sums
        )
        parts = list(zip(spans[:-1], others))
        copies += finish_units(
            1 - core,
            parts,
            observed,
            other_value,
            image,
            lambda n: sems.at[units + n],
            other_sums,
        )
        for c in range(2):
            at = slice(c * half, (c + 1) * half)
            right = zero
            for m in range(observed.shape[0]):
                seen = observed[m, :, at].astype(jnp.float32)
                right = right + seen * seen
            own[0, :, at], own[1, :, at] = sums[c]
            own[2, :, at] = jnp.sqrt(right)
            theirs[0, :, at], theirs[1, :, at] = other_sums[c]
        for copy in copies:
            copy.wait()

    by_core(lambda: work(0), lambda: work(1))


def finish_last(span, observed, message, own, theirs, _, *rest):
    image, angles, angle, value, sems = rest
    units, lines, half = value.shape

    def work(core):
        columns = [slice(c * half, (c + 1) * half) for c in range(2)]
        sums = [(theirs[0, :, at], theirs[1, :, at]) for at in columns]
        copies = finish_units(
            core,
            [(span, message)],
            observed,
            value,
            image,
            lambda n: sems.at[n],
            sums,
        )
        for (inner, left), at in zip(sums, columns):
            bound = jnp.sqrt(left + own[1, :, at]) * own[2, :, at]
            ratio = (inner + own[0, :, at]) / jnp.maximum(bound, 1.0)
            angle[:, at] = arccos(jnp.clip(ratio, -1.0, 1.0))
            here = sems.at[units + len(copies) - (span[1] - span[0])]
            copies.append(pltpu.make_async_copy(angle.at[:, at], angles.at[:, at], here))
            copies[-1].start()
        for copy in copies:
            copy.wait()

    by_core(lambda: work(1), lambda: work(0))


def on_device(
    cube,
    observed,
    along_kernels,
    along_offsets,
    across_kernels,
    across_offsets,
    resp_start,
    resp_values,
):
    f32, i16 = jnp.float32, jnp.int16
    size = lax.axis_size("line")
    bands, lines, cols = cube.shape
    count = resp_values.shape[0]
    half = cols // 2
    _, _, units = ownership(count)
    shape = jax.ShapeDtypeStruct
    swap = [(0, 1), (1, 0)]
    partner = [(i, i ^ 1) for i in range(size)]
    even_up = [(i, (i + 2 - 4 * (i % 2)) % size) for i in range(size)]
    odd_up = [(j, i) for i, j in even_up]

    def cores(zero, one):
        return [(2 * a, 2 * b) for a, b in zero] + [(2 * a + 1, 2 * b + 1) for a, b in one]

    part = shape((units, lines, half), f32)
    edges = [-(-units * i // CHUNKS) for i in range(CHUNKS + 1)]
    spans = list(zip(edges[:-1], edges[1:]))
    coded = [shape((coded_rows(b - a, lines), half), i16) for a, b in spans]

    inputs = (
        resp_start,
        across_offsets,
        resp_values,
        across_kernels,
        along_offsets,
        along_kernels,
        cube,
    )
    inputs = [pltpu.with_memory_space_constraint(x, pltpu.HBM) for x in inputs]
    planes, odd, _ = ownership(count)
    wide = shape(resp_values.shape, f32)
    table = shape((2 * cols, cols), across_kernels.dtype)
    send, middle, local, wide, table, picked = call(
        fold_other,
        inputs,
        [HBM] * len(inputs),
        [part, shape((1, lines, half), f32), cube, wide, table, along_kernels],
        scratch=[
            pltpu.SMEM(resp_start.shape, jnp.int32),
            pltpu.SMEM(across_offsets.shape, jnp.int32),
            pltpu.VMEM(resp_values.shape, resp_values.dtype),
            pltpu.SMEM(resp_values.shape, f32),
            pltpu.VMEM(across_kernels.shape, across_kernels.dtype),
            pltpu.SMEM(along_offsets.shape, jnp.int32),
            pltpu.VMEM(along_kernels.shape, along_kernels.dtype),
            pltpu.VMEM((planes + odd, lines, cols), f32),
            pltpu.SMEM((count,), jnp.int32),
            pltpu.SemaphoreType.DMA((len(inputs),)),
            pltpu.SemaphoreType.DMA((-(-bands // resp_values.shape[1]),)),
        ],
    )
    (keep,) = call(
        fold_own,
        (inputs[0], wide, local, table, middle),
        [HBM] + [VMEM] * 4,
        [part],
        scratch=[
            pltpu.SMEM(resp_start.shape, jnp.int32),
            pltpu.SMEM(resp_values.shape, f32),
            pltpu.VMEM((planes, lines, cols), f32),
            pltpu.SMEM((count,), jnp.int32),
            pltpu.SemaphoreType.DMA((2,)),
        ],
    )
    work = [pltpu.VMEM(part.shape, f32)]
    other = lax.ppermute(send, "band", swap)
    totals, near = [], []
    for i, span in enumerate(spans):
        planes = shape((span[1] - span[0], lines, half), f32)
        total, message = call(
            functools.partial(share, span),
            (picked, keep, other),
            [VMEM] * 3,
            [planes, coded[i]],
            scratch=[pltpu.VMEM(planes.shape, f32)],
        )
        totals.append(total)
        near.append(lax.ppermute(message, ("line", "band"), cores(partner, odd_up)))
    base, term = call(
        functools.partial(centre, spans),
        (picked, *totals),
        [VMEM] * (1 + len(spans)),
        [part] * 2,
    )
    far, product = [], []
    for i, span in enumerate(spans):
        (message,) = call(
            functools.partial(relay, span), (term, near[i]), [VMEM] * 2, [coded[i]], scratch=work
        )
        message, near[i] = lax.optimization_barrier((message, near[i]))
        far.append(lax.ppermute(message, ("line", "band"), cores(even_up, partner)))
        planes = shape((span[1] - span[0], lines, half), f32)
        product += call(
            functools.partial(beside, span),
            (picked, base, near[i]),
            [VMEM] * 3,
            [planes],
        )
    messages, others = [], []
    for i, span in enumerate(spans):
        planes = product[i].shape
        messages += call(
            functools.partial(settle, span),
            (picked, base, product[i], far[i]),
            [VMEM] * 4,
            [coded[i]],
            scratch=[pltpu.VMEM(planes, f32)],
        )
        others.append(lax.ppermute(messages[i], "band", swap))
    image = shape((count, lines, cols), f32)
    three = shape((3, lines, cols), f32)
    inputs = [observed, *messages, *others[:-1]]
    image, own, theirs = call(
        functools.partial(finish_most, spans),
        inputs,
        [VMEM] * len(inputs),
        [image, three, three],
        scratch=work * 2 + [pltpu.SemaphoreType.DMA((2 * units,))],
        out_specs=[HBM, VMEM, VMEM],
    )
    image, angles = call(
        functools.partial(finish_last, spans[-1]),
        (observed, others[-1], own, theirs, image),
        [VMEM] * 4 + [HBM],
        [image, shape((lines, cols), f32)],
        scratch=[pltpu.VMEM((lines, cols), f32), *work, pltpu.SemaphoreType.DMA((units + 2,))],
        out_specs=[HBM] * 2,
        aliases={4: 0},
    )
    return image, angles


def solution(mesh):
    placed = (
        P("band", ("slab", "line"), None),
        P(None, ("slab", "line"), None),
        P(),
        P(),
        P(),
        P(),
        P(),
        P(),
    )
    return jax.shard_map(
        on_device,
        mesh=mesh,
        in_specs=placed,
        out_specs=(P(None, ("slab", "line"), None), P(("slab", "line"), None)),
        check_vma=False,
    )
```
